128 devices in a mesh: slide: 2 (over x_hi), sx: 16 (over y, x_lo, core), sy: 4 (over z).
Axes of the slice: x: 4 (x_hi: 2, x_lo: 2; x = x_hi * 2 + x_lo), y: 4, z: 4, core: 2. Of those that a mesh axis runs over, the one named last changes fastest.
Arguments:
- features: bfloat16 [1024, 128, 256], P(('slide', 'sx'), 'sy'), parts along dimension 0, may hold values from -6 to 6
- return_slot: int32 [128, 16], P(('slide', 'sx'), 'sy'), parts along dimension 0, may hold values from -1 to 31, as said below
- returned_grads: bfloat16 [4, 1024, 512], P('sy', ('slide', 'sx')), parts along dimension 1, may hold values from -6 to 6
- conv_weight: float32 [7, 7, 256], replicated, may hold values from -0.875 to 0.875
- conv_bias: float32 [256], replicated, may hold values from -3 to 3
- norm_gain: float32 [256], replicated, may hold values from 0.1 to 1.9
- norm_bias: float32 [256], replicated, may hold values from -3 to 3
- expand_weight: bfloat16 [256, 1024], replicated, may hold values from -0.375 to 0.375
- expand_bias: float32 [1024], replicated, may hold values from -3 to 3
- project_weight: bfloat16 [1024, 256], replicated, may hold values from -0.1875 to 0.1875
- project_bias: float32 [256], replicated, may hold values from -3 to 3
- layer_scale: float32 [256], replicated, may hold values from 0.5 to 1.5
- down_gain: float32 [256], replicated, may hold values from 0.1 to 1.9
- down_bias: float32 [256], replicated, may hold values from -3 to 3
- down_weight: bfloat16 [1024, 512], replicated, may hold values from -0.1875 to 0.1875
- down_offset: float32 [512], replicated, may hold values from -3 to 3
Outputs:
- pooled: bfloat16 [128, 16, 512], P(('slide', 'sx'), 'sy'), parts along dimension 0
- grad_features: bfloat16 [1024, 128, 256], P(('slide', 'sx'), 'sy'), parts along dimension 0
- grad_conv_weight: float32 [14, 7, 256], P('slide'), parts along dimension 0
- grad_expand_weight: float32 [512, 1024], P('slide'), parts along dimension 0
- grad_project_weight: float32 [2048, 256], P('slide'), parts along dimension 0
- grad_down_weight: float32 [2048, 512], P('slide'), parts along dimension 0
- grad_vectors: float32 [14, 256], P('slide'), parts along dimension 0
- grad_expand_bias: float32 [2048], P('slide'), parts along dimension 0
- grad_down_offset: float32 [1024], P('slide'), parts along dimension 0
The draws below stay inside these ranges and needn't reach their ends.
There are 2 independent parts, one for each index of `slide`. The reference program is written for one: setup_inputs(seed, part) draws one part's arguments, and reference() takes and returns one part's arrays. A program takes and returns all parts, laid end to end along the dimension named above; an argument that names none is the same for every part. Nothing has to cross between parts.
Inputs may be any that keep to these rules, and one draw needn't show every extreme that they name: `return_slot`: -1 marks a tile position without tissue; otherwise a * 2 + j says that the tile's pooled gradient lies in slot j that the aggregator at sx index a, same sy index, keeps for this owner. On one device no two tiles share a value; every device has 2 or more tissue tiles, and on every device some aggregator fills all 2 of its slots. Slots that no tile names hold values that are not used.
All inputs are finite; a program needn't handle non-finite values.
Results may differ from the reference program's by a relative error of at most 0.0059.
Values may be sent and summed in bfloat16 or wider, within the bound.
A program may use at most 64 MiB of HBM per device.

```python
import jax
import jax.numpy as jnp
from jax import lax

C = 256
FF = 1024
C2 = 512
TILE = 8
TX = 4
TY = 4
NX = 512
NY = 128
CAP = 2
AROWS = 512
N_SX = 16
N_SY = 4


def draw_return_slot(key, part):
    key = jax.random.fold_in(key, 11)
    subkeys = jax.random.split(key, 4)
    per_device = TX * TY
    density = jax.random.randint(subkeys[0], (N_SX, N_SY, 1), 600, 1001)
    scores = jax.random.randint(subkeys[1], (N_SX, N_SY, per_device), 0, 1000)
    starts = jax.random.randint(subkeys[2], (N_SX, N_SY, 1), 0, per_device)
    position = jnp.arange(per_device, dtype=jnp.int32)
    forced = (position - starts) % per_device < CAP
    tissue = (scores < density) | forced
    tile_rank = jnp.maximum(jnp.cumsum(tissue.astype(jnp.int32), axis=-1) - 1, 0)
    order_keys = jax.random.randint(subkeys[3], (N_SX, N_SY, N_SX), 0, 1 << 20) * N_SX + jnp.arange(N_SX, dtype=jnp.int32)
    shuffled = jnp.argsort(order_keys, axis=-1, stable=True).astype(jnp.int32)
    group_index = tile_rank // CAP
    chosen = jnp.take_along_axis(shuffled, group_index, axis=-1)
    slot_ids = jnp.where(tissue, chosen * CAP + tile_rank % CAP, -1)
    return slot_ids.reshape(N_SX, N_SY, TX, TY).transpose(0, 2, 1, 3).reshape(N_SX * TX, N_SY * TY).astype(jnp.int32)


def level_of(stream_key, shape, cuts, least, top_value):
    factor_of, own = 1.0, jax.random.fold_in(stream_key, 6)
    for dim, blocks in cuts:
        heights = jnp.exp(jax.random.uniform(jax.random.fold_in(own, dim), (blocks,), jnp.float32, least / len(cuts), top_value / len(cuts)))
        factor_of = factor_of * jnp.repeat(heights, shape[dim] // blocks).reshape([-1 if axis == dim else 1 for axis in range(len(shape))])
    return factor_of


def normal_values(rng, dims, deviation, bound, pieces=(), kind=jnp.bfloat16):
    drawn = jax.random.normal(rng, dims, jnp.float32) * deviation
    if len(pieces) > 0:
        drawn = level_of(rng, dims, pieces, -0.22, 0.18) * drawn
    return jnp.clip(drawn, min=-bound, max=bound).astype(kind)


def setup_inputs(seed: int = 0, part: int = 0) -> dict:
    arg_keys = jax.random.split(jax.random.key(seed), 17)
    part_splits = jax.random.split(jax.random.fold_in(arg_keys[16], part), 17)
    features = normal_values(part_splits[0], (NX, NY, C), 1.0, 6.0, ((0, 16), (1, 4)))
    return_slot = draw_return_slot(jax.random.fold_in(jax.random.fold_in(arg_keys[16], part), 71), part)
    returned_grads = normal_values(part_splits[2], (N_SY, AROWS, C2), 1.0, 6.0, ((0, 4), (1, 16)))
    conv_weight = normal_values(arg_keys[3], (7, 7, C), 49 ** -0.5, 0.875, (), jnp.float32)
    conv_bias = normal_values(arg_keys[4], (C,), 0.5, 3.0, (), jnp.float32)
    norm_gain = jnp.clip(1.0 + 0.18 * jax.random.normal(arg_keys[5], (C,), jnp.float32), 0.1, 1.9)
    norm_bias = normal_values(arg_keys[6], (C,), 0.5, 3.0, (), jnp.float32)
    expand_weight = normal_values(arg_keys[7], (C, FF), C ** -0.5, 0.375)
    expand_bias = normal_values(arg_keys[8], (FF,), 0.5, 3.0, (), jnp.float32)
    project_weight = normal_values(arg_keys[9], (FF, C), FF ** -0.5, 0.1875)
    project_bias = normal_values(arg_keys[10], (C,), 0.5, 3.0, (), jnp.float32)
    layer_scale = jnp.clip(jax.random.uniform(arg_keys[11], (C,), jnp.float32, 0.5, 1.5), 0.5, 1.5)
    down_gain = jnp.clip(1.0 + 0.18 * jax.random.normal(arg_keys[12], (C,), jnp.float32), 0.1, 1.9)
    down_bias = normal_values(arg_keys[13], (C,), 0.5, 3.0, (), jnp.float32)
    down_weight = normal_values(arg_keys[14], (4 * C, C2), (4 * C) ** -0.5, 0.1875)
    down_offset = normal_values(arg_keys[15], (C2,), 0.5, 3.0, (), jnp.float32)
    return dict(features=features, return_slot=return_slot, returned_grads=returned_grads, conv_weight=conv_weight, conv_bias=conv_bias, norm_gain=norm_gain, norm_bias=norm_bias, expand_weight=expand_weight, expand_bias=expand_bias, project_weight=project_weight, project_bias=project_bias, layer_scale=layer_scale, down_gain=down_gain, down_bias=down_bias, down_weight=down_weight, down_offset=down_offset)


norm_eps = 1e-06
gelu_scale = 0.7978845608028654
gelu_cubic = 0.044715

def gelu_value(hidden):
    inner = gelu_scale * (hidden + gelu_cubic * hidden * hidden * hidden)
    return 0.5 * hidden * (1.0 + jnp.tanh(inner))

def gelu_slope(hidden):
    inner = gelu_scale * (hidden + gelu_cubic * hidden * hidden * hidden)
    tanh_val = jnp.tanh(inner)
    return 0.5 * (1.0 + tanh_val) + 0.5 * hidden * (1.0 - tanh_val * tanh_val) * gelu_scale * (1.0 + 3.0 * gelu_cubic * hidden * hidden)

def normalize(values):
    centre = lax.optimization_barrier(jnp.mean(values, axis=-1, keepdims=True))
    shifted = values - centre
    spread = lax.optimization_barrier(jnp.mean(shifted * shifted, axis=-1, keepdims=True))
    inv_std = lax.rsqrt(spread + norm_eps)
    return (shifted * inv_std, inv_std)

def normalize_back(grad_norm, normed, inv_std):
    first = lax.optimization_barrier(jnp.mean(grad_norm, axis=-1, keepdims=True))
    second = lax.optimization_barrier(jnp.mean(grad_norm * normed, axis=-1, keepdims=True))
    return inv_std * (grad_norm - first - normed * second)

def depthwise(padded, kernel, width_x, width_y):
    total = jnp.zeros((width_x, width_y, padded.shape[-1]), jnp.float32)
    for row_off in range(7):
        for col_off in range(7):
            total = total + padded[row_off:row_off + width_x, col_off:col_off + width_y] * kernel[row_off, col_off]
    return total

def kernel_grad(padded, grad_out):
    width_x, width_y = (grad_out.shape[0], grad_out.shape[1])
    rows_list = []
    for row_off in range(7):
        cols_list = []
        for col_off in range(7):
            window = padded[row_off:row_off + width_x, col_off:col_off + width_y]
            cols_list.append(lax.optimization_barrier(jnp.sum(window * grad_out, axis=(0, 1))))
        rows_list.append(jnp.stack(cols_list))
    return jnp.stack(rows_list)

def expand_apply(normed_rows, expand_weight, expand_bias, project_weight, project_bias):
    hidden = jnp.dot(normed_rows, expand_weight, preferred_element_type=jnp.float32) + expand_bias
    active = gelu_value(hidden).astype(jnp.bfloat16)
    branch = jnp.dot(active, project_weight, preferred_element_type=jnp.float32) + project_bias
    return (branch, hidden, active)

def expand_back(normed_rows, hidden, active, grad_branch, expand_weight, project_weight):
    grad_branch_b = grad_branch.astype(jnp.bfloat16)
    grad_project = lax.dot_general(active, grad_branch_b, (((0,), (0,)), ((), ())), preferred_element_type=jnp.float32)
    grad_active = lax.dot_general(grad_branch_b, project_weight, (((1,), (1,)), ((), ())), preferred_element_type=jnp.float32)
    grad_hidden = grad_active * gelu_slope(hidden)
    grad_bias = lax.optimization_barrier(jnp.sum(grad_hidden, axis=0))
    grad_hidden_b = grad_hidden.astype(jnp.bfloat16)
    grad_expand = lax.dot_general(normed_rows, grad_hidden_b, (((0,), (0,)), ((), ())), preferred_element_type=jnp.float32)
    grad_normed = lax.dot_general(grad_hidden_b, expand_weight, (((1,), (1,)), ((), ())), preferred_element_type=jnp.float32)
    return (grad_normed, grad_expand, grad_project, grad_bias)

def to_patches(grid):
    half_x, half_y, chans = (grid.shape[0] // 2, grid.shape[1] // 2, grid.shape[2])
    return grid.reshape(half_x, 2, half_y, 2, chans).transpose(0, 2, 1, 3, 4).reshape(half_x * half_y, 4 * chans)

def tile_sums(rows, tiles_x, tiles_y, half_tile):
    return rows.reshape(tiles_x, half_tile, tiles_y, half_tile, rows.shape[-1]).sum(axis=(1, 3))

def spread_tiles(per_tile, half_tile, chans):
    tiles_x, tiles_y = (per_tile.shape[0], per_tile.shape[1])
    blocks = per_tile.reshape(tiles_x, tiles_y, 2, 2, chans).transpose(0, 2, 1, 3, 4)
    wide = jnp.broadcast_to(blocks[:, None, :, :, None, :, :], (tiles_x, half_tile, 2, tiles_y, half_tile, 2, chans))
    return wide.reshape(tiles_x * half_tile * 2, tiles_y * half_tile * 2, chans)

def reference(features, return_slot, returned_grads, conv_weight, conv_bias, norm_gain, norm_bias, expand_weight, expand_bias, project_weight, project_bias, layer_scale, down_gain, down_bias, down_weight, down_offset):
    tiles_x, tiles_y = return_slot.shape
    width_x, width_y, chans = features.shape
    half_tile = TILE // 2
    tissue = return_slot >= 0
    pixel_mask = jnp.repeat(jnp.repeat(tissue, TILE, axis=0), TILE, axis=1)
    masked = features * pixel_mask[:, :, None].astype(jnp.bfloat16)
    padded_in = jnp.pad(masked.astype(jnp.float32), ((3, 3), (3, 3), (0, 0)))
    conv_out = depthwise(padded_in, conv_weight, width_x, width_y) + conv_bias
    normed_conv, inv_conv = normalize(conv_out)
    normed_in = (normed_conv * norm_gain + norm_bias).astype(jnp.bfloat16)
    block_rows = TX * TY * TILE * TILE
    row_blocks = normed_in.reshape(-1, block_rows, chans)

    def forward_block(block_in):
        return expand_apply(block_in, expand_weight, expand_bias, project_weight, project_bias)[0]
    branch = lax.map(forward_block, row_blocks).reshape(width_x, width_y, chans)
    summed = (masked.astype(jnp.float32) + layer_scale * branch).astype(jnp.bfloat16)
    normed_sum, inv_sum = normalize(summed.astype(jnp.float32))
    down_in = (normed_sum * down_gain + down_bias).astype(jnp.bfloat16)
    patches = to_patches(down_in)
    reduced = jnp.dot(patches, down_weight, preferred_element_type=jnp.float32) + down_offset
    tissue_f = tissue[:, :, None].astype(jnp.float32)
    pooled = (tile_sums(reduced, tiles_x, tiles_y, half_tile) / (half_tile * half_tile) * tissue_f).astype(jnp.bfloat16)
    owner = (jnp.arange(tiles_x, dtype=jnp.int32) // TX)[:, None]
    column = (jnp.arange(tiles_y, dtype=jnp.int32) // TY)[None, :]
    slot_ids = jnp.maximum(return_slot, 0)
    source_row = slot_ids // CAP * (N_SX * CAP) + owner * CAP + slot_ids % CAP
    column_full = jnp.broadcast_to(column, source_row.shape)
    picked = returned_grads[column_full, source_row]
    grad_pool = jnp.where(tissue[:, :, None], picked.astype(jnp.float32), 0.0)
    grad_reduced = grad_pool / (half_tile * half_tile)
    grad_reduced_b = grad_reduced.astype(jnp.bfloat16)
    patch_sums = tile_sums(patches.astype(jnp.float32), tiles_x, tiles_y, half_tile)
    grad_down_weight = lax.dot_general(patch_sums.reshape(-1, 4 * chans), grad_reduced.reshape(-1, grad_reduced.shape[-1]), (((0,), (0,)), ((), ())), precision=lax.Precision.HIGHEST, preferred_element_type=jnp.float32)
    grad_down_offset = lax.optimization_barrier(jnp.sum(grad_pool, axis=(0, 1)))
    grad_patch = lax.dot_general(grad_reduced_b, down_weight, (((2,), (1,)), ((), ())), preferred_element_type=jnp.float32)
    grad_down_in = spread_tiles(grad_patch, half_tile, chans)
    grad_down_gain = lax.optimization_barrier(jnp.sum(grad_down_in * normed_sum, axis=(0, 1)))
    grad_down_bias = lax.optimization_barrier(jnp.sum(grad_down_in, axis=(0, 1)))
    grad_summed = normalize_back(grad_down_in * down_gain, normed_sum, inv_sum)
    grad_scale = lax.optimization_barrier(jnp.sum(grad_summed * branch, axis=(0, 1)))
    grad_branch = layer_scale * grad_summed
    grad_project_bias = lax.optimization_barrier(jnp.sum(grad_branch, axis=(0, 1)))

    def backward_block(carry, inputs):
        block_in, block_grad = inputs
        part_branch, hidden, active = expand_apply(block_in, expand_weight, expand_bias, project_weight, project_bias)
        grad_normed, grad_expand, grad_project, grad_bias = expand_back(block_in, hidden, active, block_grad, expand_weight, project_weight)
        return ((carry[0] + grad_expand, carry[1] + grad_project, carry[2] + grad_bias), grad_normed)
    start = (jnp.zeros((chans, FF), jnp.float32), jnp.zeros((FF, chans), jnp.float32), jnp.zeros((FF,), jnp.float32))
    totals, grad_blocks = lax.scan(backward_block, start, (row_blocks, grad_branch.reshape(-1, block_rows, chans)))
    grad_expand_weight, grad_project_weight, grad_expand_bias = totals
    grad_normed_in = grad_blocks.reshape(width_x, width_y, chans)
    grad_norm_gain = lax.optimization_barrier(jnp.sum(grad_normed_in * normed_conv, axis=(0, 1)))
    grad_norm_bias = lax.optimization_barrier(jnp.sum(grad_normed_in, axis=(0, 1)))
    grad_conv = normalize_back(grad_normed_in * norm_gain, normed_conv, inv_conv)
    grad_conv_bias = lax.optimization_barrier(jnp.sum(grad_conv, axis=(0, 1)))
    grad_conv_weight = kernel_grad(padded_in, grad_conv)
    padded_grad = jnp.pad(grad_conv, ((3, 3), (3, 3), (0, 0)))
    grad_in = depthwise(padded_grad, conv_weight[::-1, ::-1], width_x, width_y)
    grad_features = ((grad_summed + grad_in) * pixel_mask[:, :, None].astype(jnp.float32)).astype(jnp.bfloat16)
    grad_vectors = jnp.stack([grad_conv_bias, grad_norm_gain, grad_norm_bias, grad_project_bias, grad_scale, grad_down_gain, grad_down_bias])
    return (pooled, grad_features, grad_conv_weight, grad_expand_weight, grad_project_weight, grad_down_weight, grad_vectors, grad_expand_bias, grad_down_offset)
```

```python
import functools

import jax
import jax.numpy as jnp
from jax import lax
from jax.experimental import pallas as pl
from jax.experimental.pallas import tpu as pltpu
from jax.sharding import PartitionSpec as P

F32 = jnp.float32
BF16 = jnp.bfloat16
MESH = pl.DeviceIdType.MESH

norm_eps = 1e-06
gelu_scale = 0.7978845608028654
gelu_cubic = 0.044715

WX = 32
WY = 32
LEFT = 8
PITCH = 48
PLANE = 38 * PITCH
N_SX = 16
N_SY = 4


def mm(a, b, ca, cb):
    return lax.dot_general(a, b, (((ca,), (cb,)), ((), ())), preferred_element_type=F32)


def fold8(v):
    return jnp.sum(v.reshape(v.shape[0] // 8, 8, v.shape[1]), axis=0)


def row_mean(v):
    return jnp.sum(v, axis=-1, keepdims=True) * (1.0 / v.shape[-1])


def kernel(
    slot_ref, feat_ref, ret_ref, cw_ref, cb_ref, ng_ref, nb_ref, w1_ref, b1_ref, w2_ref, b2_ref, ls_ref, dg_ref,
    db_ref, dw_ref, do_ref,
    pooled_ref, gf_ref, small_ref, big_ref,
    p_ref, pg_ref, yp_ref, yr_ref, cr_ref, wb_ref, mn_ref, mv_ref,
    rg_ref, pk_ref, rv_ref, ar_ref, gr_ref, gp_ref, ps_ref,
    co_ref, nc_ref, inv_ref, ni_ref, act_ref, sl_ref, gs_ref, gb_ref, nat_ref,
    kg_ref, v_ref, vr_ref, vz_ref, vf_ref,
    loc_ref, s0_ref, r0_ref, t0_ref, r1_ref, t1_ref, r2_ref, t2_ref, r3_ref, fin_ref,
    hs_sem, hr_sem, as_sem, ar_sem, bs_sem, br_sem, vs_sem, vr_sem, out_sem,
):
    sx = lax.axis_index("sx")
    sy = lax.axis_index("sy")
    core = lax.rem(sx, 2)
    xl = lax.rem(sx // 2, 2)
    yy = sx // 4

    def at_sx(k):
        return lax.rem(sx + k + N_SX, N_SX)

    def at_sy(k):
        return lax.rem(sy + k + N_SY, N_SY)

    barrier = pltpu.get_barrier_semaphore()

    def greet(k, c):
        pl.semaphore_signal(barrier, inc=1, device_id={"sx": at_sx(k)}, device_id_type=MESH)
        return c

    lax.fori_loop(1, N_SX, greet, 0)
    for k in range(1, N_SY):
        pl.semaphore_signal(barrier, inc=1, device_id={"sy": at_sy(k)}, device_id_type=MESH)
    for i in (-1, 1):
        for j in (-1, 1):
            pl.semaphore_signal(barrier, inc=1, device_id={"sx": at_sx(i), "sy": at_sy(j)}, device_id_type=MESH)

    sub = lax.broadcasted_iota(jnp.int32, (8, 128), 0)
    lane = lax.broadcasted_iota(jnp.int32, (8, 128), 1)
    sel = []
    for tx in range(4):
        picked = jnp.zeros((8, 128), jnp.int32)
        for ty in range(4):
            s = slot_ref[tx, ty]
            picked = jnp.where(sub // 2 == ty, s, picked)
            mn_ref[tx, ty * 8 : ty * 8 + 8, :] = jnp.where(jnp.full((8, 128), s) >= 0, 1.0, 0.0).astype(F32)
        mv_ref[tx] = jnp.where(picked >= 0, 1.0, 0.0).astype(F32)
        sel.append(jnp.where(picked == lane, 1.0, 0.0).astype(F32))
    selector = jnp.concatenate(sel, axis=0).astype(BF16)[:, :32]

    def fill(x, c):
        f = feat_ref[x].astype(F32)
        m = mn_ref[x // 8]
        at = pl.multiple_of((x + 3) * PITCH + LEFT, 8)
        for h in range(2):
            p_ref[h, pl.ds(at, WY), :] = f[:, h * 128 : h * 128 + 128] * m
        return c

    lax.fori_loop(0, WX, fill, 0)

    def pack(e, ref):
        for side, col in ((0, 0), (1, WY - 3)):
            for h in range(2):
                for c in range(3):
                    for g in range(4):
                        yp_ref[e, side, h, c, g * 8 : g * 8 + 8, :] = ref[
                            h, pl.ds((3 + g * 8) * PITCH + LEFT + col + c, 8, stride=PITCH), :
                        ]

    def halo_copies(e, ref):
        def rc(src, dst, k, dev):
            return pltpu.make_async_remote_copy(
                src_ref=src, dst_ref=dst, send_sem=hs_sem.at[e, k], recv_sem=hr_sem.at[e, k], device_id=dev,
                device_id_type=MESH,
            )

        out = [
            rc(ref.at[:, 3 * PITCH : 6 * PITCH, :], ref.at[:, 35 * PITCH : 38 * PITCH, :], 0, {"sx": at_sx(-1)}),
            rc(ref.at[:, 32 * PITCH : 35 * PITCH, :], ref.at[:, 0 : 3 * PITCH, :], 1, {"sx": at_sx(1)}),
        ]
        for side, step in ((0, -1), (1, 1)):
            out.append(rc(yp_ref.at[e, side], yr_ref.at[e, side], 2 + side, {"sy": at_sy(step)}))
            out.append(
                rc(yp_ref.at[e, side, :, :, 24:32, :], cr_ref.at[e, 2 * side], 4 + 2 * side,
                   {"sx": at_sx(1), "sy": at_sy(step)})
            )
            out.append(
                rc(yp_ref.at[e, side, :, :, 0:8, :], cr_ref.at[e, 2 * side + 1], 5 + 2 * side,
                   {"sx": at_sx(-1), "sy": at_sy(step)})
            )
        return out

    def unpack(e, ref):
        has_top = sx > 0
        has_bottom = sx < N_SX - 1

        @pl.when(jnp.logical_not(has_top))
        def _():
            ref[:, 0 : 3 * PITCH, :] = jnp.zeros((2, 3 * PITCH, 128), F32)

        @pl.when(jnp.logical_not(has_bottom))
        def _():
            ref[:, 35 * PITCH : 38 * PITCH, :] = jnp.zeros((2, 3 * PITCH, 128), F32)

        for side, col, inside in ((0, LEFT + WY, sy < N_SY - 1), (1, LEFT - 3, sy > 0)):
            keep = jnp.where(inside, 1.0, 0.0).astype(F32)
            keep_top = jnp.where(jnp.logical_and(inside, has_top), 1.0, 0.0).astype(F32)
            keep_bottom = jnp.where(jnp.logical_and(inside, has_bottom), 1.0, 0.0).astype(F32)
            for h in range(2):
                for c in range(3):
                    for g in range(4):
                        ref[h, pl.ds((3 + g * 8) * PITCH + col + c, 8, stride=PITCH), :] = (
                            yr_ref[e, side, h, c, g * 8 : g * 8 + 8, :] * keep
                        )
                    ref[h, pl.ds(col + c, 3, stride=PITCH), :] = cr_ref[e, 2 * side, h, c, 5:8, :] * keep_top
                    ref[h, pl.ds(35 * PITCH + col + c, 3, stride=PITCH), :] = (
                        cr_ref[e, 2 * side + 1, h, c, 0:3, :] * keep_bottom
                    )

    pack(0, p_ref)

    for q in range(4):
        rg_ref[q] = ret_ref[:, q * 128 : q * 128 + 128].astype(F32)
    for q in range(4):
        for s in range(2):
            pk_ref[pl.ds(2 * q + s, 16, stride=8), :] = rg_ref[q, pl.ds(s, 16, stride=2), :]

    pl.semaphore_wait(barrier, (N_SX - 1) + (N_SY - 1) + 4)

    for copy in halo_copies(0, p_ref):
        copy.start()

    def block8(i):
        return pl.ds(pl.multiple_of(i * 8, 8), 8)

    def return_copy(k):
        return pltpu.make_async_remote_copy(
            src_ref=pk_ref.at[block8(at_sx(k))], dst_ref=rv_ref.at[block8(sx)], send_sem=as_sem.at[k],
            recv_sem=ar_sem.at[k], device_id={"sx": at_sx(k)}, device_id_type=MESH,
        )

    def start_return(k, c):
        return_copy(k).start()
        return c

    lax.fori_loop(1, N_SX, start_return, 0)
    rv_ref[block8(sx), :] = pk_ref[block8(sx), :]

    for h in range(2):
        for a in range(7):
            for b in range(7):
                wb_ref[h, a * 7 + b] = jnp.broadcast_to(cw_ref[a, b : b + 1, h * 128 : h * 128 + 128], (8, 128))

    def wait_return(k, c):
        return_copy(k).wait()
        return c

    lax.fori_loop(1, N_SX, wait_return, 0)
    for q in range(4):
        for s in range(2):
            ar_ref[q, pl.ds(s, 16, stride=2), :] = rv_ref[pl.ds(2 * q + s, 16, stride=8), :]
    arrived = jnp.concatenate([ar_ref[q] for q in range(4)], axis=1).astype(BF16)
    grad_pool = mm(selector, arrived, 1, 0)
    grad_reduced = (grad_pool * (1.0 / 16.0)).astype(BF16)
    gr_ref[...] = grad_reduced
    grad_patch = mm(grad_reduced, dw_ref[...], 1, 1)
    for tx in range(4):
        gp_ref[tx] = grad_patch[tx * 8 : tx * 8 + 8, :]

    def clear(i, c):
        loc_ref[1, pl.ds(pl.multiple_of(i * 128, 128), 128), :] = jnp.zeros((128, 256), F32)
        return c

    lax.fori_loop(0, 16, clear, 0)

    kg_ref[...] = jnp.zeros_like(kg_ref)

    def add_entry(t, value):
        for h in range(2):
            kg_ref[h, t * 8 : t * 8 + 8, :] += value[:, h * 128 : h * 128 + 128]

    off_sum = jnp.sum(grad_pool.reshape(4, 8, 512), axis=0) * 0.5
    for q in range(2):
        add_entry(60 + q, off_sum[:, q * 256 : q * 256 + 256])
    bias_sum = jnp.sum(gp_ref[...], axis=0)
    bias_sum = (
        bias_sum[:, 0:256] + bias_sum[:, 256:512] + bias_sum[:, 512:768] + bias_sum[:, 768:1024]
    ) * 8.0
    add_entry(55, bias_sum)

    def plane_rows(ref, h, x, n):
        return [ref[h, pl.ds(x * PITCH + (LEFT - 3) + c, 8, stride=4), :] for c in range(n)]

    def depthwise(ref, h, x, flipped):
        sums = [[None] * 4 for _ in range(2)]
        for r in range(8):
            rows = plane_rows(ref, h, x + r, 10)
            for i in range(2):
                a = r - i
                if a < 0 or a > 6:
                    continue
                for b in range(7):
                    t = a * 7 + b
                    w = wb_ref[h, 48 - t if flipped else t]
                    for c in range(4):
                        term = rows[c + b] * w
                        sums[i][c] = term if sums[i][c] is None else sums[i][c] + term
        return sums

    for copy in halo_copies(0, p_ref):
        copy.wait()
    unpack(0, p_ref)

    def conv_step(i, c):
        x = i * 2
        for h in range(2):
            bias = cb_ref[:, h * 128 : h * 128 + 128]
            sums = depthwise(p_ref, h, x, False)
            for k in range(2):
                for q in range(4):
                    co_ref[h, block8((x + k) * 4 + q), :] = sums[k][q] + bias
        return c

    lax.fori_loop(0, WX // 2, conv_step, 0)

    r32 = lax.broadcasted_iota(jnp.int32, (32, 256), 0)
    k32 = lax.broadcasted_iota(jnp.int32, (32, 256), 1)
    off_of = (k32 // 32 % 2) * 2 + (k32 // 8 % 4) % 2
    patch_sel = jnp.where(
        (off_of == r32 // 8) & (k32 % 8 // 2 == r32 % 8 // 2) & (r32 % 2 == 0), 1.0, 0.0
    ).astype(BF16)

    def spread(blocks):
        row = [blocks[0], blocks[1]] * 2 + [blocks[2], blocks[3]] * 2
        return jnp.concatenate(row * 4, axis=0)

    def forward(tx, c):
        rows = pl.ds(pl.multiple_of(tx * 256, 256), 256)
        v = jnp.concatenate([co_ref[0, rows, :], co_ref[1, rows, :]], axis=1)
        shifted = v - row_mean(v)
        inv = lax.rsqrt(row_mean(shifted * shifted) + norm_eps)
        normed = shifted * inv
        nc_ref[rows, :] = normed
        inv_ref[rows, :] = jnp.broadcast_to(inv, (256, 128))
        normed_in = (normed * ng_ref[...] + nb_ref[...]).astype(BF16)
        ni_ref[rows, :] = normed_in
        branch = None
        for j in range(4):
            cols = slice(j * 256, j * 256 + 256)
            hid = mm(normed_in, w1_ref[:, cols], 1, 0) + b1_ref[:, cols]
            sq = hid * hid
            t = jnp.tanh(hid * (gelu_scale + (gelu_scale * gelu_cubic) * sq))
            u = 0.5 + 0.5 * t
            act = (hid * u).astype(BF16)
            act_ref[rows, cols] = act
            sl_ref[rows, cols] = u + hid * (u - u * t) * (gelu_scale + (3.0 * gelu_scale * gelu_cubic) * sq)
            part = mm(act, w2_ref[cols, :], 1, 0)
            branch = part if branch is None else branch + part
        branch = branch + b2_ref[...]
        masked = jnp.concatenate(
            [
                jnp.concatenate(
                    [
                        p_ref[h, pl.ds((tx * 8 + x + 3) * PITCH + LEFT + q, 8, stride=4), :]
                        for x in range(8)
                        for q in range(4)
                    ],
                    axis=0,
                )
                for h in range(2)
            ],
            axis=1,
        )
        summed = (masked + ls_ref[...] * branch).astype(BF16).astype(F32)
        shifted = summed - row_mean(summed)
        inv = lax.rsqrt(row_mean(shifted * shifted) + norm_eps)
        normed = shifted * inv
        down_in = (normed * dg_ref[...] + db_ref[...]).astype(BF16)
        ps_ref[tx] = mm(patch_sel, down_in, 1, 0)
        gp = gp_ref[tx]
        blocks = [gp[:, q * 256 : q * 256 + 256] for q in range(4)]
        scaled = [b * dg_ref[...] for b in blocks]
        centred = spread([s - row_mean(s) for s in scaled])
        second = row_mean(spread(scaled) * normed)
        grad_summed = inv * (centred - normed * second)
        for h in range(2):
            gs_ref[h, rows, :] = grad_summed[:, h * 128 : h * 128 + 128]
        add_entry(54, fold8(spread(blocks) * normed))
        add_entry(53, fold8(grad_summed * branch))
        scaled_grad = ls_ref[...] * grad_summed
        add_entry(52, fold8(scaled_grad))
        gb_ref[rows, :] = scaled_grad.astype(BF16)
        return c

    lax.fori_loop(0, 4, forward, 0)

    def batch(b):
        rings = ((yy, lambda k: {"sx": lax.rem(yy + k, 4) * 4 + lax.rem(sx, 4)}), (sy, lambda k: {"sy": at_sy(k)}))
        core_dev = {"sx": sx + 1 - 2 * core}
        x_dev = {"sx": sx + 2 - 4 * xl}

        def rc(src, dst, k, dev):
            return pltpu.make_async_remote_copy(
                src_ref=src, dst_ref=dst, send_sem=bs_sem.at[b, k], recv_sem=br_sem.at[b, k], device_id=dev,
                device_id_type=MESH,
            )

        def ds(i, n):
            return pl.ds(pl.multiple_of(i, n), n)

        fin = fin_ref.at[b]
        s0, r0, t0, r1 = s0_ref.at[b], r0_ref.at[b], t0_ref.at[b], r1_ref.at[b]
        t1, r2, t2, r3 = t1_ref.at[b], r2_ref.at[b], t2_ref.at[b], r3_ref.at[b]
        loc = loc_ref.at[b]

        def goff(half, depth):
            at = core * 1024 + half * 512
            if depth > 0:
                at = at + rings[half][0] * 128
            if depth > 1:
                at = at + rings[1 - half][0] * 32
            if depth > 2:
                at = at + xl * 16
            return at

        def core_in():
            return [rc(s0, r0, 0, core_dev)]

        def ring1_in():
            return [
                rc(t0.at[ds(half * 512 + lax.rem(rings[half][0] + k, 4) * 128, 128)],
                   r1.at[half * 3 + k - 1], 1 + half * 3 + k - 1, rings[half][1](k))
                for half in range(2) for k in range(1, 4)
            ]

        def ring2_in():
            return [
                rc(t1.at[half, ds(lax.rem(rings[1 - half][0] + k, 4) * 32, 32)],
                   r2.at[half * 3 + k - 1], 7 + half * 3 + k - 1, rings[1 - half][1](k))
                for half in range(2) for k in range(1, 4)
            ]

        def x_in():
            return [
                rc(t2.at[half, ds((1 - xl) * 16, 16)], r3.at[half], 13 + half, x_dev) for half in range(2)
            ]

        def x_out():
            return [
                rc(fin.at[ds(goff(half, 3), 16)], fin.at[ds(goff(half, 3), 16)], 15 + half, x_dev)
                for half in range(2)
            ]

        def ring2_out():
            return [
                rc(fin.at[ds(goff(half, 2), 32)], fin.at[ds(goff(half, 2), 32)], 17 + half * 3 + k - 1,
                   rings[1 - half][1](k))
                for half in range(2) for k in range(1, 4)
            ]

        def ring1_out():
            return [
                rc(fin.at[ds(goff(half, 1), 128)], fin.at[ds(goff(half, 1), 128)], 23 + half * 3 + k - 1,
                   rings[half][1](k))
                for half in range(2) for k in range(1, 4)
            ]

        def core_out():
            return [rc(fin.at[ds(core * 1024, 1024)], fin.at[ds(core * 1024, 1024)], 29, core_dev)]

        def start(copies):
            for copy in copies:
                copy.start()

        def wait(copies):
            for copy in copies:
                copy.wait()

        def step0():
            def cast(i, c):
                s0[ds(i * 128, 128), :] = loc[ds((1 - core) * 1024 + i * 128, 128), :].astype(BF16)
                return c

            lax.fori_loop(0, 8, cast, 0)
            start(core_in())

        def step1():
            wait(core_in())

            def add(i, c):
                t0[ds(i * 128, 128), :] = (
                    loc[ds(core * 1024 + i * 128, 128), :] + r0[ds(i * 128, 128), :].astype(F32)
                ).astype(BF16)
                return c

            lax.fori_loop(0, 8, add, 0)
            start(ring1_in())

        def step2():
            wait(ring1_in())
            for half in range(2):
                total = t0[ds(half * 512 + rings[half][0] * 128, 128), :].astype(F32)
                for k in range(3):
                    total = total + r1[half * 3 + k].astype(F32)
                t1[half] = total.astype(BF16)
            start(ring2_in())

        def step3():
            wait(ring2_in())
            for half in range(2):
                total = t1[half, ds(rings[1 - half][0] * 32, 32), :].astype(F32)
                for k in range(3):
                    total = total + r2[half * 3 + k].astype(F32)
                t2[half] = total.astype(BF16)
            start(x_in())

        def step4():
            wait(x_in())
            for half in range(2):
                total = t2[half, ds(xl * 16, 16), :].astype(F32) + r3[half].astype(F32)
                fin_ref[b, ds(goff(half, 3), 16), :] = total.astype(BF16)
            start(x_out())

        def step5():
            wait(x_out())
            start(ring2_out())

        def step6():
            wait(ring2_out())
            start(ring1_out())

        def step7():
            wait(ring1_out())
            start(core_out())

        def step8():
            wait(core_out())
            pltpu.make_async_copy(fin, big_ref.at[b], out_sem.at[b]).start()

        def step9():
            pltpu.make_async_copy(fin, big_ref.at[b], out_sem.at[b]).wait()

        return [step0, step1, step2, step3, step4, step5, step6, step7, step8, step9]

    first = batch(0)
    second = batch(1)

    gr = gr_ref[...]
    gr2 = jnp.concatenate([gr, gr], axis=0)
    pool = None
    for q in range(4):
        sums = ps_ref[:, q * 8 : q * 8 + 8, :].reshape(32, 256)
        high = sums.astype(BF16)
        low = (sums - high.astype(F32)).astype(BF16)
        both = jnp.concatenate([high, low], axis=0)
        grad_down = mm(both, gr2, 0, 0)
        loc_ref[0, q * 256 : q * 256 + 256, :] = grad_down[:, :256]
        loc_ref[0, 1024 + q * 256 : 1024 + q * 256 + 256, :] = grad_down[:, 256:]
        part = mm(both, dw_ref[q * 256 : q * 256 + 256, :], 1, 0)
        part = part[:32] + part[32:]
        pool = part if pool is None else pool + part
    tissue = jnp.concatenate([mv_ref[...].reshape(32, 128)] * 4, axis=1)
    pooled_ref[...] = (pool * (1.0 / 16.0) + do_ref[...]) * tissue
    first[0]()

    def backward(tx, c):
        rows = pl.ds(pl.multiple_of(tx * 256, 256), 256)
        grad_b = gb_ref[rows, :]
        normed_in = ni_ref[rows, :]
        grad_normed = None
        for j in range(4):
            cols = slice(j * 256, j * 256 + 256)
            grad_hidden = mm(grad_b, w2_ref[cols, :], 1, 1) * sl_ref[rows, cols]
            add_entry(56 + j, fold8(grad_hidden))
            grad_hidden_b = grad_hidden.astype(BF16)
            part = mm(grad_hidden_b, w1_ref[:, cols], 1, 1)
            grad_normed = part if grad_normed is None else grad_normed + part
            loc_ref[1, j * 256 : j * 256 + 256, :] += mm(normed_in, grad_hidden_b, 0, 0)
            loc_ref[1, 1024 + j * 256 : 1024 + j * 256 + 256, :] += mm(act_ref[rows, cols], grad_b, 0, 0)
        normed = nc_ref[rows, :]
        add_entry(50, fold8(grad_normed * normed))
        add_entry(51, fold8(grad_normed))
        scaled = grad_normed * ng_ref[...]
        inv = inv_ref[rows, :]
        inv = jnp.concatenate([inv, inv], axis=1)
        grad_conv = inv * (scaled - row_mean(scaled) - normed * row_mean(scaled * normed))
        add_entry(49, fold8(grad_conv))
        for h in range(2):
            half = grad_conv[:, h * 128 : h * 128 + 128]
            co_ref[h, rows, :] = half
            for x in range(8):
                for q in range(4):
                    at = (x * 4 + q) * 8
                    pg_ref[h, pl.ds((tx * 8 + x + 3) * PITCH + LEFT + q, 8, stride=4), :] = half[at : at + 8, :]

        @pl.when(tx == 0)
        def _():
            first[1]()

        @pl.when(tx == 2)
        def _():
            first[2]()

        return c

    lax.fori_loop(0, 4, backward, 0)
    first[3]()

    pack(1, pg_ref)
    for copy in halo_copies(1, pg_ref):
        copy.start()
    second[0]()

    def tap_step(i, c):
        h = i // 7
        a = lax.rem(i, 7)

        def rows_step(k, sums):
            sums = list(sums)
            for d in range(2):
                x = k * 2 + d
                rows = plane_rows(p_ref, h, x + a, 10)
                grads = [co_ref[h, block8(x * 4 + q), :] for q in range(4)]
                for b in range(7):
                    sums[b] = sums[b] + (
                        (rows[b] * grads[0] + rows[b + 1] * grads[1])
                        + (rows[b + 2] * grads[2] + rows[b + 3] * grads[3])
                    )
            return tuple(sums)

        sums = lax.fori_loop(0, WX // 2, rows_step, tuple(jnp.zeros((8, 128), F32) for _ in range(7)))
        for b in range(7):
            kg_ref[h, pl.ds(pl.multiple_of((a * 7 + b) * 8, 8), 8), :] = sums[b]

        @pl.when(i == 2)
        def _():
            first[4]()
            second[1]()

        @pl.when(i == 5)
        def _():
            first[5]()

        @pl.when(i == 8)
        def _():
            first[6]()

        @pl.when(i == 11)
        def _():
            second[2]()

        return c

    lax.fori_loop(0, 14, tap_step, 0)
    first[7]()

    for h in range(2):
        total = kg_ref[h, pl.ds(0, 64, stride=8), :]
        for s in range(1, 8):
            total = total + kg_ref[h, pl.ds(s, 64, stride=8), :]
        v_ref[h * 64 : h * 64 + 64, :] = total

    def small_rc(src, dst, k, dev):
        return pltpu.make_async_remote_copy(
            src_ref=src, dst_ref=dst, send_sem=vs_sem.at[k], recv_sem=vr_sem.at[k], device_id=dev,
            device_id_type=MESH,
        )

    def small_in(k):
        return small_rc(v_ref.at[block8(at_sx(k))], vr_ref.at[block8(sx)], k, {"sx": at_sx(k)})

    def small_z(k):
        return small_rc(vz_ref.at[sy], vz_ref.at[sy], 15 + k, {"sy": at_sy(k)})

    def small_out(k):
        return small_rc(vf_ref.at[block8(sx)], vf_ref.at[block8(sx)], 18 + k, {"sx": at_sx(k)})

    def each(make, act):
        def body(k, c):
            act(make(k))
            return c

        return body

    def small_step0():
        lax.fori_loop(1, N_SX, each(small_in, lambda copy: copy.start()), 0)
        vr_ref[block8(sx), :] = v_ref[block8(sx), :]

    def small_step1():
        lax.fori_loop(1, N_SX, each(small_in, lambda copy: copy.wait()), 0)
        vz_ref[sy] = jnp.sum(vr_ref[...].reshape(16, 8, 128), axis=0)
        for k in range(1, N_SY):
            small_z(k).start()

    def small_step2():
        for k in range(1, N_SY):
            small_z(k).wait()
        vf_ref[block8(sx), :] = (vz_ref[0] + vz_ref[1]) + (vz_ref[2] + vz_ref[3])
        lax.fori_loop(1, N_SX, each(small_out, lambda copy: copy.start()), 0)

    def small_step3():
        lax.fori_loop(1, N_SX, each(small_out, lambda copy: copy.wait()), 0)
        small_ref[...] = vf_ref[...]

    small_step0()

    for copy in halo_copies(1, pg_ref):
        copy.wait()
    unpack(1, pg_ref)

    def back_step(i, c):
        x = i * 2
        keep = mv_ref[x // 8]
        for h in range(2):
            sums = depthwise(pg_ref, h, x, True)
            for k in range(2):
                for q in range(4):
                    value = (sums[k][q] + gs_ref[h, block8((x + k) * 4 + q), :]) * keep
                    nat_ref[h, x + k, pl.ds(q, 8, stride=4), :] = value
        for k in range(2):
            gf_ref[x + k] = jnp.concatenate([nat_ref[0, x + k], nat_ref[1, x + k]], axis=1).astype(BF16)

        @pl.when(i == 3)
        def _():
            second[3]()
            small_step1()

        @pl.when(i == 7)
        def _():
            second[4]()
            small_step2()

        @pl.when(i == 9)
        def _():
            second[5]()

        @pl.when(i == 11)
        def _():
            second[6]()

        return c

    lax.fori_loop(0, WX // 2, back_step, 0)
    small_step3()
    second[7]()
    first[8]()
    second[8]()
    first[9]()
    second[9]()


def on_device(
    features,
    return_slot,
    returned_grads,
    conv_weight,
    conv_bias,
    norm_gain,
    norm_bias,
    expand_weight,
    expand_bias,
    project_weight,
    project_bias,
    layer_scale,
    down_gain,
    down_bias,
    down_weight,
    down_offset,
):
    vmem = pl.BlockSpec(memory_space=pltpu.VMEM)

    def row(v):
        return v.reshape(1, -1)

    def vm(*shape, dtype=F32):
        return pltpu.VMEM(shape, dtype)

    dma = pltpu.SemaphoreType.DMA
    pooled, grad_features, small, big = pl.pallas_call(
        kernel,
        out_shape=(
            jax.ShapeDtypeStruct((32, 512), F32),
            jax.ShapeDtypeStruct((WX, WY, 256), BF16),
            jax.ShapeDtypeStruct((128, 128), F32),
            jax.ShapeDtypeStruct((2, 2048, 256), BF16),
        ),
        in_specs=[pl.BlockSpec(memory_space=pltpu.SMEM)] + [vmem] * 15,
        out_specs=(vmem, vmem, vmem, pl.BlockSpec(memory_space=pl.ANY)),
        scratch_shapes=[
            vm(2, PLANE, 128), vm(2, PLANE, 128), vm(2, 2, 2, 3, 32, 128), vm(2, 2, 2, 3, 32, 128),
            vm(2, 4, 2, 3, 8, 128),
            vm(2, 49, 8, 128), vm(4, 32, 128), vm(4, 8, 128),
            vm(4, 32, 128), vm(128, 128), vm(128, 128), vm(4, 32, 128), vm(32, 512, dtype=BF16), vm(4, 8, 1024),
            vm(4, 32, 256),
            vm(2, 1024, 128), vm(1024, 256), vm(1024, 128), vm(1024, 256, dtype=BF16), vm(1024, 1024, dtype=BF16),
            vm(1024, 1024), vm(2, 1024, 128), vm(1024, 256, dtype=BF16), vm(2, 32, 32, 128),
            vm(2, 512, 128), vm(128, 128), vm(128, 128), vm(4, 8, 128), vm(128, 128),
            vm(2, 2048, 256), vm(2, 1024, 256, dtype=BF16), vm(2, 1024, 256, dtype=BF16),
            vm(2, 1024, 256, dtype=BF16), vm(2, 6, 128, 256, dtype=BF16), vm(2, 2, 128, 256, dtype=BF16),
            vm(2, 6, 32, 256, dtype=BF16), vm(2, 2, 32, 256, dtype=BF16), vm(2, 2, 16, 256, dtype=BF16),
            vm(2, 2048, 256, dtype=BF16),
            dma((2, 8)), dma((2, 8)), dma((16,)), dma((16,)), dma((2, 30)), dma((2, 30)), dma((34,)), dma((34,)),
            dma((2,)),
        ],
        compiler_params=pltpu.CompilerParams(
            collective_id=0, has_side_effects=True, vmem_limit_bytes=56 * 1024 * 1024
        ),
        cost_estimate=pl.CostEstimate(flops=4_000_000_000, bytes_accessed=8_000_000, transcendentals=1_000_000),
    )(
        return_slot, features, returned_grads[0], conv_weight, row(conv_bias), row(norm_gain), row(norm_bias),
        expand_weight, row(expand_bias), project_weight, row(project_bias), row(layer_scale), row(down_gain),
        row(down_bias), down_weight, row(down_offset),
    )
    pooled = pooled.reshape(4, 4, 2, 512)[:, :, 0].astype(BF16)
    down = jnp.concatenate([big[0, :1024], big[0, 1024:]], axis=1).astype(F32)
    expand = jnp.concatenate([big[1, j * 256 : j * 256 + 256] for j in range(4)], axis=1).astype(F32)
    project = big[1, 1024:].astype(F32)
    small = jnp.concatenate([small[:64], small[64:]], axis=1)
    return (
        pooled,
        grad_features,
        small[:49].reshape(7, 7, 256),
        expand,
        project,
        down,
        small[49:56],
        small[56:60].reshape(1024),
        small[60:62].reshape(512),
    )


def solution(mesh):
    placed = (
        P(("slide", "sx"), "sy", None),
        P(("slide", "sx"), "sy"),
        P("sy", ("slide", "sx"), None),
    ) + (P(),) * 13
    return jax.shard_map(
        on_device,
        mesh=mesh,
        in_specs=placed,
        out_specs=(
            P(("slide", "sx"), "sy", None),
            P(("slide", "sx"), "sy", None),
            P("slide", None, None),
            P("slide", None),
            P("slide", None),
            P("slide", None),
            P("slide", None),
            P("slide"),
            P("slide"),
        ),
        check_vma=False,
    )
```

```python
import functools

import jax
import jax.numpy as jnp
from jax import lax
from jax.experimental import pallas as pl
from jax.experimental.pallas import tpu as pltpu
from jax.sharding import PartitionSpec as P

F32 = jnp.float32
BF16 = jnp.bfloat16
MESH = pl.DeviceIdType.MESH

norm_eps = 1e-06
gelu_scale = 0.7978845608028654
gelu_cubic = 0.044715

WX = 32
WY = 32
LEFT = 8
PITCH = 48
PLANE = 38 * PITCH
N_SX = 16
N_SY = 4


def mm(a, b, ca, cb):
    return lax.dot_general(a, b, (((ca,), (cb,)), ((), ())), preferred_element_type=F32)


def fold8(v):
    return jnp.sum(v.reshape(v.shape[0] // 8, 8, v.shape[1]), axis=0)


def row_mean(v):
    return jnp.sum(v, axis=-1, keepdims=True) * (1.0 / v.shape[-1])


def kernel(
    slot_hbm, feat_hbm, ret_hbm, cw_hbm, cb_hbm, ng_hbm, nb_hbm, w1_hbm, b1_hbm, w2_hbm, b2_hbm, ls_hbm, dg_hbm,
    db_hbm, dw_hbm, do_hbm,
    pooled_hbm, gf_hbm, small_hbm, expand_ref, project_ref, down_ref,
    slot_ref, feat_ref, ret_ref, cw_ref, cb_ref, ng_ref, nb_ref, w1_ref, b1_ref, w2_ref, b2_ref, ls_ref, dg_ref,
    db_ref, dw_ref, do_ref, pooled_ref, gf_ref, small_ref, in_sem, res_sem,
    p_ref, pg_ref, xp_ref, xr_ref, yp_ref, yr_ref, cr_ref, wb_ref, mn_ref, mv_ref,
    rg_ref, pk_ref, rv_ref, ar_ref, gr_ref, gp_ref, ps_ref,
    co_ref, nc_ref, inv_ref, nit_ref, gbt_ref, gh_ref, act_ref, sl_ref, gs_ref, gb_ref, nat_ref,
    kg_ref, v_ref, vr_ref, vz_ref, vf_ref,
    loc_ref, s0_ref, r0_ref, s1_ref, r1_ref, s2_ref, r2_ref, fin_ref,
    hs_sem, hr_sem, as_sem, ar_sem, bs_sem, br_sem, vs_sem, vr_sem, out_sem,
):
    pairs = (
        (slot_hbm, slot_ref), (feat_hbm, feat_ref), (ret_hbm, ret_ref), (cw_hbm, cw_ref), (cb_hbm, cb_ref),
        (dw_hbm, dw_ref), (w1_hbm, w1_ref), (w2_hbm, w2_ref), (ng_hbm, ng_ref), (nb_hbm, nb_ref), (b1_hbm, b1_ref),
        (b2_hbm, b2_ref), (ls_hbm, ls_ref), (dg_hbm, dg_ref), (db_hbm, db_ref), (do_hbm, do_ref),
    )
    loads = [pltpu.make_async_copy(src, dst, in_sem.at[k]) for k, (src, dst) in enumerate(pairs)]
    for load in loads:
        load.start()

    sx = lax.axis_index("sx")
    sy = lax.axis_index("sy")
    core = lax.rem(sx, 2)
    xl = lax.rem(sx // 2, 2)
    yy = sx // 4

    def at_sx(k):
        return lax.rem(sx + k + N_SX, N_SX)

    def at_sy(k):
        return lax.rem(sy + k + N_SY, N_SY)

    barrier = pltpu.get_barrier_semaphore()

    def greet(k, c):
        pl.semaphore_signal(barrier, inc=1, device_id={"sx": at_sx(k)}, device_id_type=MESH)
        return c

    lax.fori_loop(1, N_SX, greet, 0)
    for k in range(1, N_SY):
        pl.semaphore_signal(barrier, inc=1, device_id={"sy": at_sy(k)}, device_id_type=MESH)
    for k in range(1, N_SY):
        pl.semaphore_signal(
            barrier, inc=1, device_id={"sx": sx + 2 - 4 * xl, "sy": at_sy(k)}, device_id_type=MESH
        )
    for i in (-1, 1):
        for j in (-1, 1):
            pl.semaphore_signal(barrier, inc=1, device_id={"sx": at_sx(i), "sy": at_sy(j)}, device_id_type=MESH)

    loads[0].wait()
    sub = lax.broadcasted_iota(jnp.int32, (8, 128), 0)
    lane = lax.broadcasted_iota(jnp.int32, (8, 128), 1)
    sel = []
    for tx in range(4):
        picked = jnp.zeros((8, 128), jnp.int32)
        for ty in range(4):
            s = slot_ref[tx, ty]
            picked = jnp.where(sub // 2 == ty, s, picked)
            mn_ref[tx, ty * 8 : ty * 8 + 8, :] = jnp.where(jnp.full((8, 128), s) >= 0, 1.0, 0.0).astype(F32)
        mv_ref[tx] = jnp.where(picked >= 0, 1.0, 0.0).astype(F32)
        sel.append(jnp.where(picked == lane, 1.0, 0.0).astype(F32))
    selector = jnp.concatenate(sel, axis=0).astype(BF16)[:, :32]

    loads[1].wait()
    def fill(x, c):
        f = feat_ref[x].astype(F32)
        m = mn_ref[x // 8]
        at = pl.multiple_of((x + 3) * PITCH + LEFT, 8)
        for h in range(2):
            p_ref[h, pl.ds(at, WY), :] = f[:, h * 128 : h * 128 + 128] * m
            p_ref[h, pl.ds(at - 8, 8), :] = jnp.zeros((8, 128), F32)
            p_ref[h, pl.ds(at + WY, 8), :] = jnp.zeros((8, 128), F32)
        return c

    lax.fori_loop(0, WX, fill, 0)
    for row in (0, 35):
        p_ref[:, row * PITCH : (row + 3) * PITCH, :] = jnp.zeros((2, 3 * PITCH, 128), F32)

    def pack(e, ref):
        for side, row in ((0, 3), (1, 32)):
            for h in range(2):
                for a in range(3):
                    xp_ref[e, side, h, a] = ref[
                        h, pl.ds((row + a) * PITCH + LEFT, WY), :
                    ].astype(BF16)
        for side, col in ((0, 0), (1, WY - 3)):
            for h in range(2):
                for c in range(3):
                    yp_ref[e, side, h, c] = ref[h, pl.ds(3 * PITCH + LEFT + col + c, WX, stride=PITCH), :].astype(BF16)

    def halo_copies(e):
        def rc(src, dst, k, dev):
            return pltpu.make_async_remote_copy(
                src_ref=src, dst_ref=dst, send_sem=hs_sem.at[e, k], recv_sem=hr_sem.at[e, k], device_id=dev,
                device_id_type=MESH,
            )

        out = []
        for side, step in ((0, -1), (1, 1)):
            out.append(rc(yp_ref.at[e, side], yr_ref.at[e, side], 2 + side, {"sy": at_sy(step)}))
            out.append(rc(xp_ref.at[e, side], xr_ref.at[e, side], side, {"sx": at_sx(step)}))
            out.append(
                rc(yp_ref.at[e, side, :, :, 16:32, :], cr_ref.at[e, 2 * side], 4 + 2 * side,
                   {"sx": at_sx(1), "sy": at_sy(step)})
            )
            out.append(
                rc(yp_ref.at[e, side, :, :, 0:16, :], cr_ref.at[e, 2 * side + 1], 5 + 2 * side,
                   {"sx": at_sx(-1), "sy": at_sy(step)})
            )
        return out

    has_top = sx > 0
    has_bottom = sx < N_SX - 1
    keep_below = jnp.where(has_bottom, 1.0, 0.0).astype(F32)
    keep_above = jnp.where(has_top, 1.0, 0.0).astype(F32)
    keep_right = jnp.where(sy < N_SY - 1, 1.0, 0.0).astype(F32)
    keep_left = jnp.where(sy > 0, 1.0, 0.0).astype(F32)

    def unpack_sides(e, ref):
        for side, col, keep in ((0, LEFT + WY, keep_right), (1, LEFT - 3, keep_left)):
            for h in range(2):
                for c in range(3):
                    ref[h, pl.ds(3 * PITCH + col + c, WX, stride=PITCH), :] = (
                        yr_ref[e, side, h, c].astype(F32) * keep
                    )

    def unpack_ends(e, ref):
        for side, row, keep in ((0, 35, keep_below), (1, 0, keep_above)):
            for h in range(2):
                for a in range(3):
                    ref[h, pl.ds((row + a) * PITCH + LEFT, WY), :] = xr_ref[e, side, h, a].astype(F32) * keep
        for side, col, keep in ((0, LEFT + WY, keep_right), (1, LEFT - 3, keep_left)):
            for h in range(2):
                for c in range(3):
                    top = cr_ref[e, 2 * side, h, c].astype(F32) * (keep * keep_above)
                    ref[h, pl.ds(col + c, 3, stride=PITCH), :] = top[13:16, :]
                    bottom = cr_ref[e, 2 * side + 1, h, c].astype(F32) * (keep * keep_below)
                    ref[h, pl.ds(35 * PITCH + col + c, 3, stride=PITCH), :] = bottom[0:3, :]

    pack(0, p_ref)

    loads[2].wait()
    for q in range(4):
        rg_ref[q] = ret_ref[:, q * 128 : q * 128 + 128].astype(F32)
    for q in range(4):
        for s in range(2):
            pk_ref[pl.ds(2 * q + s, 16, stride=8), :] = rg_ref[q, pl.ds(s, 16, stride=2), :]

    pl.semaphore_wait(barrier, (N_SX - 1) + 2 * (N_SY - 1) + 4)

    for copy in halo_copies(0):
        copy.start()

    def block8(i):
        return pl.ds(pl.multiple_of(i * 8, 8), 8)

    def return_copy(k):
        return pltpu.make_async_remote_copy(
            src_ref=pk_ref.at[block8(at_sx(k))], dst_ref=rv_ref.at[block8(sx)], send_sem=as_sem.at[k],
            recv_sem=ar_sem.at[k], device_id={"sx": at_sx(k)}, device_id_type=MESH,
        )

    def start_return(k, c):
        return_copy(k).start()
        return c

    lax.fori_loop(1, N_SX, start_return, 0)
    rv_ref[block8(sx), :] = pk_ref[block8(sx), :]

    loads[3].wait()
    for h in range(2):
        for a in range(7):
            for b in range(7):
                wb_ref[h, a * 7 + b] = jnp.broadcast_to(cw_ref[a, b : b + 1, h * 128 : h * 128 + 128], (8, 128))

    kg_ref[...] = jnp.zeros_like(kg_ref)

    def add_entry(t, value):
        for h in range(2):
            kg_ref[h, t * 8 : t * 8 + 8, :] += value[:, h * 128 : h * 128 + 128]

    def plane_rows(ref, h, x, n):
        return [ref[h, pl.ds(x * PITCH + (LEFT - 3) + c, 8, stride=4), :] for c in range(n)]

    def depthwise(ref, h, x, flipped):
        sums = [[None] * 4 for _ in range(2)]
        for r in range(8):
            rows = plane_rows(ref, h, x + r, 10)
            for i in range(2):
                a = r - i
                if a < 0 or a > 6:
                    continue
                for b in range(7):
                    t = a * 7 + b
                    w = wb_ref[h, 48 - t if flipped else t]
                    for c in range(4):
                        term = rows[c + b] * w
                        sums[i][c] = term if sums[i][c] is None else sums[i][c] + term
        return sums

    loads[4].wait()

    def conv_step(i, c):
        x = i * 2
        for h in range(2):
            bias = cb_ref[:, h * 128 : h * 128 + 128]
            sums = depthwise(p_ref, h, x, False)
            for k in range(2):
                for q in range(4):
                    co_ref[h, block8((x + k) * 4 + q), :] = sums[k][q] + bias
        return c

    lax.fori_loop(0, WX // 2, conv_step, 0)

    loads[5].wait()

    def wait_return(k, c):
        return_copy(k).wait()
        return c

    lax.fori_loop(1, N_SX, wait_return, 0)
    for q in range(4):
        for s in range(2):
            ar_ref[q, pl.ds(s, 16, stride=2), :] = rv_ref[pl.ds(2 * q + s, 16, stride=8), :]
    arrived = jnp.concatenate([ar_ref[q] for q in range(4)], axis=1).astype(BF16)
    grad_pool = mm(selector, arrived, 1, 0)
    grad_reduced = (grad_pool * (1.0 / 16.0)).astype(BF16)
    gr_ref[...] = grad_reduced
    grad_patch = mm(grad_reduced, dw_ref[...], 1, 1)
    for tx in range(4):
        gp_ref[tx] = grad_patch[tx * 8 : tx * 8 + 8, :]

    off_sum = jnp.sum(grad_pool.reshape(4, 8, 512), axis=0) * 0.5
    for q in range(2):
        add_entry(60 + q, off_sum[:, q * 256 : q * 256 + 256])
    bias_sum = jnp.sum(gp_ref[...], axis=0)
    bias_sum = (
        bias_sum[:, 0:256] + bias_sum[:, 256:512] + bias_sum[:, 512:768] + bias_sum[:, 768:1024]
    ) * 8.0
    add_entry(55, bias_sum)

    for copy in halo_copies(0):
        copy.wait()
    unpack_sides(0, p_ref)

    def side_step(g, c):
        for h in range(2):
            for first_col, taps_of, out_y in (
                (LEFT - 3, ((0, 0, 0), (0, 1, 1), (0, 2, 2), (1, 0, 1), (1, 1, 2), (2, 0, 2)), 0),
                (LEFT + WY, ((0, 6, 0), (1, 5, 0), (1, 6, 1), (2, 4, 0), (2, 5, 1), (2, 6, 2)), 29),
            ):
                sums = [None] * 3
                for a in range(7):
                    cols = [p_ref[h, pl.ds((g * 8 + a) * PITCH + first_col + q, 8, stride=PITCH), :] for q in range(3)]
                    for y, b, q in taps_of:
                        term = cols[q] * wb_ref[h, a * 7 + b]
                        sums[y] = term if sums[y] is None else sums[y] + term
                for y in range(3):
                    row = (out_y + y) % 4 * 8 + (out_y + y) // 4
                    at = pl.ds(g * 256 + row, 8, stride=32)
                    co_ref[h, at, :] = co_ref[h, at, :] + sums[y]
        return c

    lax.fori_loop(0, 4, side_step, 0)
    unpack_ends(0, p_ref)

    def end_step(h, c):
        for first_row, pairs_of in (
            (0, ((0, 0), (0, 1), (0, 2), (1, 0), (1, 1), (2, 0))),
            (29, ((0, 6), (1, 5), (1, 6), (2, 4), (2, 5), (2, 6))),
        ):
            sums = [[None] * 4 for _ in range(3)]
            for x, a in pairs_of:
                rows = plane_rows(p_ref, h, first_row + x + a, 10)
                for b in range(7):
                    w = wb_ref[h, a * 7 + b]
                    for q in range(4):
                        term = rows[q + b] * w
                        sums[x][q] = term if sums[x][q] is None else sums[x][q] + term
            for x in range(3):
                for q in range(4):
                    row = ((first_row + x) * 4 + q) * 8
                    co_ref[h, row : row + 8, :] = co_ref[h, row : row + 8, :] + sums[x][q]
        return c

    lax.fori_loop(0, 2, end_step, 0)

    for load in loads[6:]:
        load.wait()
    r32 = lax.broadcasted_iota(jnp.int32, (32, 256), 0)
    k32 = lax.broadcasted_iota(jnp.int32, (32, 256), 1)
    off_of = (k32 // 32 % 2) * 2 + (k32 // 8 % 4) % 2
    patch_sel = jnp.where(
        (off_of == r32 // 8) & (k32 % 8 // 2 == r32 % 8 // 2) & (r32 % 2 == 0), 1.0, 0.0
    ).astype(BF16)

    def spread(blocks):
        row = [blocks[0], blocks[1]] * 2 + [blocks[2], blocks[3]] * 2
        return jnp.concatenate(row * 4, axis=0)

    def forward(tx, c):
        rows = pl.ds(pl.multiple_of(tx * 256, 256), 256)
        v = jnp.concatenate([co_ref[0, rows, :], co_ref[1, rows, :]], axis=1)
        shifted = v - row_mean(v)
        inv = lax.rsqrt(row_mean(shifted * shifted) + norm_eps)
        normed = shifted * inv
        nc_ref[rows, :] = normed
        inv_ref[rows, :] = jnp.broadcast_to(inv, (256, 128))
        normed_in = (normed * ng_ref[...] + nb_ref[...]).astype(BF16)
        branch = None
        for j in range(4):
            cols = slice(j * 256, j * 256 + 256)
            hid = mm(normed_in, w1_ref[:, cols], 1, 0) + b1_ref[:, cols]
            sq = hid * hid
            t = jnp.tanh(hid * (gelu_scale + (gelu_scale * gelu_cubic) * sq))
            u = 0.5 + 0.5 * t
            act = (hid * u).astype(BF16)
            act_ref[rows, cols] = act
            sl_ref[rows, cols] = u + hid * (u - u * t) * (gelu_scale + (3.0 * gelu_scale * gelu_cubic) * sq)
            part = mm(act, w2_ref[cols, :], 1, 0)
            branch = part if branch is None else branch + part
        branch = branch + b2_ref[...]
        masked = jnp.concatenate(
            [
                jnp.concatenate(
                    [
                        p_ref[h, pl.ds((tx * 8 + x + 3) * PITCH + LEFT + q, 8, stride=4), :]
                        for x in range(8)
                        for q in range(4)
                    ],
                    axis=0,
                )
                for h in range(2)
            ],
            axis=1,
        )
        summed = (masked + ls_ref[...] * branch).astype(BF16).astype(F32)
        shifted = summed - row_mean(summed)
        inv = lax.rsqrt(row_mean(shifted * shifted) + norm_eps)
        normed = shifted * inv
        down_in = (normed * dg_ref[...] + db_ref[...]).astype(BF16)
        ps_ref[tx] = mm(patch_sel, down_in, 1, 0)
        gp = gp_ref[tx]
        blocks = [gp[:, q * 256 : q * 256 + 256] for q in range(4)]
        scaled = [b * dg_ref[...] for b in blocks]
        centred = spread([s - row_mean(s) for s in scaled])
        second = row_mean(spread(scaled) * normed)
        grad_summed = inv * (centred - normed * second)
        for h in range(2):
            gs_ref[h, rows, :] = grad_summed[:, h * 128 : h * 128 + 128]
        add_entry(54, fold8(spread(blocks) * normed))
        add_entry(53, fold8(grad_summed * branch))
        scaled_grad = ls_ref[...] * grad_summed
        add_entry(52, fold8(scaled_grad))
        grad_b = scaled_grad.astype(BF16)
        gb_ref[rows, :] = grad_b
        gbt_ref[:, rows] = grad_b.T
        nit_ref[:, rows] = normed_in.T
        return c

    lax.fori_loop(0, 4, forward, 0)

    def batch(b):
        core_dev = {"sx": sx + 1 - 2 * core}

        def y_dev(k, m):
            x_core = lax.rem(sx, 4) if m == 0 else lax.rem(sx + 2, 4)
            return {"sx": lax.rem(yy + k, 4) * 4 + x_core}

        def z_dev(k, m):
            return {"sy": at_sy(k)} if m == 0 else {"sy": at_sy(k), "sx": sx + 2 - 4 * xl}

        rings = ((yy, y_dev), (sy, z_dev))
        others = [(k, m) for m in range(2) for k in range(4) if (k, m) != (0, 0)]

        def rc(src, dst, k, dev):
            return pltpu.make_async_remote_copy(
                src_ref=src, dst_ref=dst, send_sem=bs_sem.at[b, k], recv_sem=br_sem.at[b, k], device_id=dev,
                device_id_type=MESH,
            )

        def ds(i, n):
            return pl.ds(pl.multiple_of(i, n), n)

        fin = fin_ref.at[b]
        loc = loc_ref.at[b]
        s0, r0, r1 = s0_ref.at[b], r0_ref.at[b], r1_ref.at[b]
        s1, s2, r2 = s1_ref.at[b], s2_ref.at[b], r2_ref.at[b]

        def ring_at(half, k=0):
            return half * 512 + lax.rem(rings[half][0] + k, 4) * 128

        def plane_at(half, k=0, m=0):
            return lax.rem(rings[1 - half][0] + k, 4) * 32 + (xl if m == 0 else 1 - xl) * 16

        def core_in(q):
            return rc(s0.at[ds(q * 256, 256)], r0.at[ds(q * 256, 256)], q, core_dev)

        def ring_in(half, k):
            return rc(s1.at[ds(ring_at(half, k), 128)], r1.at[half, k - 1], 4 + half * 3 + k - 1, rings[half][1](k, 0))

        def plane_in(half, i):
            k, m = others[i]
            return rc(
                s2.at[half, ds(plane_at(half, k, m), 16)], r2.at[half, i], 10 + half * 7 + i, rings[1 - half][1](k, m)
            )

        def plane_out(half, i):
            k, m = others[i]
            at = ds(core * 1024 + ring_at(half) + plane_at(half), 16)
            return rc(fin.at[at], fin.at[at], 24 + half * 7 + i, rings[1 - half][1](k, m))

        def ring_out(half, k):
            at = ds(core * 1024 + ring_at(half), 128)
            return rc(fin.at[at], fin.at[at], 38 + half * 3 + k - 1, rings[half][1](k, 0))

        def core_out(half, k):
            at = ds(core * 1024 + ring_at(half, (4 - k) % 4), 128)
            return rc(fin.at[at], fin.at[at], 44 + half * 4 + k, core_dev)

        def step0(part=None):
            for q in range(4) if part is None else part:
                s0[ds(q * 256, 256), :] = loc[ds((1 - core) * 1024 + q * 256, 256), :].astype(BF16)
                core_in(q).start()

        def step1():
            for half in range(2):
                for q in (2 * half, 2 * half + 1):
                    core_in(q).wait()
                    at = ds(core * 1024 + q * 256, 256)
                    total = loc[at, :] + r0[ds(q * 256, 256), :].astype(F32)
                    loc[at, :] = total
                    s1[ds(q * 256, 256), :] = total.astype(BF16)
                for k in (2, 1, 3):
                    ring_in(half, k).start()

        def step2():
            for half in range(2):
                total = loc[ds(core * 1024 + ring_at(half), 128), :]
                for k in range(1, 4):
                    ring_in(half, k).wait()
                    total = total + r1[half, k - 1].astype(F32)
                loc[ds(core * 1024 + ring_at(half), 128), :] = total
                s2[half] = total.astype(BF16)
                for i in range(7):
                    plane_in(half, i).start()

        def step3():
            for half in range(2):
                at = ds(core * 1024 + ring_at(half) + plane_at(half), 16)
                total = loc[at, :]
                for i in range(7):
                    plane_in(half, i).wait()
                    total = total + r2[half, i].astype(F32)
                fin[at, :] = total.astype(BF16)
                for i in range(7):
                    plane_out(half, i).start()

        def step4():
            for half in range(2):
                for i in range(7):
                    plane_out(half, i).wait()
                for k in (2, 1, 3):
                    ring_out(half, k).start()
                core_out(half, 0).start()

        def step5():
            for half in range(2):
                for k in (1, 3, 2):
                    ring_out(half, k).wait()
                    core_out(half, k).start()

        def out_copies():
            if b == 0:
                return [
                    pltpu.make_async_copy(
                        fin.at[pl.ds(q * 1024, 1024)], down_ref.at[:, q * 256 : q * 256 + 256], out_sem.at[b, q]
                    )
                    for q in range(2)
                ]
            return [
                pltpu.make_async_copy(
                    fin.at[pl.ds(q * 256, 256)], expand_ref.at[:, q * 256 : q * 256 + 256], out_sem.at[b, q]
                )
                for q in range(4)
            ] + [pltpu.make_async_copy(fin.at[pl.ds(1024, 1024)], project_ref, out_sem.at[b, 4])]

        def step6():
            for half in range(2):
                for k in range(4):
                    core_out(half, k).wait()
            for copy in out_copies():
                copy.start()

        def step7():
            for copy in out_copies():
                copy.wait()

        return [step0, step1, step2, step3, step4, step5, step6, step7]

    first = batch(0)
    second = batch(1)

    gr = gr_ref[...]
    gr2 = jnp.concatenate([gr, gr], axis=0)
    pool = None
    for q in range(4):
        sums = ps_ref[:, q * 8 : q * 8 + 8, :].reshape(32, 256)
        high = sums.astype(BF16)
        low = (sums - high.astype(F32)).astype(BF16)
        both = jnp.concatenate([high, low], axis=0)
        grad_down = mm(both, gr2, 0, 0)
        loc_ref[0, q * 256 : q * 256 + 256, :] = grad_down[:, :256]
        loc_ref[0, 1024 + q * 256 : 1024 + q * 256 + 256, :] = grad_down[:, 256:]
        part = mm(both, dw_ref[q * 256 : q * 256 + 256, :], 1, 0)
        part = part[:32] + part[32:]
        pool = part if pool is None else pool + part
    tissue = jnp.concatenate([mv_ref[...].reshape(32, 128)] * 4, axis=1)
    pooled_ref[...] = (pool * (1.0 / 16.0) + do_ref[...]) * tissue
    pooled_out = pltpu.make_async_copy(pooled_ref, pooled_hbm, res_sem.at[0])
    pooled_out.start()
    first[0]()

    def hidden_back(j):
        cols = slice(j * 256, j * 256 + 256)
        grad_hidden = mm(gb_ref[...], w2_ref[cols, :], 1, 1) * sl_ref[:, cols]
        add_entry(56 + j, fold8(grad_hidden))
        grad_hidden_b = grad_hidden.astype(BF16)
        gh_ref[:, cols] = grad_hidden_b
        loc_ref[1, j * 256 : j * 256 + 256, :] = mm(nit_ref[...], grad_hidden_b, 1, 0)
        loc_ref[1, 1024 + j * 256 : 1024 + j * 256 + 256, :] = mm(gbt_ref[...], act_ref[:, cols], 1, 0).T

    hidden_back(0)
    hidden_back(1)
    first[1]()
    hidden_back(2)
    hidden_back(3)
    second[0]()

    def backward(tx, c):
        rows = pl.ds(pl.multiple_of(tx * 256, 256), 256)
        grad_normed = mm(gh_ref[rows, :], w1_ref[...], 1, 1)
        normed = nc_ref[rows, :]
        add_entry(50, fold8(grad_normed * normed))
        add_entry(51, fold8(grad_normed))
        scaled = grad_normed * ng_ref[...]
        inv = inv_ref[rows, :]
        inv = jnp.concatenate([inv, inv], axis=1)
        grad_conv = inv * (scaled - row_mean(scaled) - normed * row_mean(scaled * normed))
        add_entry(49, fold8(grad_conv))
        for h in range(2):
            half = grad_conv[:, h * 128 : h * 128 + 128]
            co_ref[h, rows, :] = half
            for x in range(8):
                for q in range(4):
                    at = (x * 4 + q) * 8
                    pg_ref[h, pl.ds((tx * 8 + x + 3) * PITCH + LEFT + q, 8, stride=4), :] = half[at : at + 8, :]

        @pl.when(tx == 1)
        def _():
            second[1]()

        return c

    lax.fori_loop(0, 4, backward, 0)

    pack(1, pg_ref)
    for copy in halo_copies(1):
        copy.start()

    def taps(a0, n, hooks):
        def half_step(h, c):
            def rows_step(i, sums):
                x = i * 2
                sums = list(sums)
                grads = [[co_ref[h, block8((x + d) * 4 + q), :] for q in range(4)] for d in range(2)]
                for r in range(n + 1):
                    rows = plane_rows(p_ref, h, x + a0 + r, 10)
                    for d in range(2):
                        a = r - d
                        if a < 0 or a >= n:
                            continue
                        for b in range(7):
                            g = grads[d]
                            sums[a * 7 + b] = sums[a * 7 + b] + (
                                (rows[b] * g[0] + rows[b + 1] * g[1]) + (rows[b + 2] * g[2] + rows[b + 3] * g[3])
                            )
                for when, hook in hooks:

                    @pl.when(h * 16 + i == when)
                    def _(hook=hook):
                        hook()

                return tuple(sums)

            sums = lax.fori_loop(0, WX // 2, rows_step, tuple(jnp.zeros((8, 128), F32) for _ in range(7 * n)))
            for t in range(7 * n):
                kg_ref[h, pl.ds((a0 * 7 + t) * 8, 8), :] = sums[t]
            return c

        lax.fori_loop(0, 2, half_step, 0)

    taps(0, 4, ((16, first[2]),))
    taps(4, 3, ((10, second[2]),))

    for h in range(2):
        total = kg_ref[h, pl.ds(0, 64, stride=8), :]
        for s in range(1, 8):
            total = total + kg_ref[h, pl.ds(s, 64, stride=8), :]
        v_ref[h * 64 : h * 64 + 64, :] = total

    def small_rc(src, dst, k, dev):
        return pltpu.make_async_remote_copy(
            src_ref=src, dst_ref=dst, send_sem=vs_sem.at[k], recv_sem=vr_sem.at[k], device_id=dev,
            device_id_type=MESH,
        )

    def small_in(k):
        return small_rc(v_ref.at[block8(at_sx(k))], vr_ref.at[block8(sx)], k, {"sx": at_sx(k)})

    def small_z(k):
        return small_rc(vz_ref.at[sy], vz_ref.at[sy], 15 + k, {"sy": at_sy(k)})

    def small_out(k):
        return small_rc(vf_ref.at[block8(sx)], vf_ref.at[block8(sx)], 18 + k, {"sx": at_sx(k)})

    def each(make, act):
        def body(k, c):
            act(make(k))
            return c

        return body

    def small_step0():
        lax.fori_loop(1, N_SX, each(small_in, lambda copy: copy.start()), 0)
        vr_ref[block8(sx), :] = v_ref[block8(sx), :]

    def small_step1():
        lax.fori_loop(1, N_SX, each(small_in, lambda copy: copy.wait()), 0)
        vz_ref[sy] = jnp.sum(vr_ref[...].reshape(16, 8, 128), axis=0)
        for k in range(1, N_SY):
            small_z(k).start()

    def small_step2():
        for k in range(1, N_SY):
            small_z(k).wait()
        vf_ref[block8(sx), :] = (vz_ref[0] + vz_ref[1]) + (vz_ref[2] + vz_ref[3])
        lax.fori_loop(1, N_SX, each(small_out, lambda copy: copy.start()), 0)

    def small_step3():
        lax.fori_loop(1, N_SX, each(small_out, lambda copy: copy.wait()), 0)
        small_ref[...] = vf_ref[...]

    small_step0()

    for copy in halo_copies(1):
        copy.wait()
    unpack_sides(1, pg_ref)
    unpack_ends(1, pg_ref)

    def back_step(i, c):
        x = i * 2
        keep = mv_ref[x // 8]
        for h in range(2):
            sums = depthwise(pg_ref, h, x, True)
            for k in range(2):
                for q in range(4):
                    value = (sums[k][q] + gs_ref[h, block8((x + k) * 4 + q), :]) * keep
                    nat_ref[h, x + k, pl.ds(q, 8, stride=4), :] = value
        for k in range(2):
            gf_ref[x + k] = jnp.concatenate([nat_ref[0, x + k], nat_ref[1, x + k]], axis=1).astype(BF16)

        for when, hook in ((4, first[3]), (12, second[3])):

            @pl.when(i == when)
            def _(hook=hook):
                hook()

        return c

    lax.fori_loop(0, WX // 2, back_step, 0)
    gf_out = pltpu.make_async_copy(gf_ref, gf_hbm, res_sem.at[1])
    gf_out.start()
    small_step1()
    first[4]()
    second[4]()
    small_step2()
    first[5]()
    second[5]()
    small_step3()
    small_out_copy = pltpu.make_async_copy(small_ref, small_hbm, res_sem.at[2])
    small_out_copy.start()
    first[6]()
    second[6]()
    pooled_out.wait()
    gf_out.wait()
    small_out_copy.wait()
    first[7]()
    second[7]()


def finish_kernel(
    pooled_hbm, gf_hbm, small_hbm, expand_hbm, project_hbm, down_hbm,
    pooled_ref, gf_ref, cw_ref, expand_ref, project_ref, down_ref, vec_ref, eb_ref, do_ref,
    gf_in, pooled_in, small_in, expand_in, project_in, down_in, big_ref, in_sem, sem,
):
    pairs = ((down_hbm, down_in, down_ref), (project_hbm, project_in, project_ref), (expand_hbm, expand_in, expand_ref))
    loads = [pltpu.make_async_copy(src, dst, in_sem.at[k]) for k, (src, dst, _) in enumerate(pairs)]
    loads.append(pltpu.make_async_copy(pooled_hbm, pooled_in, in_sem.at[3]))
    loads.append(pltpu.make_async_copy(small_hbm, small_in, in_sem.at[4]))
    loads.append(pltpu.make_async_copy(gf_hbm, gf_in, in_sem.at[5]))
    for load in loads:
        load.start()
    copies = []
    at = 0
    for load, (_, src, dst) in zip(loads, pairs):
        load.wait()
        rows, lanes = src.shape
        step = 65536 // lanes * 2
        for i in range(0, rows, step):
            k = len(copies)
            view = big_ref.at[pl.ds(at, step), pl.ds(0, lanes)]
            view[...] = src[i : i + step, :].astype(F32)
            copies.append(pltpu.make_async_copy(view, dst.at[pl.ds(i, step)], sem.at[k]))
            copies[-1].start()
            at += step
    loads[5].wait()
    copies.append(pltpu.make_async_copy(gf_in, gf_ref, sem.at[len(copies)]))
    copies[-1].start()
    loads[3].wait()
    loads[4].wait()
    for tx in range(4):
        for ty in range(4):
            pooled_ref[tx, ty : ty + 1, :] = pooled_in[tx * 8 + ty * 2 : tx * 8 + ty * 2 + 1, :].astype(BF16)
    for h in range(2):
        cols = slice(h * 128, h * 128 + 128)
        for a in range(7):
            cw_ref[a, :, cols] = small_in[h * 64 + a * 7 : h * 64 + a * 7 + 7, :]
        vec_ref[:, cols] = small_in[h * 64 + 49 : h * 64 + 56, :]
        for q in range(4):
            eb_ref[:, q * 256 + h * 128 : q * 256 + h * 128 + 128] = small_in[h * 64 + 56 + q : h * 64 + 57 + q, :]
        for q in range(2):
            do_ref[:, q * 256 + h * 128 : q * 256 + h * 128 + 128] = small_in[h * 64 + 60 + q : h * 64 + 61 + q, :]
    for copy in copies:
        copy.wait()


def finish(pooled, grad_features, small, expand, project, down):
    vmem = pl.BlockSpec(memory_space=pltpu.VMEM)
    hbm = pl.BlockSpec(memory_space=pl.ANY)
    out = pl.pallas_call(
        finish_kernel,
        out_shape=(
            jax.ShapeDtypeStruct((4, 4, 512), BF16),
            jax.ShapeDtypeStruct((WX, WY, 256), BF16),
            jax.ShapeDtypeStruct((7, 7, 256), F32),
            jax.ShapeDtypeStruct((256, 1024), F32),
            jax.ShapeDtypeStruct((1024, 256), F32),
            jax.ShapeDtypeStruct((1024, 512), F32),
            jax.ShapeDtypeStruct((7, 256), F32),
            jax.ShapeDtypeStruct((1, 1024), F32),
            jax.ShapeDtypeStruct((1, 512), F32),
        ),
        in_specs=[hbm] * 6,
        out_specs=(vmem, hbm, vmem, hbm, hbm, hbm, vmem, vmem, vmem),
        scratch_shapes=[
            pltpu.VMEM((WX, WY, 256), BF16), pltpu.VMEM((32, 512), F32), pltpu.VMEM((128, 128), F32),
            pltpu.VMEM((256, 1024), BF16),
            pltpu.VMEM((1024, 256), BF16), pltpu.VMEM((1024, 512), BF16), pltpu.VMEM((2304, 1024), F32),
            pltpu.SemaphoreType.DMA((6,)), pltpu.SemaphoreType.DMA((16,)),
        ],
        compiler_params=pltpu.CompilerParams(vmem_limit_bytes=60 * 1024 * 1024),
        cost_estimate=pl.CostEstimate(flops=1_000_000, bytes_accessed=7_000_000, transcendentals=0),
    )(pooled, grad_features, small, expand, project, down)
    return out[:7] + (out[7].reshape(1024), out[8].reshape(512))


def on_device(
    features,
    return_slot,
    returned_grads,
    conv_weight,
    conv_bias,
    norm_gain,
    norm_bias,
    expand_weight,
    expand_bias,
    project_weight,
    project_bias,
    layer_scale,
    down_gain,
    down_bias,
    down_weight,
    down_offset,
):
    hbm = pl.BlockSpec(memory_space=pl.ANY)

    def row(v):
        return v.reshape(1, -1)

    def vm(*shape, dtype=F32):
        return pltpu.VMEM(shape, dtype)

    dma = pltpu.SemaphoreType.DMA
    parts = pl.pallas_call(
        kernel,
        out_shape=(
            jax.ShapeDtypeStruct((32, 512), F32),
            jax.ShapeDtypeStruct((WX, WY, 256), BF16),
            jax.ShapeDtypeStruct((128, 128), F32),
            jax.ShapeDtypeStruct((256, 1024), BF16),
            jax.ShapeDtypeStruct((1024, 256), BF16),
            jax.ShapeDtypeStruct((1024, 512), BF16),
        ),
        in_specs=[hbm] * 16,
        out_specs=(hbm,) * 6,
        scratch_shapes=[
            pltpu.SMEM((4, 4), jnp.int32), vm(WX, WY, 256, dtype=BF16), vm(32, 512, dtype=BF16), vm(7, 7, 256),
            vm(1, 256), vm(1, 256), vm(1, 256), vm(256, 1024, dtype=BF16), vm(1, 1024), vm(1024, 256, dtype=BF16),
            vm(1, 256), vm(1, 256), vm(1, 256), vm(1, 256), vm(1024, 512, dtype=BF16), vm(1, 512),
            vm(32, 512), vm(WX, WY, 256, dtype=BF16), vm(128, 128), dma((16,)), dma((3,)),
            vm(2, PLANE, 128), vm(2, PLANE, 128), vm(2, 2, 2, 3, 32, 128, dtype=BF16),
            vm(2, 2, 2, 3, 32, 128, dtype=BF16), vm(2, 2, 2, 3, 32, 128, dtype=BF16),
            vm(2, 2, 2, 3, 32, 128, dtype=BF16), vm(2, 4, 2, 3, 16, 128, dtype=BF16),
            vm(2, 49, 8, 128), vm(4, 32, 128), vm(4, 8, 128),
            vm(4, 32, 128), vm(128, 128), vm(128, 128), vm(4, 32, 128), vm(32, 512, dtype=BF16), vm(4, 8, 1024),
            vm(4, 32, 256),
            vm(2, 1024, 128), vm(1024, 256), vm(1024, 128), vm(256, 1024, dtype=BF16), vm(256, 1024, dtype=BF16),
            vm(1024, 1024, dtype=BF16), vm(1024, 1024, dtype=BF16),
            vm(1024, 1024), vm(2, 1024, 128), vm(1024, 256, dtype=BF16), vm(2, 32, 32, 128),
            vm(2, 512, 128), vm(128, 128), vm(128, 128), vm(4, 8, 128), vm(128, 128),
            vm(2, 2048, 256), vm(2, 1024, 256, dtype=BF16), vm(2, 1024, 256, dtype=BF16),
            vm(2, 1024, 256, dtype=BF16), vm(2, 2, 3, 128, 256, dtype=BF16),
            vm(2, 2, 128, 256, dtype=BF16), vm(2, 2, 7, 16, 256, dtype=BF16), vm(2, 2048, 256, dtype=BF16),
            dma((2, 8)), dma((2, 8)), dma((16,)), dma((16,)), dma((2, 52)), dma((2, 52)), dma((34,)), dma((34,)),
            dma((2, 5)),
        ],
        compiler_params=pltpu.CompilerParams(
            collective_id=0, has_side_effects=True, vmem_limit_bytes=60 * 1024 * 1024
        ),
        cost_estimate=pl.CostEstimate(flops=4_000_000_000, bytes_accessed=8_000_000, transcendentals=1_000_000),
    )(
        return_slot, features, returned_grads[0], conv_weight, row(conv_bias), row(norm_gain), row(norm_bias),
        expand_weight, row(expand_bias), project_weight, row(project_bias), row(layer_scale), row(down_gain),
        row(down_bias), down_weight, row(down_offset),
    )
    return finish(*parts)


def solution(mesh):
    placed = (
        P(("slide", "sx"), "sy", None),
        P(("slide", "sx"), "sy"),
        P("sy", ("slide", "sx"), None),
    ) + (P(),) * 13
    return jax.shard_map(
        on_device,
        mesh=mesh,
        in_specs=placed,
        out_specs=(
            P(("slide", "sx"), "sy", None),
            P(("slide", "sx"), "sy", None),
            P("slide", None, None),
            P("slide", None),
            P("slide", None),
            P("slide", None),
            P("slide", None),
            P("slide"),
            P("slide"),
        ),
        check_vma=False,
    )
```

```python
import functools

import jax
import jax.numpy as jnp
from jax import lax
from jax.experimental import pallas as pl
from jax.experimental.pallas import tpu as pltpu
from jax.sharding import PartitionSpec as P

F32 = jnp.float32
BF16 = jnp.bfloat16
MESH = pl.DeviceIdType.MESH

norm_eps = 1e-06
gelu_scale = 0.7978845608028654
gelu_cubic = 0.044715

WX = 32
WY = 32
LEFT = 8
PITCH = 48
PLANE = 38 * PITCH
N_SX = 16
N_SY = 4


def mm(a, b, ca, cb):
    return lax.dot_general(a, b, (((ca,), (cb,)), ((), ())), preferred_element_type=F32)


def fold8(v):
    return jnp.sum(v.reshape(v.shape[0] // 8, 8, v.shape[1]), axis=0)


def row_mean(v):
    return jnp.sum(v, axis=-1, keepdims=True) * (1.0 / v.shape[-1])


def kernel(
    slot_hbm, feat_hbm, ret_hbm, cw_hbm, cb_hbm, ng_hbm, nb_hbm, w1_hbm, b1_hbm, w2_hbm, b2_hbm, ls_hbm, dg_hbm,
    db_hbm, dw_hbm, do_hbm,
    pooled_hbm, gf_hbm, small_hbm, expand_ref, project_ref, down_ref,
    slot_ref, feat_ref, ret_ref, cw_ref, cb_ref, ng_ref, nb_ref, w1_ref, b1_ref, w2_ref, b2_ref, ls_ref, dg_ref,
    db_ref, dw_ref, do_ref, pooled_ref, gf_ref, small_ref, in_sem, res_sem,
    p_ref, pg_ref, xp_ref, xr_ref, yp_ref, yr_ref, cr_ref, wb_ref, mn_ref, mv_ref,
    rg_ref, pk_ref, rv_ref, ar_ref, gr_ref, gp_ref, ps_ref,
    co_ref, nc_ref, inv_ref, nit_ref, gbt_ref, gh_ref, act_ref, sl_ref, gs_ref, gb_ref, nat_ref,
    kg_ref, v_ref, vr_ref, vz_ref, vf_ref,
    loc_ref, s0_ref, r0_ref, s1_ref, r1_ref, s2_ref, r2_ref, fin_ref,
    hs_sem, hr_sem, as_sem, ar_sem, bs_sem, br_sem, vs_sem, vr_sem, out_sem,
):
    pairs = (
        (slot_hbm, slot_ref), (feat_hbm, feat_ref), (ret_hbm, ret_ref), (cw_hbm, cw_ref), (cb_hbm, cb_ref),
        (dw_hbm, dw_ref), (w1_hbm, w1_ref), (w2_hbm, w2_ref), (ng_hbm, ng_ref), (nb_hbm, nb_ref), (b1_hbm, b1_ref),
        (b2_hbm, b2_ref), (ls_hbm, ls_ref), (dg_hbm, dg_ref), (db_hbm, db_ref), (do_hbm, do_ref),
    )
    loads = [pltpu.make_async_copy(src, dst, in_sem.at[k]) for k, (src, dst) in enumerate(pairs)]
    for load in loads:
        load.start()

    sx = lax.axis_index("sx")
    sy = lax.axis_index("sy")
    core = lax.rem(sx, 2)
    xl = lax.rem(sx // 2, 2)
    yy = sx // 4

    def at_sx(k):
        return lax.rem(sx + k + N_SX, N_SX)

    def at_sy(k):
        return lax.rem(sy + k + N_SY, N_SY)

    barrier = pltpu.get_barrier_semaphore()

    def greet(k, c):
        pl.semaphore_signal(barrier, inc=1, device_id={"sx": at_sx(k)}, device_id_type=MESH)
        return c

    lax.fori_loop(1, N_SX, greet, 0)
    for k in range(1, N_SY):
        pl.semaphore_signal(barrier, inc=1, device_id={"sy": at_sy(k)}, device_id_type=MESH)
    for k in range(1, N_SY):
        pl.semaphore_signal(
            barrier, inc=1, device_id={"sx": sx + 2 - 4 * xl, "sy": at_sy(k)}, device_id_type=MESH
        )
    for i in (-1, 1):
        for j in (-1, 1):
            pl.semaphore_signal(barrier, inc=1, device_id={"sx": at_sx(i), "sy": at_sy(j)}, device_id_type=MESH)

    loads[0].wait()
    sub = lax.broadcasted_iota(jnp.int32, (8, 128), 0)
    lane = lax.broadcasted_iota(jnp.int32, (8, 128), 1)
    sel = []
    for tx in range(4):
        picked = jnp.zeros((8, 128), jnp.int32)
        for ty in range(4):
            s = slot_ref[tx, ty]
            picked = jnp.where(sub // 2 == ty, s, picked)
            mn_ref[tx, ty * 8 : ty * 8 + 8, :] = jnp.where(jnp.full((8, 128), s) >= 0, 1.0, 0.0).astype(F32)
        mv_ref[tx] = jnp.where(picked >= 0, 1.0, 0.0).astype(F32)
        sel.append(jnp.where(picked == lane, 1.0, 0.0).astype(F32))
    selector = jnp.concatenate(sel, axis=0).astype(BF16)[:, :32]

    loads[1].wait()
    def fill(x, c):
        f = feat_ref[x].astype(F32)
        m = mn_ref[x // 8]
        at = pl.multiple_of((x + 3) * PITCH + LEFT, 8)
        for h in range(2):
            p_ref[h, pl.ds(at, WY), :] = f[:, h * 128 : h * 128 + 128] * m
            p_ref[h, pl.ds(at - 8, 8), :] = jnp.zeros((8, 128), F32)
            p_ref[h, pl.ds(at + WY, 8), :] = jnp.zeros((8, 128), F32)
        return c

    lax.fori_loop(0, WX, fill, 0)
    for row in (0, 35):
        p_ref[:, row * PITCH : (row + 3) * PITCH, :] = jnp.zeros((2, 3 * PITCH, 128), F32)

    def pack(e, ref):
        for side, row in ((0, 3), (1, 32)):
            for h in range(2):
                for a in range(3):
                    xp_ref[e, side, h, a] = ref[
                        h, pl.ds((row + a) * PITCH + LEFT, WY), :
                    ].astype(BF16)
        for side, col in ((0, 0), (1, WY - 3)):
            for h in range(2):
                for c in range(3):
                    yp_ref[e, side, h, c] = ref[h, pl.ds(3 * PITCH + LEFT + col + c, WX, stride=PITCH), :].astype(BF16)

    def halo_copies(e):
        def rc(src, dst, k, dev):
            return pltpu.make_async_remote_copy(
                src_ref=src, dst_ref=dst, send_sem=hs_sem.at[e, k], recv_sem=hr_sem.at[e, k], device_id=dev,
                device_id_type=MESH,
            )

        out = []
        for side, step in ((0, -1), (1, 1)):
            out.append(rc(yp_ref.at[e, side], yr_ref.at[e, side], 2 + side, {"sy": at_sy(step)}))
            out.append(rc(xp_ref.at[e, side], xr_ref.at[e, side], side, {"sx": at_sx(step)}))
            out.append(
                rc(yp_ref.at[e, side, :, :, 16:32, :], cr_ref.at[e, 2 * side], 4 + 2 * side,
                   {"sx": at_sx(1), "sy": at_sy(step)})
            )
            out.append(
                rc(yp_ref.at[e, side, :, :, 0:16, :], cr_ref.at[e, 2 * side + 1], 5 + 2 * side,
                   {"sx": at_sx(-1), "sy": at_sy(step)})
            )
        return out

    has_top = sx > 0
    has_bottom = sx < N_SX - 1
    keep_below = jnp.where(has_bottom, 1.0, 0.0).astype(F32)
    keep_above = jnp.where(has_top, 1.0, 0.0).astype(F32)
    keep_right = jnp.where(sy < N_SY - 1, 1.0, 0.0).astype(F32)
    keep_left = jnp.where(sy > 0, 1.0, 0.0).astype(F32)

    def unpack_sides(e, ref):
        for side, col, keep in ((0, LEFT + WY, keep_right), (1, LEFT - 3, keep_left)):
            for h in range(2):
                for c in range(3):
                    ref[h, pl.ds(3 * PITCH + col + c, WX, stride=PITCH), :] = (
                        yr_ref[e, side, h, c].astype(F32) * keep
                    )

    def unpack_ends(e, ref):
        for side, row, keep in ((0, 35, keep_below), (1, 0, keep_above)):
            for h in range(2):
                for a in range(3):
                    ref[h, pl.ds((row + a) * PITCH + LEFT, WY), :] = xr_ref[e, side, h, a].astype(F32) * keep
        for side, col, keep in ((0, LEFT + WY, keep_right), (1, LEFT - 3, keep_left)):
            for h in range(2):
                for c in range(3):
                    top = cr_ref[e, 2 * side, h, c].astype(F32) * (keep * keep_above)
                    ref[h, pl.ds(col + c, 3, stride=PITCH), :] = top[13:16, :]
                    bottom = cr_ref[e, 2 * side + 1, h, c].astype(F32) * (keep * keep_below)
                    ref[h, pl.ds(35 * PITCH + col + c, 3, stride=PITCH), :] = bottom[0:3, :]

    pack(0, p_ref)

    loads[2].wait()
    for q in range(4):
        rg_ref[q] = ret_ref[:, q * 128 : q * 128 + 128].astype(F32)
    for q in range(4):
        for s in range(2):
            pk_ref[pl.ds(2 * q + s, 16, stride=8), :] = rg_ref[q, pl.ds(s, 16, stride=2), :]

    pl.semaphore_wait(barrier, (N_SX - 1) + 2 * (N_SY - 1) + 4)

    for copy in halo_copies(0):
        copy.start()

    def block8(i):
        return pl.ds(pl.multiple_of(i * 8, 8), 8)

    def return_copy(k):
        return pltpu.make_async_remote_copy(
            src_ref=pk_ref.at[block8(at_sx(k))], dst_ref=rv_ref.at[block8(sx)], send_sem=as_sem.at[k],
            recv_sem=ar_sem.at[k], device_id={"sx": at_sx(k)}, device_id_type=MESH,
        )

    def start_return(k, c):
        return_copy(k).start()
        return c

    lax.fori_loop(1, N_SX, start_return, 0)
    rv_ref[block8(sx), :] = pk_ref[block8(sx), :]

    loads[3].wait()
    for h in range(2):
        for a in range(7):
            for b in range(7):
                wb_ref[h, a * 7 + b] = jnp.broadcast_to(cw_ref[a, b : b + 1, h * 128 : h * 128 + 128], (8, 128))

    kg_ref[...] = jnp.zeros_like(kg_ref)

    def add_entry(t, value):
        for h in range(2):
            kg_ref[h, t * 8 : t * 8 + 8, :] += value[:, h * 128 : h * 128 + 128]

    def plane_rows(ref, h, x, n):
        return [ref[h, pl.ds(x * PITCH + (LEFT - 3) + c, 8, stride=4), :] for c in range(n)]

    def depthwise(ref, h, x, flipped):
        sums = [[None] * 4 for _ in range(2)]
        for r in range(8):
            rows = plane_rows(ref, h, x + r, 10)
            for i in range(2):
                a = r - i
                if a < 0 or a > 6:
                    continue
                for b in range(7):
                    t = a * 7 + b
                    w = wb_ref[h, 48 - t if flipped else t]
                    for c in range(4):
                        term = rows[c + b] * w
                        sums[i][c] = term if sums[i][c] is None else sums[i][c] + term
        return sums

    loads[4].wait()

    def conv_step(i, c):
        x = i * 2
        for h in range(2):
            bias = cb_ref[:, h * 128 : h * 128 + 128]
            sums = depthwise(p_ref, h, x, False)
            for k in range(2):
                for q in range(4):
                    co_ref[h, block8((x + k) * 4 + q), :] = sums[k][q] + bias
        return c

    lax.fori_loop(0, WX // 2, conv_step, 0)

    loads[5].wait()

    def wait_return(k, c):
        return_copy(k).wait()
        return c

    lax.fori_loop(1, N_SX, wait_return, 0)
    for q in range(4):
        for s in range(2):
            ar_ref[q, pl.ds(s, 16, stride=2), :] = rv_ref[pl.ds(2 * q + s, 16, stride=8), :]
    arrived = jnp.concatenate([ar_ref[q] for q in range(4)], axis=1).astype(BF16)
    grad_pool = mm(selector, arrived, 1, 0)
    grad_reduced = (grad_pool * (1.0 / 16.0)).astype(BF16)
    gr_ref[...] = grad_reduced
    grad_patch = mm(grad_reduced, dw_ref[...], 1, 1)
    for tx in range(4):
        gp_ref[tx] = grad_patch[tx * 8 : tx * 8 + 8, :]

    off_sum = jnp.sum(grad_pool.reshape(4, 8, 512), axis=0) * 0.5
    for q in range(2):
        add_entry(60 + q, off_sum[:, q * 256 : q * 256 + 256])
    bias_sum = jnp.sum(gp_ref[...], axis=0)
    bias_sum = (
        bias_sum[:, 0:256] + bias_sum[:, 256:512] + bias_sum[:, 512:768] + bias_sum[:, 768:1024]
    ) * 8.0
    add_entry(55, bias_sum)

    for copy in halo_copies(0):
        copy.wait()
    unpack_sides(0, p_ref)

    def side_step(g, c):
        for h in range(2):
            for first_col, taps_of, out_y in (
                (LEFT - 3, ((0, 0, 0), (0, 1, 1), (0, 2, 2), (1, 0, 1), (1, 1, 2), (2, 0, 2)), 0),
                (LEFT + WY, ((0, 6, 0), (1, 5, 0), (1, 6, 1), (2, 4, 0), (2, 5, 1), (2, 6, 2)), 29),
            ):
                sums = [None] * 3
                for a in range(7):
                    cols = [p_ref[h, pl.ds((g * 8 + a) * PITCH + first_col + q, 8, stride=PITCH), :] for q in range(3)]
                    for y, b, q in taps_of:
                        term = cols[q] * wb_ref[h, a * 7 + b]
                        sums[y] = term if sums[y] is None else sums[y] + term
                for y in range(3):
                    row = (out_y + y) % 4 * 8 + (out_y + y) // 4
                    at = pl.ds(g * 256 + row, 8, stride=32)
                    co_ref[h, at, :] = co_ref[h, at, :] + sums[y]
        return c

    lax.fori_loop(0, 4, side_step, 0)
    unpack_ends(0, p_ref)

    def end_step(h, c):
        for first_row, pairs_of in (
            (0, ((0, 0), (0, 1), (0, 2), (1, 0), (1, 1), (2, 0))),
            (29, ((0, 6), (1, 5), (1, 6), (2, 4), (2, 5), (2, 6))),
        ):
            sums = [[None] * 4 for _ in range(3)]
            for x, a in pairs_of:
                rows = plane_rows(p_ref, h, first_row + x + a, 10)
                for b in range(7):
                    w = wb_ref[h, a * 7 + b]
                    for q in range(4):
                        term = rows[q + b] * w
                        sums[x][q] = term if sums[x][q] is None else sums[x][q] + term
            for x in range(3):
                for q in range(4):
                    row = ((first_row + x) * 4 + q) * 8
                    co_ref[h, row : row + 8, :] = co_ref[h, row : row + 8, :] + sums[x][q]
        return c

    lax.fori_loop(0, 2, end_step, 0)

    for load in loads[6:]:
        load.wait()
    r32 = lax.broadcasted_iota(jnp.int32, (32, 256), 0)
    k32 = lax.broadcasted_iota(jnp.int32, (32, 256), 1)
    off_of = (k32 // 32 % 2) * 2 + (k32 // 8 % 4) % 2
    patch_sel = jnp.where(
        (off_of == r32 // 8) & (k32 % 8 // 2 == r32 % 8 // 2) & (r32 % 2 == 0), 1.0, 0.0
    ).astype(BF16)

    def spread(blocks):
        row = [blocks[0], blocks[1]] * 2 + [blocks[2], blocks[3]] * 2
        return jnp.concatenate(row * 4, axis=0)

    def forward(tx, c):
        rows = pl.ds(tx * 256, 256)
        v = jnp.concatenate([co_ref[0, rows, :], co_ref[1, rows, :]], axis=1)
        shifted = v - row_mean(v)
        inv = lax.rsqrt(row_mean(shifted * shifted) + norm_eps)
        normed = shifted * inv
        nc_ref[rows, :] = normed
        inv_ref[rows, :] = jnp.broadcast_to(inv, (256, 128))
        normed_in = (normed * ng_ref[...] + nb_ref[...]).astype(BF16)
        branch = None
        for j in range(4):
            cols = slice(j * 256, j * 256 + 256)
            hid = mm(normed_in, w1_ref[:, cols], 1, 0) + b1_ref[:, cols]
            sq = hid * hid
            t = jnp.tanh(hid * (gelu_scale + (gelu_scale * gelu_cubic) * sq))
            u = 0.5 + 0.5 * t
            act = (hid * u).astype(BF16)
            act_ref[rows, cols] = act
            sl_ref[rows, cols] = u + hid * (u - u * t) * (gelu_scale + (3.0 * gelu_scale * gelu_cubic) * sq)
            part = mm(act, w2_ref[cols, :], 1, 0)
            branch = part if branch is None else branch + part
        branch = branch + b2_ref[...]
        masked = jnp.concatenate(
            [
                jnp.concatenate(
                    [
                        p_ref[h, pl.ds((tx * 8 + x + 3) * PITCH + LEFT + q, 8, stride=4), :]
                        for x in range(8)
                        for q in range(4)
                    ],
                    axis=0,
                )
                for h in range(2)
            ],
            axis=1,
        )
        summed = (masked + ls_ref[...] * branch).astype(BF16).astype(F32)
        shifted = summed - row_mean(summed)
        inv = lax.rsqrt(row_mean(shifted * shifted) + norm_eps)
        normed = shifted * inv
        down_in = (normed * dg_ref[...] + db_ref[...]).astype(BF16)
        ps_ref[tx] = mm(patch_sel, down_in, 1, 0)
        gp = gp_ref[tx]
        blocks = [gp[:, q * 256 : q * 256 + 256] for q in range(4)]
        scaled = [b * dg_ref[...] for b in blocks]
        centred = spread([s - row_mean(s) for s in scaled])
        second = row_mean(spread(scaled) * normed)
        grad_summed = inv * (centred - normed * second)
        for h in range(2):
            gs_ref[h, rows, :] = grad_summed[:, h * 128 : h * 128 + 128]
        add_entry(54, fold8(spread(blocks) * normed))
        add_entry(53, fold8(grad_summed * branch))
        scaled_grad = ls_ref[...] * grad_summed
        add_entry(52, fold8(scaled_grad))
        grad_b = scaled_grad.astype(BF16)
        gb_ref[rows, :] = grad_b
        gbt_ref[:, rows] = grad_b.T
        nit_ref[:, rows] = normed_in.T
        return c

    for tx in range(4):
        forward(tx, 0)

    def batch(b):
        core_dev = {"sx": sx + 1 - 2 * core}

        def y_dev(k, m):
            x_core = lax.rem(sx, 4) if m == 0 else lax.rem(sx + 2, 4)
            return {"sx": lax.rem(yy + k, 4) * 4 + x_core}

        def z_dev(k, m):
            return {"sy": at_sy(k)} if m == 0 else {"sy": at_sy(k), "sx": sx + 2 - 4 * xl}

        rings = ((yy, y_dev), (sy, z_dev))
        others = [(k, m) for m in range(2) for k in range(4) if (k, m) != (0, 0)]

        def rc(src, dst, k, dev):
            return pltpu.make_async_remote_copy(
                src_ref=src, dst_ref=dst, send_sem=bs_sem.at[b, k], recv_sem=br_sem.at[b, k], device_id=dev,
                device_id_type=MESH,
            )

        def ds(i, n):
            return pl.ds(pl.multiple_of(i, n), n)

        fin = fin_ref.at[b]
        loc = loc_ref.at[b]
        s0, r0, r1 = s0_ref.at[b], r0_ref.at[b], r1_ref.at[b]
        s1, s2, r2 = s1_ref.at[b], s2_ref.at[b], r2_ref.at[b]

        def ring_at(half, k=0):
            return half * 512 + lax.rem(rings[half][0] + k, 4) * 128

        def plane_at(half, k=0, m=0):
            return lax.rem(rings[1 - half][0] + k, 4) * 32 + (xl if m == 0 else 1 - xl) * 16

        def core_in(q):
            return rc(s0.at[ds(q * 256, 256)], r0.at[ds(q * 256, 256)], q, core_dev)

        def ring_in(half, k):
            return rc(s1.at[ds(ring_at(half, k), 128)], r1.at[half, k - 1], 4 + half * 3 + k - 1, rings[half][1](k, 0))

        def plane_in(half, i):
            k, m = others[i]
            return rc(
                s2.at[half, ds(plane_at(half, k, m), 16)], r2.at[half, i], 10 + half * 7 + i, rings[1 - half][1](k, m)
            )

        def plane_out(half, i):
            k, m = others[i]
            at = ds(core * 1024 + ring_at(half) + plane_at(half), 16)
            return rc(fin.at[at], fin.at[at], 24 + half * 7 + i, rings[1 - half][1](k, m))

        def ring_out(half, k):
            at = ds(core * 1024 + ring_at(half), 128)
            return rc(fin.at[at], fin.at[at], 38 + half * 3 + k - 1, rings[half][1](k, 0))

        def core_out(half, k):
            at = ds(core * 1024 + ring_at(half, (4 - k) % 4), 128)
            return rc(fin.at[at], fin.at[at], 44 + half * 4 + k, core_dev)

        def step0(part=None):
            for q in range(4) if part is None else part:
                s0[ds(q * 256, 256), :] = loc[ds((1 - core) * 1024 + q * 256, 256), :].astype(BF16)
                core_in(q).start()

        def step1():
            for half in range(2):
                for q in (2 * half, 2 * half + 1):
                    core_in(q).wait()
                    at = ds(core * 1024 + q * 256, 256)
                    total = loc[at, :] + r0[ds(q * 256, 256), :].astype(F32)
                    loc[at, :] = total
                    s1[ds(q * 256, 256), :] = total.astype(BF16)
                for k in (2, 1, 3):
                    ring_in(half, k).start()

        def step2():
            for half in range(2):
                total = loc[ds(core * 1024 + ring_at(half), 128), :]
                for k in range(1, 4):
                    ring_in(half, k).wait()
                    total = total + r1[half, k - 1].astype(F32)
                loc[ds(core * 1024 + ring_at(half), 128), :] = total
                s2[half] = total.astype(BF16)
                for i in range(7):
                    plane_in(half, i).start()

        def step3():
            for half in range(2):
                at = ds(core * 1024 + ring_at(half) + plane_at(half), 16)
                total = loc[at, :]
                for i in range(7):
                    plane_in(half, i).wait()
                    total = total + r2[half, i].astype(F32)
                fin[at, :] = total.astype(BF16)
                for i in range(7):
                    plane_out(half, i).start()

        def step4():
            for half in range(2):
                for i in range(7):
                    plane_out(half, i).wait()
                for k in (2, 1, 3):
                    ring_out(half, k).start()
                core_out(half, 0).start()

        def step5():
            for half in range(2):
                for k in (1, 3, 2):
                    ring_out(half, k).wait()
                    core_out(half, k).start()

        def out_copies():
            if b == 0:
                return [
                    pltpu.make_async_copy(
                        fin.at[pl.ds(q * 1024, 1024)], down_ref.at[:, q * 256 : q * 256 + 256], out_sem.at[b, q]
                    )
                    for q in range(2)
                ]
            return [
                pltpu.make_async_copy(
                    fin.at[pl.ds(q * 256, 256)], expand_ref.at[:, q * 256 : q * 256 + 256], out_sem.at[b, q]
                )
                for q in range(4)
            ] + [pltpu.make_async_copy(fin.at[pl.ds(1024, 1024)], project_ref, out_sem.at[b, 4])]

        def step6():
            for half in range(2):
                for k in range(4):
                    core_out(half, k).wait()
            for copy in out_copies():
                copy.start()

        def step7():
            for copy in out_copies():
                copy.wait()

        return [step0, step1, step2, step3, step4, step5, step6, step7]

    first = batch(0)
    second = batch(1)

    gr = gr_ref[...]
    gr2 = jnp.concatenate([gr, gr], axis=0)
    pool = None
    for q in range(4):
        sums = ps_ref[:, q * 8 : q * 8 + 8, :].reshape(32, 256)
        high = sums.astype(BF16)
        low = (sums - high.astype(F32)).astype(BF16)
        both = jnp.concatenate([high, low], axis=0)
        grad_down = mm(both, gr2, 0, 0)
        loc_ref[0, q * 256 : q * 256 + 256, :] = grad_down[:, :256]
        loc_ref[0, 1024 + q * 256 : 1024 + q * 256 + 256, :] = grad_down[:, 256:]
        part = mm(both, dw_ref[q * 256 : q * 256 + 256, :], 1, 0)
        part = part[:32] + part[32:]
        pool = part if pool is None else pool + part
    tissue = jnp.concatenate([mv_ref[...].reshape(32, 128)] * 4, axis=1)
    pooled_ref[...] = (pool * (1.0 / 16.0) + do_ref[...]) * tissue
    pooled_out = pltpu.make_async_copy(pooled_ref, pooled_hbm, res_sem.at[0])
    pooled_out.start()
    first[0]()

    def hidden_back(j):
        cols = slice(j * 256, j * 256 + 256)
        grad_hidden = mm(gb_ref[...], w2_ref[cols, :], 1, 1) * sl_ref[:, cols]
        add_entry(56 + j, fold8(grad_hidden))
        grad_hidden_b = grad_hidden.astype(BF16)
        gh_ref[:, cols] = grad_hidden_b
        loc_ref[1, j * 256 : j * 256 + 256, :] = mm(nit_ref[...], grad_hidden_b, 1, 0)
        loc_ref[1, 1024 + j * 256 : 1024 + j * 256 + 256, :] = mm(gbt_ref[...], act_ref[:, cols], 1, 0).T

    hidden_back(0)
    second[0]((0,))
    hidden_back(1)
    second[0]((1,))
    first[1]()
    hidden_back(2)
    second[0]((2,))
    hidden_back(3)
    second[0]((3,))

    def backward(tx, c):
        rows = pl.ds(tx * 256, 256)
        grad_normed = mm(gh_ref[rows, :], w1_ref[...], 1, 1)
        normed = nc_ref[rows, :]
        add_entry(50, fold8(grad_normed * normed))
        add_entry(51, fold8(grad_normed))
        scaled = grad_normed * ng_ref[...]
        inv = inv_ref[rows, :]
        inv = jnp.concatenate([inv, inv], axis=1)
        grad_conv = inv * (scaled - row_mean(scaled) - normed * row_mean(scaled * normed))
        add_entry(49, fold8(grad_conv))
        for h in range(2):
            half = grad_conv[:, h * 128 : h * 128 + 128]
            co_ref[h, rows, :] = half
            for x in range(8):
                for q in range(4):
                    at = (x * 4 + q) * 8
                    pg_ref[h, pl.ds((tx * 8 + x + 3) * PITCH + LEFT + q, 8, stride=4), :] = half[at : at + 8, :]

        return c

    backward(0, 0)
    second[1]()
    for tx in range(1, 4):
        backward(tx, 0)

    pack(1, pg_ref)
    for copy in halo_copies(1):
        copy.start()

    def taps(a0, n, hooks):
        def half_step(h, c):
            def rows_step(i, sums):
                x = i * 2
                sums = list(sums)
                grads = [[co_ref[h, block8((x + d) * 4 + q), :] for q in range(4)] for d in range(2)]
                for r in range(n + 1):
                    rows = plane_rows(p_ref, h, x + a0 + r, 10)
                    for d in range(2):
                        a = r - d
                        if a < 0 or a >= n:
                            continue
                        for b in range(7):
                            g = grads[d]
                            sums[a * 7 + b] = sums[a * 7 + b] + (
                                (rows[b] * g[0] + rows[b + 1] * g[1]) + (rows[b + 2] * g[2] + rows[b + 3] * g[3])
                            )
                return tuple(sums)

            sums = lax.fori_loop(0, WX // 2, rows_step, tuple(jnp.zeros((8, 128), F32) for _ in range(7 * n)))
            for t in range(7 * n):
                kg_ref[h, pl.ds((a0 * 7 + t) * 8, 8), :] = sums[t]
            for when, hook in hooks:

                @pl.when(h == when)
                def _(hook=hook):
                    hook()

            return c

        lax.fori_loop(0, 2, half_step, 0)

    taps(0, 4, ((0, first[2]),))
    taps(4, 3, ((0, second[2]),))

    for h in range(2):
        total = kg_ref[h, pl.ds(0, 64, stride=8), :]
        for s in range(1, 8):
            total = total + kg_ref[h, pl.ds(s, 64, stride=8), :]
        v_ref[h * 64 : h * 64 + 64, :] = total

    def small_rc(src, dst, k, dev):
        return pltpu.make_async_remote_copy(
            src_ref=src, dst_ref=dst, send_sem=vs_sem.at[k], recv_sem=vr_sem.at[k], device_id=dev,
            device_id_type=MESH,
        )

    def small_in(k):
        return small_rc(v_ref.at[block8(at_sx(k))], vr_ref.at[block8(sx)], k, {"sx": at_sx(k)})

    def small_z(k):
        return small_rc(vz_ref.at[sy], vz_ref.at[sy], 15 + k, {"sy": at_sy(k)})

    def small_out(k):
        return small_rc(vf_ref.at[block8(sx)], vf_ref.at[block8(sx)], 18 + k, {"sx": at_sx(k)})

    def each(make, act):
        def body(k, c):
            act(make(k))
            return c

        return body

    def small_step0():
        lax.fori_loop(1, N_SX, each(small_in, lambda copy: copy.start()), 0)
        vr_ref[block8(sx), :] = v_ref[block8(sx), :]

    def small_step1():
        lax.fori_loop(1, N_SX, each(small_in, lambda copy: copy.wait()), 0)
        vz_ref[sy] = jnp.sum(vr_ref[...].reshape(16, 8, 128), axis=0)
        for k in range(1, N_SY):
            small_z(k).start()

    def small_step2():
        for k in range(1, N_SY):
            small_z(k).wait()
        vf_ref[block8(sx), :] = (vz_ref[0] + vz_ref[1]) + (vz_ref[2] + vz_ref[3])
        lax.fori_loop(1, N_SX, each(small_out, lambda copy: copy.start()), 0)

    def small_step3():
        lax.fori_loop(1, N_SX, each(small_out, lambda copy: copy.wait()), 0)
        small_ref[...] = vf_ref[...]

    small_step0()

    for copy in halo_copies(1):
        copy.wait()
    unpack_sides(1, pg_ref)
    unpack_ends(1, pg_ref)

    def back_step(i, c):
        x = i * 2
        keep = mv_ref[x // 8]
        for h in range(2):
            sums = depthwise(pg_ref, h, x, True)
            for k in range(2):
                for q in range(4):
                    value = (sums[k][q] + gs_ref[h, block8((x + k) * 4 + q), :]) * keep
                    nat_ref[h, x + k, pl.ds(q, 8, stride=4), :] = value
        for k in range(2):
            gf_ref[x + k] = jnp.concatenate([nat_ref[0, x + k], nat_ref[1, x + k]], axis=1).astype(BF16)

        return c

    def back_part(g, c):
        lax.fori_loop(g * 4, g * 4 + 4, back_step, 0)
        for when, hook in ((0, first[3]), (2, second[3]),):

            @pl.when(g == when)
            def _(hook=hook):
                hook()

        return c

    lax.fori_loop(0, 4, back_part, 0)
    gf_out = pltpu.make_async_copy(gf_ref, gf_hbm, res_sem.at[1])
    gf_out.start()
    small_step1()
    first[4]()
    second[4]()
    small_step2()
    first[5]()
    second[5]()
    small_step3()
    small_out_copy = pltpu.make_async_copy(small_ref, small_hbm, res_sem.at[2])
    small_out_copy.start()
    first[6]()
    second[6]()
    pooled_out.wait()
    gf_out.wait()
    small_out_copy.wait()
    first[7]()
    second[7]()


def finish_kernel(
    pooled_hbm, gf_hbm, small_hbm, expand_hbm, project_hbm, down_hbm,
    pooled_out, gf_out, cw_out, expand_out, project_out, down_out, vec_out, eb_out, do_out,
    gf_in, pooled_in, small_in, expand_in, project_in, down_in, big_ref,
    pooled_ref, cw_ref, vec_ref, eb_ref, do_ref, in_sem, sem,
):
    loads = []

    def load(src, dst):
        loads.append(pltpu.make_async_copy(src, dst, in_sem.at[len(loads)]))
        loads[-1].start()

    stores = []

    def store(src, dst):
        stores.append(pltpu.make_async_copy(src, dst, sem.at[len(stores)]))
        stores[-1].start()

    load(pooled_hbm, pooled_in)
    load(small_hbm, small_in)
    pieces = []
    for src, mid, dst in (
        (down_hbm, down_in, down_out), (project_hbm, project_in, project_out), (expand_hbm, expand_in, expand_out)
    ):
        rows, lanes = src.shape
        step = 131072 // lanes
        for i in range(0, rows, step):
            load(src.at[pl.ds(i, step)], mid.at[pl.ds(i, step)])
            pieces.append((mid, dst, i, step, lanes))
    load(gf_hbm, gf_in)

    loads[0].wait()
    for tx in range(4):
        for ty in range(4):
            pooled_ref[tx, ty : ty + 1, :] = pooled_in[tx * 8 + ty * 2 : tx * 8 + ty * 2 + 1, :].astype(BF16)
    store(pooled_ref, pooled_out)
    loads[1].wait()
    for h in range(2):
        cols = slice(h * 128, h * 128 + 128)
        for a in range(7):
            cw_ref[a, :, cols] = small_in[h * 64 + a * 7 : h * 64 + a * 7 + 7, :]
        vec_ref[:, cols] = small_in[h * 64 + 49 : h * 64 + 56, :]
        for q in range(4):
            eb_ref[:, q * 256 + h * 128 : q * 256 + h * 128 + 128] = small_in[h * 64 + 56 + q : h * 64 + 57 + q, :]
        for q in range(2):
            do_ref[:, q * 256 + h * 128 : q * 256 + h * 128 + 128] = small_in[h * 64 + 60 + q : h * 64 + 61 + q, :]
    for src, dst in ((cw_ref, cw_out), (vec_ref, vec_out), (eb_ref, eb_out), (do_ref, do_out)):
        store(src, dst)
    at = 0
    for k, (mid, dst, i, step, lanes) in enumerate(pieces):
        loads[2 + k].wait()
        view = big_ref.at[pl.ds(at, step), pl.ds(0, lanes)]
        view[...] = mid[i : i + step, :].astype(F32)
        store(view, dst.at[pl.ds(i, step)])
        at += step
    loads[-1].wait()
    store(gf_in, gf_out)
    for copy in stores:
        copy.wait()


def finish(pooled, grad_features, small, expand, project, down):
    hbm = pl.BlockSpec(memory_space=pl.ANY)
    out = pl.pallas_call(
        finish_kernel,
        out_shape=(
            jax.ShapeDtypeStruct((4, 4, 512), BF16),
            jax.ShapeDtypeStruct((WX, WY, 256), BF16),
            jax.ShapeDtypeStruct((7, 7, 256), F32),
            jax.ShapeDtypeStruct((256, 1024), F32),
            jax.ShapeDtypeStruct((1024, 256), F32),
            jax.ShapeDtypeStruct((1024, 512), F32),
            jax.ShapeDtypeStruct((7, 256), F32),
            jax.ShapeDtypeStruct((1, 1024), F32),
            jax.ShapeDtypeStruct((1, 512), F32),
        ),
        in_specs=[hbm] * 6,
        out_specs=(hbm,) * 9,
        scratch_shapes=[
            pltpu.VMEM((WX, WY, 256), BF16), pltpu.VMEM((32, 512), F32), pltpu.VMEM((128, 128), F32),
            pltpu.VMEM((256, 1024), BF16),
            pltpu.VMEM((1024, 256), BF16), pltpu.VMEM((1024, 512), BF16), pltpu.VMEM((2304, 1024), F32),
            pltpu.VMEM((4, 4, 512), BF16), pltpu.VMEM((7, 7, 256), F32), pltpu.VMEM((7, 256), F32),
            pltpu.VMEM((1, 1024), F32), pltpu.VMEM((1, 512), F32),
            pltpu.SemaphoreType.DMA((11,)), pltpu.SemaphoreType.DMA((14,)),
        ],
        compiler_params=pltpu.CompilerParams(vmem_limit_bytes=60 * 1024 * 1024),
        cost_estimate=pl.CostEstimate(flops=1_000_000, bytes_accessed=7_000_000, transcendentals=0),
    )(pooled, grad_features, small, expand, project, down)
    return out[:7] + (out[7].reshape(1024), out[8].reshape(512))


def on_device(
    features,
    return_slot,
    returned_grads,
    conv_weight,
    conv_bias,
    norm_gain,
    norm_bias,
    expand_weight,
    expand_bias,
    project_weight,
    project_bias,
    layer_scale,
    down_gain,
    down_bias,
    down_weight,
    down_offset,
):
    hbm = pl.BlockSpec(memory_space=pl.ANY)

    def row(v):
        return v.reshape(1, -1)

    def vm(*shape, dtype=F32):
        return pltpu.VMEM(shape, dtype)

    dma = pltpu.SemaphoreType.DMA
    parts = pl.pallas_call(
        kernel,
        out_shape=(
            jax.ShapeDtypeStruct((32, 512), F32),
            jax.ShapeDtypeStruct((WX, WY, 256), BF16),
            jax.ShapeDtypeStruct((128, 128), F32),
            jax.ShapeDtypeStruct((256, 1024), BF16),
            jax.ShapeDtypeStruct((1024, 256), BF16),
            jax.ShapeDtypeStruct((1024, 512), BF16),
        ),
        in_specs=[hbm] * 16,
        out_specs=(hbm,) * 6,
        scratch_shapes=[
            pltpu.SMEM((4, 4), jnp.int32), vm(WX, WY, 256, dtype=BF16), vm(32, 512, dtype=BF16), vm(7, 7, 256),
            vm(1, 256), vm(1, 256), vm(1, 256), vm(256, 1024, dtype=BF16), vm(1, 1024), vm(1024, 256, dtype=BF16),
            vm(1, 256), vm(1, 256), vm(1, 256), vm(1, 256), vm(1024, 512, dtype=BF16), vm(1, 512),
            vm(32, 512), vm(WX, WY, 256, dtype=BF16), vm(128, 128), dma((16,)), dma((3,)),
            vm(2, PLANE, 128), vm(2, PLANE, 128), vm(2, 2, 2, 3, 32, 128, dtype=BF16),
            vm(2, 2, 2, 3, 32, 128, dtype=BF16), vm(2, 2, 2, 3, 32, 128, dtype=BF16),
            vm(2, 2, 2, 3, 32, 128, dtype=BF16), vm(2, 4, 2, 3, 16, 128, dtype=BF16),
            vm(2, 49, 8, 128), vm(4, 32, 128), vm(4, 8, 128),
            vm(4, 32, 128), vm(128, 128), vm(128, 128), vm(4, 32, 128), vm(32, 512, dtype=BF16), vm(4, 8, 1024),
            vm(4, 32, 256),
            vm(2, 1024, 128), vm(1024, 256), vm(1024, 128), vm(256, 1024, dtype=BF16), vm(256, 1024, dtype=BF16),
            vm(1024, 1024, dtype=BF16), vm(1024, 1024, dtype=BF16),
            vm(1024, 1024), vm(2, 1024, 128), vm(1024, 256, dtype=BF16), vm(2, 32, 32, 128),
            vm(2, 512, 128), vm(128, 128), vm(128, 128), vm(4, 8, 128), vm(128, 128),
            vm(2, 2048, 256), vm(2, 1024, 256, dtype=BF16), vm(2, 1024, 256, dtype=BF16),
            vm(2, 1024, 256, dtype=BF16), vm(2, 2, 3, 128, 256, dtype=BF16),
            vm(2, 2, 128, 256, dtype=BF16), vm(2, 2, 7, 16, 256, dtype=BF16), vm(2, 2048, 256, dtype=BF16),
            dma((2, 8)), dma((2, 8)), dma((16,)), dma((16,)), dma((2, 52)), dma((2, 52)), dma((34,)), dma((34,)),
            dma((2, 5)),
        ],
        compiler_params=pltpu.CompilerParams(
            collective_id=0, has_side_effects=True, vmem_limit_bytes=60 * 1024 * 1024
        ),
        cost_estimate=pl.CostEstimate(flops=4_000_000_000, bytes_accessed=8_000_000, transcendentals=1_000_000),
    )(
        return_slot, features, returned_grads[0], conv_weight, row(conv_bias), row(norm_gain), row(norm_bias),
        expand_weight, row(expand_bias), project_weight, row(project_bias), row(layer_scale), row(down_gain),
        row(down_bias), down_weight, row(down_offset),
    )
    return finish(*parts)


def solution(mesh):
    placed = (
        P(("slide", "sx"), "sy", None),
        P(("slide", "sx"), "sy"),
        P("sy", ("slide", "sx"), None),
    ) + (P(),) * 13
    return jax.shard_map(
        on_device,
        mesh=mesh,
        in_specs=placed,
        out_specs=(
            P(("slide", "sx"), "sy", None),
            P(("slide", "sx"), "sy", None),
            P("slide", None, None),
            P("slide", None),
            P("slide", None),
            P("slide", None),
            P("slide", None),
            P("slide"),
            P("slide"),
        ),
        check_vma=False,
    )
```

```python
import functools

import jax
import jax.numpy as jnp
from jax import lax
from jax.experimental import pallas as pl
from jax.experimental.pallas import tpu as pltpu
from jax.sharding import PartitionSpec as P

F32 = jnp.float32
BF16 = jnp.bfloat16
MESH = pl.DeviceIdType.MESH

norm_eps = 1e-06
gelu_scale = 0.7978845608028654
gelu_cubic = 0.044715

WX = 32
WY = 32
LEFT = 8
PITCH = 48
PLANE = 38 * PITCH
N_SX = 16
N_SY = 4


def mm(a, b, ca, cb):
    return lax.dot_general(a, b, (((ca,), (cb,)), ((), ())), preferred_element_type=F32)


def fold8(v):
    return jnp.sum(v.reshape(v.shape[0] // 8, 8, v.shape[1]), axis=0)


def row_mean(v):
    return jnp.sum(v, axis=-1, keepdims=True) * (1.0 / v.shape[-1])


def kernel(
    slot_hbm, feat_hbm, ret_hbm, cw_hbm, cb_hbm, ng_hbm, nb_hbm, w1_hbm, b1_hbm, w2_hbm, b2_hbm, ls_hbm, dg_hbm,
    db_hbm, dw_hbm, do_hbm,
    pooled_ref, gf_ref, small_ref, expand_ref, project_ref, down_ref,
    slot_ref, feat_ref, ret_ref, cw_ref, cb_ref, ng_ref, nb_ref, w1_ref, b1_ref, w2_ref, b2_ref, ls_ref, dg_ref,
    db_ref, dw_ref, do_ref, in_sem,
    p_ref, pg_ref, xp_ref, xr_ref, yp_ref, yr_ref, cr_ref, wb_ref, mn_ref, mv_ref,
    rg_ref, pk_ref, rv_ref, ar_ref, gr_ref, gp_ref, ps_ref,
    co_ref, nc_ref, inv_ref, nit_ref, gbt_ref, gh_ref, act_ref, sl_ref, gs_ref, gb_ref, nat_ref,
    kg_ref, v_ref, vr_ref, vz_ref, vf_ref,
    loc_ref, s0_ref, r0_ref, s1_ref, r1_ref, s2_ref, r2_ref, fin_ref,
    hs_sem, hr_sem, as_sem, ar_sem, bs_sem, br_sem, vs_sem, vr_sem, out_sem,
):
    pairs = (
        (slot_hbm, slot_ref), (feat_hbm, feat_ref), (ret_hbm, ret_ref), (cw_hbm, cw_ref), (cb_hbm, cb_ref),
        (dw_hbm, dw_ref), (w1_hbm, w1_ref), (w2_hbm, w2_ref), (ng_hbm, ng_ref), (nb_hbm, nb_ref), (b1_hbm, b1_ref),
        (b2_hbm, b2_ref), (ls_hbm, ls_ref), (dg_hbm, dg_ref), (db_hbm, db_ref), (do_hbm, do_ref),
    )
    loads = [pltpu.make_async_copy(src, dst, in_sem.at[k]) for k, (src, dst) in enumerate(pairs)]
    for load in loads:
        load.start()

    sx = lax.axis_index("sx")
    sy = lax.axis_index("sy")
    core = lax.rem(sx, 2)
    xl = lax.rem(sx // 2, 2)
    yy = sx // 4

    def at_sx(k):
        return lax.rem(sx + k + N_SX, N_SX)

    def at_sy(k):
        return lax.rem(sy + k + N_SY, N_SY)

    barrier = pltpu.get_barrier_semaphore()

    def greet(k, c):
        pl.semaphore_signal(barrier, inc=1, device_id={"sx": at_sx(k)}, device_id_type=MESH)
        return c

    lax.fori_loop(1, N_SX, greet, 0)
    for k in range(1, N_SY):
        pl.semaphore_signal(barrier, inc=1, device_id={"sy": at_sy(k)}, device_id_type=MESH)
    for k in range(1, N_SY):
        pl.semaphore_signal(
            barrier, inc=1, device_id={"sx": sx + 2 - 4 * xl, "sy": at_sy(k)}, device_id_type=MESH
        )
    for i in (-1, 1):
        for j in (-1, 1):
            pl.semaphore_signal(barrier, inc=1, device_id={"sx": at_sx(i), "sy": at_sy(j)}, device_id_type=MESH)

    loads[0].wait()
    sub = lax.broadcasted_iota(jnp.int32, (8, 128), 0)
    lane = lax.broadcasted_iota(jnp.int32, (8, 128), 1)
    sel = []
    for tx in range(4):
        picked = jnp.zeros((8, 128), jnp.int32)
        for ty in range(4):
            s = slot_ref[tx, ty]
            picked = jnp.where(sub // 2 == ty, s, picked)
            mn_ref[tx, ty * 8 : ty * 8 + 8, :] = jnp.where(jnp.full((8, 128), s) >= 0, 1.0, 0.0).astype(F32)
        mv_ref[tx] = jnp.where(picked >= 0, 1.0, 0.0).astype(F32)
        sel.append(jnp.where(picked == lane, 1.0, 0.0).astype(F32))
    selector = jnp.concatenate(sel, axis=0).astype(BF16)[:, :32]

    loads[1].wait()
    def fill(x, c):
        f = feat_ref[x].astype(F32)
        m = mn_ref[x // 8]
        at = pl.multiple_of((x + 3) * PITCH + LEFT, 8)
        for h in range(2):
            p_ref[h, pl.ds(at, WY), :] = f[:, h * 128 : h * 128 + 128] * m
            p_ref[h, pl.ds(at - 8, 8), :] = jnp.zeros((8, 128), F32)
            p_ref[h, pl.ds(at + WY, 8), :] = jnp.zeros((8, 128), F32)
        return c

    lax.fori_loop(0, WX, fill, 0)
    for row in (0, 35):
        p_ref[:, row * PITCH : (row + 3) * PITCH, :] = jnp.zeros((2, 3 * PITCH, 128), F32)

    def pack(e, ref):
        for side, row in ((0, 3), (1, 32)):
            for h in range(2):
                for a in range(3):
                    xp_ref[e, side, h, a] = ref[
                        h, pl.ds((row + a) * PITCH + LEFT, WY), :
                    ].astype(BF16)
        for side, col in ((0, 0), (1, WY - 3)):
            for h in range(2):
                for c in range(3):
                    yp_ref[e, side, h, c] = ref[h, pl.ds(3 * PITCH + LEFT + col + c, WX, stride=PITCH), :].astype(BF16)

    def halo_copies(e):
        def rc(src, dst, k, dev):
            return pltpu.make_async_remote_copy(
                src_ref=src, dst_ref=dst, send_sem=hs_sem.at[e, k], recv_sem=hr_sem.at[e, k], device_id=dev,
                device_id_type=MESH,
            )

        out = []
        for side, step in ((0, -1), (1, 1)):
            out.append(rc(yp_ref.at[e, side], yr_ref.at[e, side], 2 + side, {"sy": at_sy(step)}))
            out.append(rc(xp_ref.at[e, side], xr_ref.at[e, side], side, {"sx": at_sx(step)}))
            out.append(
                rc(yp_ref.at[e, side, :, :, 16:32, :], cr_ref.at[e, 2 * side], 4 + 2 * side,
                   {"sx": at_sx(1), "sy": at_sy(step)})
            )
            out.append(
                rc(yp_ref.at[e, side, :, :, 0:16, :], cr_ref.at[e, 2 * side + 1], 5 + 2 * side,
                   {"sx": at_sx(-1), "sy": at_sy(step)})
            )
        return out

    has_top = sx > 0
    has_bottom = sx < N_SX - 1
    keep_below = jnp.where(has_bottom, 1.0, 0.0).astype(F32)
    keep_above = jnp.where(has_top, 1.0, 0.0).astype(F32)
    keep_right = jnp.where(sy < N_SY - 1, 1.0, 0.0).astype(F32)
    keep_left = jnp.where(sy > 0, 1.0, 0.0).astype(F32)

    def unpack_sides(e, ref):
        for side, col, keep in ((0, LEFT + WY, keep_right), (1, LEFT - 3, keep_left)):
            for h in range(2):
                for c in range(3):
                    ref[h, pl.ds(3 * PITCH + col + c, WX, stride=PITCH), :] = (
                        yr_ref[e, side, h, c].astype(F32) * keep
                    )

    def unpack_ends(e, ref):
        for side, row, keep in ((0, 35, keep_below), (1, 0, keep_above)):
            for h in range(2):
                for a in range(3):
                    ref[h, pl.ds((row + a) * PITCH + LEFT, WY), :] = xr_ref[e, side, h, a].astype(F32) * keep
        for side, col, keep in ((0, LEFT + WY, keep_right), (1, LEFT - 3, keep_left)):
            for h in range(2):
                for c in range(3):
                    top = cr_ref[e, 2 * side, h, c].astype(F32) * (keep * keep_above)
                    ref[h, pl.ds(col + c, 3, stride=PITCH), :] = top[13:16, :]
                    bottom = cr_ref[e, 2 * side + 1, h, c].astype(F32) * (keep * keep_below)
                    ref[h, pl.ds(35 * PITCH + col + c, 3, stride=PITCH), :] = bottom[0:3, :]

    pack(0, p_ref)

    loads[2].wait()
    for q in range(4):
        rg_ref[q] = ret_ref[:, q * 128 : q * 128 + 128].astype(F32)
    for q in range(4):
        for s in range(2):
            pk_ref[pl.ds(2 * q + s, 16, stride=8), :] = rg_ref[q, pl.ds(s, 16, stride=2), :]

    pl.semaphore_wait(barrier, (N_SX - 1) + 2 * (N_SY - 1) + 4)

    for copy in halo_copies(0):
        copy.start()

    def block8(i):
        return pl.ds(pl.multiple_of(i * 8, 8), 8)

    def return_copy(k):
        return pltpu.make_async_remote_copy(
            src_ref=pk_ref.at[block8(at_sx(k))], dst_ref=rv_ref.at[block8(sx)], send_sem=as_sem.at[k],
            recv_sem=ar_sem.at[k], device_id={"sx": at_sx(k)}, device_id_type=MESH,
        )

    def start_return(k, c):
        return_copy(k).start()
        return c

    lax.fori_loop(1, N_SX, start_return, 0)
    rv_ref[block8(sx), :] = pk_ref[block8(sx), :]

    loads[3].wait()
    for h in range(2):
        for a in range(7):
            for b in range(7):
                wb_ref[h, a * 7 + b] = jnp.broadcast_to(cw_ref[a, b : b + 1, h * 128 : h * 128 + 128], (8, 128))

    kg_ref[...] = jnp.zeros_like(kg_ref)

    def add_entry(t, value):
        for h in range(2):
            kg_ref[h, t * 8 : t * 8 + 8, :] += value[:, h * 128 : h * 128 + 128]

    def plane_rows(ref, h, x, n):
        return [ref[h, pl.ds(x * PITCH + (LEFT - 3) + c, 8, stride=4), :] for c in range(n)]

    def depthwise(ref, h, x, flipped):
        sums = [[None] * 4 for _ in range(2)]
        for r in range(8):
            rows = plane_rows(ref, h, x + r, 10)
            for i in range(2):
                a = r - i
                if a < 0 or a > 6:
                    continue
                for b in range(7):
                    t = a * 7 + b
                    w = wb_ref[h, 48 - t if flipped else t]
                    for c in range(4):
                        term = rows[c + b] * w
                        sums[i][c] = term if sums[i][c] is None else sums[i][c] + term
        return sums

    loads[4].wait()

    def conv_step(i, c):
        x = i * 2
        for h in range(2):
            bias = cb_ref[:, h * 128 : h * 128 + 128]
            sums = depthwise(p_ref, h, x, False)
            for k in range(2):
                for q in range(4):
                    co_ref[h, block8((x + k) * 4 + q), :] = sums[k][q] + bias
        return c

    lax.fori_loop(0, WX // 2, conv_step, 0)

    loads[5].wait()

    def wait_return(k, c):
        return_copy(k).wait()
        return c

    lax.fori_loop(1, N_SX, wait_return, 0)
    for q in range(4):
        for s in range(2):
            ar_ref[q, pl.ds(s, 16, stride=2), :] = rv_ref[pl.ds(2 * q + s, 16, stride=8), :]
    arrived = jnp.concatenate([ar_ref[q] for q in range(4)], axis=1).astype(BF16)
    grad_pool = mm(selector, arrived, 1, 0)
    grad_reduced = (grad_pool * (1.0 / 16.0)).astype(BF16)
    gr_ref[...] = grad_reduced
    grad_patch = mm(grad_reduced, dw_ref[...], 1, 1)
    for tx in range(4):
        gp_ref[tx] = grad_patch[tx * 8 : tx * 8 + 8, :]

    off_sum = jnp.sum(grad_pool.reshape(4, 8, 512), axis=0) * 0.5
    for q in range(2):
        add_entry(60 + q, off_sum[:, q * 256 : q * 256 + 256])
    bias_sum = jnp.sum(gp_ref[...], axis=0)
    bias_sum = (
        bias_sum[:, 0:256] + bias_sum[:, 256:512] + bias_sum[:, 512:768] + bias_sum[:, 768:1024]
    ) * 8.0
    add_entry(55, bias_sum)

    for copy in halo_copies(0):
        copy.wait()
    unpack_sides(0, p_ref)

    def side_step(g, c):
        for h in range(2):
            for first_col, taps_of, out_y in (
                (LEFT - 3, ((0, 0, 0), (0, 1, 1), (0, 2, 2), (1, 0, 1), (1, 1, 2), (2, 0, 2)), 0),
                (LEFT + WY, ((0, 6, 0), (1, 5, 0), (1, 6, 1), (2, 4, 0), (2, 5, 1), (2, 6, 2)), 29),
            ):
                sums = [None] * 3
                for a in range(7):
                    cols = [p_ref[h, pl.ds((g * 8 + a) * PITCH + first_col + q, 8, stride=PITCH), :] for q in range(3)]
                    for y, b, q in taps_of:
                        term = cols[q] * wb_ref[h, a * 7 + b]
                        sums[y] = term if sums[y] is None else sums[y] + term
                for y in range(3):
                    row = (out_y + y) % 4 * 8 + (out_y + y) // 4
                    at = pl.ds(g * 256 + row, 8, stride=32)
                    co_ref[h, at, :] = co_ref[h, at, :] + sums[y]
        return c

    lax.fori_loop(0, 4, side_step, 0)
    unpack_ends(0, p_ref)

    def end_step(h, c):
        for first_row, pairs_of in (
            (0, ((0, 0), (0, 1), (0, 2), (1, 0), (1, 1), (2, 0))),
            (29, ((0, 6), (1, 5), (1, 6), (2, 4), (2, 5), (2, 6))),
        ):
            sums = [[None] * 4 for _ in range(3)]
            for x, a in pairs_of:
                rows = plane_rows(p_ref, h, first_row + x + a, 10)
                for b in range(7):
                    w = wb_ref[h, a * 7 + b]
                    for q in range(4):
                        term = rows[q + b] * w
                        sums[x][q] = term if sums[x][q] is None else sums[x][q] + term
            for x in range(3):
                for q in range(4):
                    row = ((first_row + x) * 4 + q) * 8
                    co_ref[h, row : row + 8, :] = co_ref[h, row : row + 8, :] + sums[x][q]
        return c

    lax.fori_loop(0, 2, end_step, 0)

    for load in loads[6:]:
        load.wait()
    r32 = lax.broadcasted_iota(jnp.int32, (32, 256), 0)
    k32 = lax.broadcasted_iota(jnp.int32, (32, 256), 1)
    off_of = (k32 // 32 % 2) * 2 + (k32 // 8 % 4) % 2
    patch_sel = jnp.where(
        (off_of == r32 // 8) & (k32 % 8 // 2 == r32 % 8 // 2) & (r32 % 2 == 0), 1.0, 0.0
    ).astype(BF16)

    def spread(blocks):
        row = [blocks[0], blocks[1]] * 2 + [blocks[2], blocks[3]] * 2
        return jnp.concatenate(row * 4, axis=0)

    def forward(tx, c):
        rows = pl.ds(tx * 256, 256)
        v = jnp.concatenate([co_ref[0, rows, :], co_ref[1, rows, :]], axis=1)
        shifted = v - row_mean(v)
        inv = lax.rsqrt(row_mean(shifted * shifted) + norm_eps)
        normed = shifted * inv
        nc_ref[rows, :] = normed
        inv_ref[rows, :] = jnp.broadcast_to(inv, (256, 128))
        normed_in = (normed * ng_ref[...] + nb_ref[...]).astype(BF16)
        branch = None
        for j in range(4):
            cols = slice(j * 256, j * 256 + 256)
            hid = mm(normed_in, w1_ref[:, cols], 1, 0) + b1_ref[:, cols]
            sq = hid * hid
            t = jnp.tanh(hid * (gelu_scale + (gelu_scale * gelu_cubic) * sq))
            u = 0.5 + 0.5 * t
            act = (hid * u).astype(BF16)
            act_ref[rows, cols] = act
            sl_ref[rows, cols] = u + hid * (u - u * t) * (gelu_scale + (3.0 * gelu_scale * gelu_cubic) * sq)
            part = mm(act, w2_ref[cols, :], 1, 0)
            branch = part if branch is None else branch + part
        branch = branch + b2_ref[...]
        masked = jnp.concatenate(
            [
                jnp.concatenate(
                    [
                        p_ref[h, pl.ds((tx * 8 + x + 3) * PITCH + LEFT + q, 8, stride=4), :]
                        for x in range(8)
                        for q in range(4)
                    ],
                    axis=0,
                )
                for h in range(2)
            ],
            axis=1,
        )
        summed = (masked + ls_ref[...] * branch).astype(BF16).astype(F32)
        shifted = summed - row_mean(summed)
        inv = lax.rsqrt(row_mean(shifted * shifted) + norm_eps)
        normed = shifted * inv
        down_in = (normed * dg_ref[...] + db_ref[...]).astype(BF16)
        ps_ref[tx] = mm(patch_sel, down_in, 1, 0)
        gp = gp_ref[tx]
        blocks = [gp[:, q * 256 : q * 256 + 256] for q in range(4)]
        scaled = [b * dg_ref[...] for b in blocks]
        centred = spread([s - row_mean(s) for s in scaled])
        second = row_mean(spread(scaled) * normed)
        grad_summed = inv * (centred - normed * second)
        for h in range(2):
            gs_ref[h, rows, :] = grad_summed[:, h * 128 : h * 128 + 128]
        add_entry(54, fold8(spread(blocks) * normed))
        add_entry(53, fold8(grad_summed * branch))
        scaled_grad = ls_ref[...] * grad_summed
        add_entry(52, fold8(scaled_grad))
        grad_b = scaled_grad.astype(BF16)
        gb_ref[rows, :] = grad_b
        gbt_ref[:, rows] = grad_b.T
        nit_ref[:, rows] = normed_in.T
        return c

    for tx in range(4):
        forward(tx, 0)

    def batch(b):
        core_dev = {"sx": sx + 1 - 2 * core}

        def y_dev(k, m):
            x_core = lax.rem(sx, 4) if m == 0 else lax.rem(sx + 2, 4)
            return {"sx": lax.rem(yy + k, 4) * 4 + x_core}

        def z_dev(k, m):
            return {"sy": at_sy(k)} if m == 0 else {"sy": at_sy(k), "sx": sx + 2 - 4 * xl}

        rings = ((yy, y_dev), (sy, z_dev))
        others = [(k, m) for m in range(2) for k in range(4) if (k, m) != (0, 0)]

        def rc(src, dst, k, dev):
            return pltpu.make_async_remote_copy(
                src_ref=src, dst_ref=dst, send_sem=bs_sem.at[b, k], recv_sem=br_sem.at[b, k], device_id=dev,
                device_id_type=MESH,
            )

        def ds(i, n):
            return pl.ds(pl.multiple_of(i, n), n)

        fin = fin_ref.at[b]
        loc = loc_ref.at[b]
        s0, r0, r1 = s0_ref.at[b], r0_ref.at[b], r1_ref.at[b]
        s1, s2, r2 = s1_ref.at[b], s2_ref.at[b], r2_ref.at[b]

        def ring_at(half, k=0):
            return half * 512 + lax.rem(rings[half][0] + k, 4) * 128

        def plane_at(half, k=0, m=0):
            return lax.rem(rings[1 - half][0] + k, 4) * 32 + (xl if m == 0 else 1 - xl) * 16

        def core_in(q):
            return rc(s0.at[ds(q * 256, 256)], r0.at[ds(q * 256, 256)], q, core_dev)

        def ring_in(half, k):
            return rc(s1.at[ds(ring_at(half, k), 128)], r1.at[half, k - 1], 4 + half * 3 + k - 1, rings[half][1](k, 0))

        def plane_in(half, i):
            k, m = others[i]
            return rc(
                s2.at[half, ds(plane_at(half, k, m), 16)], r2.at[half, i], 10 + half * 7 + i, rings[1 - half][1](k, m)
            )

        def plane_out(half, i):
            k, m = others[i]
            at = ds(core * 1024 + ring_at(half) + plane_at(half), 16)
            return rc(fin.at[at], fin.at[at], 24 + half * 7 + i, rings[1 - half][1](k, m))

        def ring_out(half, k):
            at = ds(core * 1024 + ring_at(half), 128)
            return rc(fin.at[at], fin.at[at], 38 + half * 3 + k - 1, rings[half][1](k, 0))

        def core_out(half, k):
            at = ds(core * 1024 + ring_at(half, (4 - k) % 4), 128)
            return rc(fin.at[at], fin.at[at], 44 + half * 4 + k, core_dev)

        def step0(part=None):
            for q in range(4) if part is None else part:
                s0[ds(q * 256, 256), :] = loc[ds((1 - core) * 1024 + q * 256, 256), :].astype(BF16)
                core_in(q).start()

        def step1():
            for half in range(2):
                for q in (2 * half, 2 * half + 1):
                    core_in(q).wait()
                    at = ds(core * 1024 + q * 256, 256)
                    total = loc[at, :] + r0[ds(q * 256, 256), :].astype(F32)
                    loc[at, :] = total
                    s1[ds(q * 256, 256), :] = total.astype(BF16)
                for k in (2, 1, 3):
                    ring_in(half, k).start()

        def step2():
            for half in range(2):
                total = loc[ds(core * 1024 + ring_at(half), 128), :]
                for k in range(1, 4):
                    ring_in(half, k).wait()
                    total = total + r1[half, k - 1].astype(F32)
                loc[ds(core * 1024 + ring_at(half), 128), :] = total
                s2[half] = total.astype(BF16)
                for i in range(7):
                    plane_in(half, i).start()

        def step3():
            for half in range(2):
                at = ds(core * 1024 + ring_at(half) + plane_at(half), 16)
                total = loc[at, :]
                for i in range(7):
                    plane_in(half, i).wait()
                    total = total + r2[half, i].astype(F32)
                fin[at, :] = total.astype(BF16)
                for i in range(7):
                    plane_out(half, i).start()

        def step4():
            for half in range(2):
                for i in range(7):
                    plane_out(half, i).wait()
                for k in (2, 1, 3):
                    ring_out(half, k).start()
                core_out(half, 0).start()

        def step5():
            for half in range(2):
                for k in (1, 3, 2):
                    ring_out(half, k).wait()
                    core_out(half, k).start()

        def out_copies():
            if b == 0:
                return [
                    pltpu.make_async_copy(
                        fin.at[pl.ds(q * 1024, 1024)], down_ref.at[:, q * 256 : q * 256 + 256], out_sem.at[b, q]
                    )
                    for q in range(2)
                ]
            return [
                pltpu.make_async_copy(
                    fin.at[pl.ds(q * 256, 256)], expand_ref.at[:, q * 256 : q * 256 + 256], out_sem.at[b, q]
                )
                for q in range(4)
            ] + [pltpu.make_async_copy(fin.at[pl.ds(1024, 1024)], project_ref, out_sem.at[b, 4])]

        def step6():
            for half in range(2):
                for k in range(4):
                    core_out(half, k).wait()
            for copy in out_copies():
                copy.start()

        def step7():
            for copy in out_copies():
                copy.wait()

        return [step0, step1, step2, step3, step4, step5, step6, step7]

    first = batch(0)
    second = batch(1)

    gr = gr_ref[...]
    gr2 = jnp.concatenate([gr, gr], axis=0)
    pool = None
    for q in range(4):
        sums = ps_ref[:, q * 8 : q * 8 + 8, :].reshape(32, 256)
        high = sums.astype(BF16)
        low = (sums - high.astype(F32)).astype(BF16)
        both = jnp.concatenate([high, low], axis=0)
        grad_down = mm(both, gr2, 0, 0)
        loc_ref[0, q * 256 : q * 256 + 256, :] = grad_down[:, :256]
        loc_ref[0, 1024 + q * 256 : 1024 + q * 256 + 256, :] = grad_down[:, 256:]
        part = mm(both, dw_ref[q * 256 : q * 256 + 256, :], 1, 0)
        part = part[:32] + part[32:]
        pool = part if pool is None else pool + part
    tissue = jnp.concatenate([mv_ref[...].reshape(32, 128)] * 4, axis=1)
    pooled_ref[...] = (pool * (1.0 / 16.0) + do_ref[...]) * tissue
    first[0]()

    def hidden_back(j):
        cols = slice(j * 256, j * 256 + 256)
        grad_hidden = mm(gb_ref[...], w2_ref[cols, :], 1, 1) * sl_ref[:, cols]
        add_entry(56 + j, fold8(grad_hidden))
        grad_hidden_b = grad_hidden.astype(BF16)
        gh_ref[:, cols] = grad_hidden_b
        loc_ref[1, j * 256 : j * 256 + 256, :] = mm(nit_ref[...], grad_hidden_b, 1, 0)
        loc_ref[1, 1024 + j * 256 : 1024 + j * 256 + 256, :] = mm(gbt_ref[...], act_ref[:, cols], 1, 0).T

    hidden_back(0)
    second[0]((0,))
    hidden_back(1)
    second[0]((1,))
    first[1]()
    hidden_back(2)
    second[0]((2,))
    hidden_back(3)
    second[0]((3,))

    def backward(tx, c):
        rows = pl.ds(tx * 256, 256)
        grad_normed = mm(gh_ref[rows, :], w1_ref[...], 1, 1)
        normed = nc_ref[rows, :]
        add_entry(50, fold8(grad_normed * normed))
        add_entry(51, fold8(grad_normed))
        scaled = grad_normed * ng_ref[...]
        inv = inv_ref[rows, :]
        inv = jnp.concatenate([inv, inv], axis=1)
        grad_conv = inv * (scaled - row_mean(scaled) - normed * row_mean(scaled * normed))
        add_entry(49, fold8(grad_conv))
        for h in range(2):
            half = grad_conv[:, h * 128 : h * 128 + 128]
            co_ref[h, rows, :] = half
            for x in range(8):
                for q in range(4):
                    at = (x * 4 + q) * 8
                    pg_ref[h, pl.ds((tx * 8 + x + 3) * PITCH + LEFT + q, 8, stride=4), :] = half[at : at + 8, :]

        return c

    backward(0, 0)
    second[1]()
    for tx in range(1, 4):
        backward(tx, 0)

    pack(1, pg_ref)
    for copy in halo_copies(1):
        copy.start()

    def taps(a0, n, hooks):
        def half_step(h, c):
            def rows_step(i, sums):
                x = i * 2
                sums = list(sums)
                grads = [[co_ref[h, block8((x + d) * 4 + q), :] for q in range(4)] for d in range(2)]
                for r in range(n + 1):
                    rows = plane_rows(p_ref, h, x + a0 + r, 10)
                    for d in range(2):
                        a = r - d
                        if a < 0 or a >= n:
                            continue
                        for b in range(7):
                            g = grads[d]
                            sums[a * 7 + b] = sums[a * 7 + b] + (
                                (rows[b] * g[0] + rows[b + 1] * g[1]) + (rows[b + 2] * g[2] + rows[b + 3] * g[3])
                            )
                return tuple(sums)

            sums = lax.fori_loop(0, WX // 2, rows_step, tuple(jnp.zeros((8, 128), F32) for _ in range(7 * n)))
            for t in range(7 * n):
                kg_ref[h, pl.ds((a0 * 7 + t) * 8, 8), :] = sums[t]
            for when, hook in hooks:

                @pl.when(h == when)
                def _(hook=hook):
                    hook()

            return c

        lax.fori_loop(0, 2, half_step, 0)

    taps(0, 4, ((0, first[2]),))
    taps(4, 3, ((0, second[2]),))

    for h in range(2):
        total = kg_ref[h, pl.ds(0, 64, stride=8), :]
        for s in range(1, 8):
            total = total + kg_ref[h, pl.ds(s, 64, stride=8), :]
        v_ref[h * 64 : h * 64 + 64, :] = total

    def small_rc(src, dst, k, dev):
        return pltpu.make_async_remote_copy(
            src_ref=src, dst_ref=dst, send_sem=vs_sem.at[k], recv_sem=vr_sem.at[k], device_id=dev,
            device_id_type=MESH,
        )

    def small_in(k):
        return small_rc(v_ref.at[block8(at_sx(k))], vr_ref.at[block8(sx)], k, {"sx": at_sx(k)})

    def small_z(k):
        return small_rc(vz_ref.at[sy], vz_ref.at[sy], 15 + k, {"sy": at_sy(k)})

    def small_out(k):
        return small_rc(vf_ref.at[block8(sx)], vf_ref.at[block8(sx)], 18 + k, {"sx": at_sx(k)})

    def each(make, act):
        def body(k, c):
            act(make(k))
            return c

        return body

    def small_step0():
        lax.fori_loop(1, N_SX, each(small_in, lambda copy: copy.start()), 0)
        vr_ref[block8(sx), :] = v_ref[block8(sx), :]

    def small_step1():
        lax.fori_loop(1, N_SX, each(small_in, lambda copy: copy.wait()), 0)
        vz_ref[sy] = jnp.sum(vr_ref[...].reshape(16, 8, 128), axis=0)
        for k in range(1, N_SY):
            small_z(k).start()

    def small_step2():
        for k in range(1, N_SY):
            small_z(k).wait()
        vf_ref[block8(sx), :] = (vz_ref[0] + vz_ref[1]) + (vz_ref[2] + vz_ref[3])
        lax.fori_loop(1, N_SX, each(small_out, lambda copy: copy.start()), 0)

    def small_step3():
        lax.fori_loop(1, N_SX, each(small_out, lambda copy: copy.wait()), 0)
        small_ref[...] = vf_ref[...]

    small_step0()

    for copy in halo_copies(1):
        copy.wait()
    unpack_sides(1, pg_ref)
    unpack_ends(1, pg_ref)

    def back_step(i, c):
        x = i * 2
        keep = mv_ref[x // 8]
        for h in range(2):
            sums = depthwise(pg_ref, h, x, True)
            for k in range(2):
                for q in range(4):
                    value = (sums[k][q] + gs_ref[h, block8((x + k) * 4 + q), :]) * keep
                    nat_ref[h, x + k, pl.ds(q, 8, stride=4), :] = value
        for k in range(2):
            gf_ref[x + k] = jnp.concatenate([nat_ref[0, x + k], nat_ref[1, x + k]], axis=1).astype(BF16)

        return c

    def back_part(g, c):
        lax.fori_loop(g * 4, g * 4 + 4, back_step, 0)
        for when, hook in ((0, first[3]), (2, second[3]),):

            @pl.when(g == when)
            def _(hook=hook):
                hook()

        return c

    lax.fori_loop(0, 4, back_part, 0)
    small_step1()
    first[4]()
    second[4]()
    small_step2()
    first[5]()
    second[5]()
    small_step3()
    first[6]()
    second[6]()
    first[7]()
    second[7]()


def finish_kernel(
    pooled_in, gf_in, small_in, expand_in, project_in, down_in,
    pooled_out, gf_out, cw_out, expand_out, project_out, down_out, vec_out, eb_out, do_out,
    big_ref, pooled_ref, cw_ref, vec_ref, eb_ref, do_ref, sem,
):
    stores = []

    def store(src, dst):
        stores.append(pltpu.make_async_copy(src, dst, sem.at[len(stores)]))
        stores[-1].start()

    store(gf_in, gf_out)
    pieces = []
    for src, dst in ((down_in, down_out), (project_in, project_out), (expand_in, expand_out)):
        rows, lanes = src.shape
        step = 131072 // lanes
        for i in range(0, rows, step):
            pieces.append((src, dst, i, step, lanes))

    at = 0
    for mid, dst, i, step, lanes in pieces:
        view = big_ref.at[pl.ds(at, step), pl.ds(0, lanes)]
        view[...] = mid[i : i + step, :].astype(F32)
        store(view, dst.at[pl.ds(i, step)])
        at += step
    for tx in range(4):
        for ty in range(4):
            pooled_ref[tx, ty : ty + 1, :] = pooled_in[tx * 8 + ty * 2 : tx * 8 + ty * 2 + 1, :].astype(BF16)
    store(pooled_ref, pooled_out)
    for h in range(2):
        cols = slice(h * 128, h * 128 + 128)
        for a in range(7):
            cw_ref[a, :, cols] = small_in[h * 64 + a * 7 : h * 64 + a * 7 + 7, :]
        vec_ref[:, cols] = small_in[h * 64 + 49 : h * 64 + 56, :]
        for q in range(4):
            eb_ref[:, q * 256 + h * 128 : q * 256 + h * 128 + 128] = small_in[h * 64 + 56 + q : h * 64 + 57 + q, :]
        for q in range(2):
            do_ref[:, q * 256 + h * 128 : q * 256 + h * 128 + 128] = small_in[h * 64 + 60 + q : h * 64 + 61 + q, :]
    for src, dst in ((cw_ref, cw_out), (vec_ref, vec_out), (eb_ref, eb_out), (do_ref, do_out)):
        store(src, dst)
    for copy in stores:
        copy.wait()


def finish(pooled, grad_features, small, expand, project, down):
    hbm = pl.BlockSpec(memory_space=pl.ANY)
    out = pl.pallas_call(
        finish_kernel,
        out_shape=(
            jax.ShapeDtypeStruct((4, 4, 512), BF16),
            jax.ShapeDtypeStruct((WX, WY, 256), BF16),
            jax.ShapeDtypeStruct((7, 7, 256), F32),
            jax.ShapeDtypeStruct((256, 1024), F32),
            jax.ShapeDtypeStruct((1024, 256), F32),
            jax.ShapeDtypeStruct((1024, 512), F32),
            jax.ShapeDtypeStruct((7, 256), F32),
            jax.ShapeDtypeStruct((1, 1024), F32),
            jax.ShapeDtypeStruct((1, 512), F32),
        ),
        in_specs=[pl.BlockSpec(memory_space=pltpu.VMEM)] * 6,
        out_specs=(hbm,) * 9,
        scratch_shapes=[
            pltpu.VMEM((2304, 1024), F32),
            pltpu.VMEM((4, 4, 512), BF16), pltpu.VMEM((7, 7, 256), F32), pltpu.VMEM((7, 256), F32),
            pltpu.VMEM((1, 1024), F32), pltpu.VMEM((1, 512), F32),
            pltpu.SemaphoreType.DMA((14,)),
        ],
        compiler_params=pltpu.CompilerParams(vmem_limit_bytes=24 * 1024 * 1024),
        cost_estimate=pl.CostEstimate(flops=1_000_000, bytes_accessed=7_000_000, transcendentals=0),
    )(pooled, grad_features, small, expand, project, down)
    return out[:7] + (out[7].reshape(1024), out[8].reshape(512))


def on_device(
    features,
    return_slot,
    returned_grads,
    conv_weight,
    conv_bias,
    norm_gain,
    norm_bias,
    expand_weight,
    expand_bias,
    project_weight,
    project_bias,
    layer_scale,
    down_gain,
    down_bias,
    down_weight,
    down_offset,
):
    hbm = pl.BlockSpec(memory_space=pl.ANY)

    def row(v):
        return v.reshape(1, -1)

    def vm(*shape, dtype=F32):
        return pltpu.VMEM(shape, dtype)

    dma = pltpu.SemaphoreType.DMA
    parts = pl.pallas_call(
        kernel,
        out_shape=(
            pltpu.VMEM((32, 512), F32),
            pltpu.VMEM((WX, WY, 256), BF16),
            pltpu.VMEM((128, 128), F32),
            pltpu.VMEM((256, 1024), BF16),
            pltpu.VMEM((1024, 256), BF16),
            pltpu.VMEM((1024, 512), BF16),
        ),
        in_specs=[pl.BlockSpec(memory_space=pltpu.HBM)] * 16,
        out_specs=(pl.BlockSpec(memory_space=pltpu.VMEM),) * 6,
        scratch_shapes=[
            pltpu.SMEM((4, 4), jnp.int32), vm(WX, WY, 256, dtype=BF16), vm(32, 512, dtype=BF16), vm(7, 7, 256),
            vm(1, 256), vm(1, 256), vm(1, 256), vm(256, 1024, dtype=BF16), vm(1, 1024), vm(1024, 256, dtype=BF16),
            vm(1, 256), vm(1, 256), vm(1, 256), vm(1, 256), vm(1024, 512, dtype=BF16), vm(1, 512),
            dma((16,)),
            vm(2, PLANE, 128), vm(2, PLANE, 128), vm(2, 2, 2, 3, 32, 128, dtype=BF16),
            vm(2, 2, 2, 3, 32, 128, dtype=BF16), vm(2, 2, 2, 3, 32, 128, dtype=BF16),
            vm(2, 2, 2, 3, 32, 128, dtype=BF16), vm(2, 4, 2, 3, 16, 128, dtype=BF16),
            vm(2, 49, 8, 128), vm(4, 32, 128), vm(4, 8, 128),
            vm(4, 32, 128), vm(128, 128), vm(128, 128), vm(4, 32, 128), vm(32, 512, dtype=BF16), vm(4, 8, 1024),
            vm(4, 32, 256),
            vm(2, 1024, 128), vm(1024, 256), vm(1024, 128), vm(256, 1024, dtype=BF16), vm(256, 1024, dtype=BF16),
            vm(1024, 1024, dtype=BF16), vm(1024, 1024, dtype=BF16),
            vm(1024, 1024), vm(2, 1024, 128), vm(1024, 256, dtype=BF16), vm(2, 32, 32, 128),
            vm(2, 512, 128), vm(128, 128), vm(128, 128), vm(4, 8, 128), vm(128, 128),
            vm(2, 2048, 256), vm(2, 1024, 256, dtype=BF16), vm(2, 1024, 256, dtype=BF16),
            vm(2, 1024, 256, dtype=BF16), vm(2, 2, 3, 128, 256, dtype=BF16),
            vm(2, 2, 128, 256, dtype=BF16), vm(2, 2, 7, 16, 256, dtype=BF16), vm(2, 2048, 256, dtype=BF16),
            dma((2, 8)), dma((2, 8)), dma((16,)), dma((16,)), dma((2, 52)), dma((2, 52)), dma((34,)), dma((34,)),
            dma((2, 5)),
        ],
        compiler_params=pltpu.CompilerParams(
            collective_id=0, has_side_effects=True, vmem_limit_bytes=48 * 1024 * 1024
        ),
        cost_estimate=pl.CostEstimate(flops=4_000_000_000, bytes_accessed=8_000_000, transcendentals=1_000_000),
    )(
        *(pltpu.with_memory_space_constraint(v, pltpu.HBM) for v in (
        return_slot, features, returned_grads[0], conv_weight, row(conv_bias), row(norm_gain), row(norm_bias),
        expand_weight, row(expand_bias), project_weight, row(project_bias), row(layer_scale), row(down_gain),
        row(down_bias), down_weight, row(down_offset),
        ))
    )
    return finish(*parts)


def solution(mesh):
    placed = (
        P(("slide", "sx"), "sy", None),
        P(("slide", "sx"), "sy"),
        P("sy", ("slide", "sx"), None),
    ) + (P(),) * 13
    return jax.shard_map(
        on_device,
        mesh=mesh,
        in_specs=placed,
        out_specs=(
            P(("slide", "sx"), "sy", None),
            P(("slide", "sx"), "sy", None),
            P("slide", None, None),
            P("slide", None),
            P("slide", None),
            P("slide", None),
            P("slide", None),
            P("slide"),
            P("slide"),
        ),
        check_vma=False,
    )
```

```python
import functools

import jax
import jax.numpy as jnp
from jax import lax
from jax.experimental import pallas as pl
from jax.experimental.pallas import tpu as pltpu
from jax.sharding import PartitionSpec as P

F32 = jnp.float32
BF16 = jnp.bfloat16
MESH = pl.DeviceIdType.MESH

norm_eps = 1e-06
gelu_scale = 0.7978845608028654
gelu_cubic = 0.044715

WX = 32
WY = 32
LEFT = 8
PITCH = 48
PLANE = 38 * PITCH
N_SX = 16
N_SY = 4


def mm(a, b, ca, cb):
    return lax.dot_general(a, b, (((ca,), (cb,)), ((), ())), preferred_element_type=F32)


def fold8(v):
    return jnp.sum(v.reshape(v.shape[0] // 8, 8, v.shape[1]), axis=0)


def row_mean(v):
    return jnp.sum(v, axis=-1, keepdims=True) * (1.0 / v.shape[-1])


def kernel(
    slot_hbm, feat_hbm, ret_hbm, cw_hbm, cb_hbm, ng_hbm, nb_hbm, w1_hbm, b1_hbm, w2_hbm, b2_hbm, ls_hbm, dg_hbm,
    db_hbm, dw_hbm, do_hbm,
    pooled_ref, gf_ref, small_ref, fin_ref,
    slot_ref, feat_ref, ret_ref, cw_ref, cb_ref, ng_ref, nb_ref, w1_ref, b1_ref, w2_ref, b2_ref, ls_ref, dg_ref,
    db_ref, dw_ref, do_ref, in_sem,
    p_ref, pg_ref, xp_ref, xr_ref, yp_ref, yr_ref, cr_ref, wb_ref, mn_ref, mv_ref,
    rg_ref, pk_ref, rv_ref, ar_ref, gr_ref, gp_ref, ps_ref,
    co_ref, nc_ref, inv_ref, nit_ref, gbt_ref, gh_ref, act_ref, sl_ref, gs_ref, gb_ref, nat_ref,
    kg_ref, v_ref, vr_ref, vz_ref, vf_ref,
    loc_ref, s0_ref, r0_ref, s1_ref, r1_ref, s2_ref, r2_ref,
    hs_sem, hr_sem, as_sem, ar_sem, bs_sem, br_sem, vs_sem, vr_sem,
):
    pairs = (
        (slot_hbm, slot_ref), (feat_hbm, feat_ref), (ret_hbm, ret_ref), (cw_hbm, cw_ref), (cb_hbm, cb_ref),
        (dw_hbm, dw_ref), (w1_hbm, w1_ref), (w2_hbm, w2_ref), (ng_hbm, ng_ref), (nb_hbm, nb_ref), (b1_hbm, b1_ref),
        (b2_hbm, b2_ref), (ls_hbm, ls_ref), (dg_hbm, dg_ref), (db_hbm, db_ref), (do_hbm, do_ref),
    )
    loads = [pltpu.make_async_copy(src, dst, in_sem.at[k]) for k, (src, dst) in enumerate(pairs)]
    for load in loads:
        load.start()

    sx = lax.axis_index("sx")
    sy = lax.axis_index("sy")
    core = lax.rem(sx, 2)
    xl = lax.rem(sx // 2, 2)
    yy = sx // 4

    def at_sx(k):
        return lax.rem(sx + k + N_SX, N_SX)

    def at_sy(k):
        return lax.rem(sy + k + N_SY, N_SY)

    barrier = pltpu.get_barrier_semaphore()

    def greet(k, c):
        pl.semaphore_signal(barrier, inc=1, device_id={"sx": at_sx(k)}, device_id_type=MESH)
        return c

    lax.fori_loop(1, N_SX, greet, 0)
    for k in range(1, N_SY):
        pl.semaphore_signal(barrier, inc=1, device_id={"sy": at_sy(k)}, device_id_type=MESH)
    for k in range(1, N_SY):
        pl.semaphore_signal(
            barrier, inc=1, device_id={"sx": sx + 2 - 4 * xl, "sy": at_sy(k)}, device_id_type=MESH
        )
    for i in (-1, 1):
        for j in (-1, 1):
            pl.semaphore_signal(barrier, inc=1, device_id={"sx": at_sx(i), "sy": at_sy(j)}, device_id_type=MESH)

    loads[0].wait()
    sub = lax.broadcasted_iota(jnp.int32, (8, 128), 0)
    lane = lax.broadcasted_iota(jnp.int32, (8, 128), 1)
    sel = []
    for tx in range(4):
        picked = jnp.zeros((8, 128), jnp.int32)
        for ty in range(4):
            s = slot_ref[tx, ty]
            picked = jnp.where(sub // 2 == ty, s, picked)
            mn_ref[tx, ty * 8 : ty * 8 + 8, :] = jnp.where(jnp.full((8, 128), s) >= 0, 1.0, 0.0).astype(F32)
        mv_ref[tx] = jnp.where(picked >= 0, 1.0, 0.0).astype(F32)
        sel.append(jnp.where(picked == lane, 1.0, 0.0).astype(F32))
    selector = jnp.concatenate(sel, axis=0).astype(BF16)[:, :32]

    loads[1].wait()
    def fill(x, c):
        f = feat_ref[x].astype(F32)
        m = mn_ref[x // 8]
        at = pl.multiple_of((x + 3) * PITCH + LEFT, 8)
        for h in range(2):
            p_ref[h, pl.ds(at, WY), :] = f[:, h * 128 : h * 128 + 128] * m
            p_ref[h, pl.ds(at - 8, 8), :] = jnp.zeros((8, 128), F32)
            p_ref[h, pl.ds(at + WY, 8), :] = jnp.zeros((8, 128), F32)
        return c

    lax.fori_loop(0, WX, fill, 0)
    for row in (0, 35):
        p_ref[:, row * PITCH : (row + 3) * PITCH, :] = jnp.zeros((2, 3 * PITCH, 128), F32)

    def pack(e, ref):
        for side, row in ((0, 3), (1, 32)):
            for h in range(2):
                for a in range(3):
                    xp_ref[e, side, h, a] = ref[
                        h, pl.ds((row + a) * PITCH + LEFT, WY), :
                    ].astype(BF16)
        for side, col in ((0, 0), (1, WY - 3)):
            for h in range(2):
                for c in range(3):
                    yp_ref[e, side, h, c] = ref[h, pl.ds(3 * PITCH + LEFT + col + c, WX, stride=PITCH), :].astype(BF16)

    def halo_copies(e):
        def rc(src, dst, k, dev):
            return pltpu.make_async_remote_copy(
                src_ref=src, dst_ref=dst, send_sem=hs_sem.at[e, k], recv_sem=hr_sem.at[e, k], device_id=dev,
                device_id_type=MESH,
            )

        out = []
        for side, step in ((0, -1), (1, 1)):
            out.append(rc(yp_ref.at[e, side], yr_ref.at[e, side], 2 + side, {"sy": at_sy(step)}))
            out.append(rc(xp_ref.at[e, side], xr_ref.at[e, side], side, {"sx": at_sx(step)}))
            out.append(
                rc(yp_ref.at[e, side, :, :, 16:32, :], cr_ref.at[e, 2 * side], 4 + 2 * side,
                   {"sx": at_sx(1), "sy": at_sy(step)})
            )
            out.append(
                rc(yp_ref.at[e, side, :, :, 0:16, :], cr_ref.at[e, 2 * side + 1], 5 + 2 * side,
                   {"sx": at_sx(-1), "sy": at_sy(step)})
            )
        return out

    has_top = sx > 0
    has_bottom = sx < N_SX - 1
    keep_below = jnp.where(has_bottom, 1.0, 0.0).astype(F32)
    keep_above = jnp.where(has_top, 1.0, 0.0).astype(F32)
    keep_right = jnp.where(sy < N_SY - 1, 1.0, 0.0).astype(F32)
    keep_left = jnp.where(sy > 0, 1.0, 0.0).astype(F32)

    def unpack_sides(e, ref):
        for side, col, keep in ((0, LEFT + WY, keep_right), (1, LEFT - 3, keep_left)):
            for h in range(2):
                for c in range(3):
                    ref[h, pl.ds(3 * PITCH + col + c, WX, stride=PITCH), :] = (
                        yr_ref[e, side, h, c].astype(F32) * keep
                    )

    def unpack_ends(e, ref):
        for side, row, keep in ((0, 35, keep_below), (1, 0, keep_above)):
            for h in range(2):
                for a in range(3):
                    ref[h, pl.ds((row + a) * PITCH + LEFT, WY), :] = xr_ref[e, side, h, a].astype(F32) * keep
        for side, col, keep in ((0, LEFT + WY, keep_right), (1, LEFT - 3, keep_left)):
            for h in range(2):
                for c in range(3):
                    top = cr_ref[e, 2 * side, h, c].astype(F32) * (keep * keep_above)
                    ref[h, pl.ds(col + c, 3, stride=PITCH), :] = top[13:16, :]
                    bottom = cr_ref[e, 2 * side + 1, h, c].astype(F32) * (keep * keep_below)
                    ref[h, pl.ds(35 * PITCH + col + c, 3, stride=PITCH), :] = bottom[0:3, :]

    pack(0, p_ref)

    loads[2].wait()
    for q in range(4):
        rg_ref[q] = ret_ref[:, q * 128 : q * 128 + 128].astype(F32)
    for q in range(4):
        for s in range(2):
            pk_ref[pl.ds(2 * q + s, 16, stride=8), :] = rg_ref[q, pl.ds(s, 16, stride=2), :]

    pl.semaphore_wait(barrier, (N_SX - 1) + 2 * (N_SY - 1) + 4)

    for copy in halo_copies(0):
        copy.start()

    def block8(i):
        return pl.ds(pl.multiple_of(i * 8, 8), 8)

    def return_copy(k):
        return pltpu.make_async_remote_copy(
            src_ref=pk_ref.at[block8(at_sx(k))], dst_ref=rv_ref.at[block8(sx)], send_sem=as_sem.at[k],
            recv_sem=ar_sem.at[k], device_id={"sx": at_sx(k)}, device_id_type=MESH,
        )

    def start_return(k, c):
        return_copy(k).start()
        return c

    lax.fori_loop(1, N_SX, start_return, 0)
    rv_ref[block8(sx), :] = pk_ref[block8(sx), :]

    loads[3].wait()
    for h in range(2):
        for a in range(7):
            for b in range(7):
                wb_ref[h, a * 7 + b] = jnp.broadcast_to(cw_ref[a, b : b + 1, h * 128 : h * 128 + 128], (8, 128))

    kg_ref[...] = jnp.zeros_like(kg_ref)

    def add_entry(t, value):
        for h in range(2):
            kg_ref[h, t * 8 : t * 8 + 8, :] += value[:, h * 128 : h * 128 + 128]

    def plane_rows(ref, h, x, n):
        return [ref[h, pl.ds(x * PITCH + (LEFT - 3) + c, 8, stride=4), :] for c in range(n)]

    def depthwise(ref, h, x, flipped):
        sums = [[None] * 4 for _ in range(2)]
        for r in range(8):
            rows = plane_rows(ref, h, x + r, 10)
            for i in range(2):
                a = r - i
                if a < 0 or a > 6:
                    continue
                for b in range(7):
                    t = a * 7 + b
                    w = wb_ref[h, 48 - t if flipped else t]
                    for c in range(4):
                        term = rows[c + b] * w
                        sums[i][c] = term if sums[i][c] is None else sums[i][c] + term
        return sums

    loads[4].wait()

    def conv_step(i, c):
        x = i * 2
        for h in range(2):
            bias = cb_ref[:, h * 128 : h * 128 + 128]
            sums = depthwise(p_ref, h, x, False)
            for k in range(2):
                for q in range(4):
                    co_ref[h, block8((x + k) * 4 + q), :] = sums[k][q] + bias
        return c

    lax.fori_loop(0, WX // 2, conv_step, 0)

    loads[5].wait()

    def wait_return(k, c):
        return_copy(k).wait()
        return c

    lax.fori_loop(1, N_SX, wait_return, 0)
    for q in range(4):
        for s in range(2):
            ar_ref[q, pl.ds(s, 16, stride=2), :] = rv_ref[pl.ds(2 * q + s, 16, stride=8), :]
    arrived = jnp.concatenate([ar_ref[q] for q in range(4)], axis=1).astype(BF16)
    grad_pool = mm(selector, arrived, 1, 0)
    grad_reduced = (grad_pool * (1.0 / 16.0)).astype(BF16)
    gr_ref[...] = grad_reduced
    grad_patch = mm(grad_reduced, dw_ref[...], 1, 1)
    for tx in range(4):
        gp_ref[tx] = grad_patch[tx * 8 : tx * 8 + 8, :]

    off_sum = jnp.sum(grad_pool.reshape(4, 8, 512), axis=0) * 0.5
    for q in range(2):
        add_entry(60 + q, off_sum[:, q * 256 : q * 256 + 256])
    bias_sum = jnp.sum(gp_ref[...], axis=0)
    bias_sum = (
        bias_sum[:, 0:256] + bias_sum[:, 256:512] + bias_sum[:, 512:768] + bias_sum[:, 768:1024]
    ) * 8.0
    add_entry(55, bias_sum)

    for copy in halo_copies(0):
        copy.wait()
    unpack_sides(0, p_ref)

    def side_step(g, c):
        for h in range(2):
            for first_col, taps_of, out_y in (
                (LEFT - 3, ((0, 0, 0), (0, 1, 1), (0, 2, 2), (1, 0, 1), (1, 1, 2), (2, 0, 2)), 0),
                (LEFT + WY, ((0, 6, 0), (1, 5, 0), (1, 6, 1), (2, 4, 0), (2, 5, 1), (2, 6, 2)), 29),
            ):
                sums = [None] * 3
                for a in range(7):
                    cols = [p_ref[h, pl.ds((g * 8 + a) * PITCH + first_col + q, 8, stride=PITCH), :] for q in range(3)]
                    for y, b, q in taps_of:
                        term = cols[q] * wb_ref[h, a * 7 + b]
                        sums[y] = term if sums[y] is None else sums[y] + term
                for y in range(3):
                    row = (out_y + y) % 4 * 8 + (out_y + y) // 4
                    at = pl.ds(g * 256 + row, 8, stride=32)
                    co_ref[h, at, :] = co_ref[h, at, :] + sums[y]
        return c

    lax.fori_loop(0, 4, side_step, 0)
    unpack_ends(0, p_ref)

    def end_step(h, c):
        for first_row, pairs_of in (
            (0, ((0, 0), (0, 1), (0, 2), (1, 0), (1, 1), (2, 0))),
            (29, ((0, 6), (1, 5), (1, 6), (2, 4), (2, 5), (2, 6))),
        ):
            sums = [[None] * 4 for _ in range(3)]
            for x, a in pairs_of:
                rows = plane_rows(p_ref, h, first_row + x + a, 10)
                for b in range(7):
                    w = wb_ref[h, a * 7 + b]
                    for q in range(4):
                        term = rows[q + b] * w
                        sums[x][q] = term if sums[x][q] is None else sums[x][q] + term
            for x in range(3):
                for q in range(4):
                    row = ((first_row + x) * 4 + q) * 8
                    co_ref[h, row : row + 8, :] = co_ref[h, row : row + 8, :] + sums[x][q]
        return c

    lax.fori_loop(0, 2, end_step, 0)

    for load in loads[6:]:
        load.wait()
    r32 = lax.broadcasted_iota(jnp.int32, (32, 256), 0)
    k32 = lax.broadcasted_iota(jnp.int32, (32, 256), 1)
    off_of = (k32 // 32 % 2) * 2 + (k32 // 8 % 4) % 2
    patch_sel = jnp.where(
        (off_of == r32 // 8) & (k32 % 8 // 2 == r32 % 8 // 2) & (r32 % 2 == 0), 1.0, 0.0
    ).astype(BF16)

    def spread(blocks):
        row = [blocks[0], blocks[1]] * 2 + [blocks[2], blocks[3]] * 2
        return jnp.concatenate(row * 4, axis=0)

    def forward(tx, c):
        rows = pl.ds(tx * 256, 256)
        v = jnp.concatenate([co_ref[0, rows, :], co_ref[1, rows, :]], axis=1)
        shifted = v - row_mean(v)
        inv = lax.rsqrt(row_mean(shifted * shifted) + norm_eps)
        normed = shifted * inv
        nc_ref[rows, :] = normed
        inv_ref[rows, :] = jnp.broadcast_to(inv, (256, 128))
        normed_in = (normed * ng_ref[...] + nb_ref[...]).astype(BF16)
        branch = None
        for j in range(4):
            cols = slice(j * 256, j * 256 + 256)
            hid = mm(normed_in, w1_ref[:, cols], 1, 0) + b1_ref[:, cols]
            sq = hid * hid
            t = jnp.tanh(hid * (gelu_scale + (gelu_scale * gelu_cubic) * sq))
            u = 0.5 + 0.5 * t
            act = (hid * u).astype(BF16)
            act_ref[rows, cols] = act
            sl_ref[rows, cols] = u + hid * (u - u * t) * (gelu_scale + (3.0 * gelu_scale * gelu_cubic) * sq)
            part = mm(act, w2_ref[cols, :], 1, 0)
            branch = part if branch is None else branch + part
        branch = branch + b2_ref[...]
        masked = jnp.concatenate(
            [
                jnp.concatenate(
                    [
                        p_ref[h, pl.ds((tx * 8 + x + 3) * PITCH + LEFT + q, 8, stride=4), :]
                        for x in range(8)
                        for q in range(4)
                    ],
                    axis=0,
                )
                for h in range(2)
            ],
            axis=1,
        )
        summed = (masked + ls_ref[...] * branch).astype(BF16).astype(F32)
        shifted = summed - row_mean(summed)
        inv = lax.rsqrt(row_mean(shifted * shifted) + norm_eps)
        normed = shifted * inv
        down_in = (normed * dg_ref[...] + db_ref[...]).astype(BF16)
        ps_ref[tx] = mm(patch_sel, down_in, 1, 0)
        gp = gp_ref[tx]
        blocks = [gp[:, q * 256 : q * 256 + 256] for q in range(4)]
        scaled = [b * dg_ref[...] for b in blocks]
        centred = spread([s - row_mean(s) for s in scaled])
        second = row_mean(spread(scaled) * normed)
        grad_summed = inv * (centred - normed * second)
        for h in range(2):
            gs_ref[h, rows, :] = grad_summed[:, h * 128 : h * 128 + 128]
        add_entry(54, fold8(spread(blocks) * normed))
        add_entry(53, fold8(grad_summed * branch))
        scaled_grad = ls_ref[...] * grad_summed
        add_entry(52, fold8(scaled_grad))
        grad_b = scaled_grad.astype(BF16)
        gb_ref[rows, :] = grad_b
        gbt_ref[:, rows] = grad_b.T
        nit_ref[:, rows] = normed_in.T
        return c

    for tx in range(4):
        forward(tx, 0)

    def batch(b):
        core_dev = {"sx": sx + 1 - 2 * core}

        def y_dev(k, m):
            x_core = lax.rem(sx, 4) if m == 0 else lax.rem(sx + 2, 4)
            return {"sx": lax.rem(yy + k, 4) * 4 + x_core}

        def z_dev(k, m):
            return {"sy": at_sy(k)} if m == 0 else {"sy": at_sy(k), "sx": sx + 2 - 4 * xl}

        rings = ((yy, y_dev), (sy, z_dev))
        others = [(k, m) for m in range(2) for k in range(4) if (k, m) != (0, 0)]

        def rc(src, dst, k, dev):
            return pltpu.make_async_remote_copy(
                src_ref=src, dst_ref=dst, send_sem=bs_sem.at[b, k], recv_sem=br_sem.at[b, k], device_id=dev,
                device_id_type=MESH,
            )

        def ds(i, n):
            return pl.ds(pl.multiple_of(i, n), n)

        fin = fin_ref.at[b]
        loc = loc_ref.at[b]
        s0, r0, r1 = s0_ref.at[b], r0_ref.at[b], r1_ref.at[b]
        s1, s2, r2 = s1_ref.at[b], s2_ref.at[b], r2_ref.at[b]

        def ring_at(half, k=0):
            return half * 512 + lax.rem(rings[half][0] + k, 4) * 128

        def plane_at(half, k=0, m=0):
            return lax.rem(rings[1 - half][0] + k, 4) * 32 + (xl if m == 0 else 1 - xl) * 16

        def core_in(q):
            return rc(s0.at[ds(q * 256, 256)], r0.at[ds(q * 256, 256)], q, core_dev)

        def ring_in(half, k):
            return rc(s1.at[ds(ring_at(half, k), 128)], r1.at[half, k - 1], 4 + half * 3 + k - 1, rings[half][1](k, 0))

        def plane_in(half, i):
            k, m = others[i]
            return rc(
                s2.at[half, ds(plane_at(half, k, m), 16)], r2.at[half, i], 10 + half * 7 + i, rings[1 - half][1](k, m)
            )

        def plane_out(half, i):
            k, m = others[i]
            at = ds(core * 1024 + ring_at(half) + plane_at(half), 16)
            return rc(fin.at[at], fin.at[at], 24 + half * 7 + i, rings[1 - half][1](k, m))

        def ring_out(half, k):
            at = ds(core * 1024 + ring_at(half), 128)
            return rc(fin.at[at], fin.at[at], 38 + half * 3 + k - 1, rings[half][1](k, 0))

        def core_out(half, k):
            at = ds(core * 1024 + ring_at(half, (4 - k) % 4), 128)
            return rc(fin.at[at], fin.at[at], 44 + half * 4 + k, core_dev)

        def step0(part=None):
            for q in range(4) if part is None else part:
                s0[ds(q * 256, 256), :] = loc[ds((1 - core) * 1024 + q * 256, 256), :].astype(BF16)
                core_in(q).start()

        def step1():
            for half in range(2):
                for q in (2 * half, 2 * half + 1):
                    core_in(q).wait()
                    at = ds(core * 1024 + q * 256, 256)
                    total = loc[at, :] + r0[ds(q * 256, 256), :].astype(F32)
                    loc[at, :] = total
                    s1[ds(q * 256, 256), :] = total.astype(BF16)
                for k in (2, 1, 3):
                    ring_in(half, k).start()

        def step2():
            for half in range(2):
                total = loc[ds(core * 1024 + ring_at(half), 128), :]
                for k in range(1, 4):
                    ring_in(half, k).wait()
                    total = total + r1[half, k - 1].astype(F32)
                loc[ds(core * 1024 + ring_at(half), 128), :] = total
                s2[half] = total.astype(BF16)
                for i in range(7):
                    plane_in(half, i).start()

        def step3():
            for half in range(2):
                at = ds(core * 1024 + ring_at(half) + plane_at(half), 16)
                total = loc[at, :]
                for i in range(7):
                    plane_in(half, i).wait()
                    total = total + r2[half, i].astype(F32)
                fin[at, :] = total.astype(BF16)
                for i in range(7):
                    plane_out(half, i).start()

        def step4():
            for half in range(2):
                for i in range(7):
                    plane_out(half, i).wait()
                for k in (2, 1, 3):
                    ring_out(half, k).start()
                core_out(half, 0).start()

        def step5():
            for half in range(2):
                for k in (1, 3, 2):
                    ring_out(half, k).wait()
                    core_out(half, k).start()

        def step6():
            for half in range(2):
                for k in range(4):
                    core_out(half, k).wait()

        return [step0, step1, step2, step3, step4, step5, step6]

    first = batch(0)
    second = batch(1)

    gr = gr_ref[...]
    gr2 = jnp.concatenate([gr, gr], axis=0)

    def two_terms(q):
        sums = ps_ref[:, q * 8 : q * 8 + 8, :].reshape(32, 256)
        high = sums.astype(BF16)
        low = (sums - high.astype(F32)).astype(BF16)
        return jnp.concatenate([high, low], axis=0)

    for q in range(4):
        grad_down = mm(two_terms(q), gr2, 0, 0)
        loc_ref[0, q * 256 : q * 256 + 256, :] = grad_down[:, :256]
        loc_ref[0, 1024 + q * 256 : 1024 + q * 256 + 256, :] = grad_down[:, 256:]
    first[0]()

    def hidden_back(j):
        cols = slice(j * 256, j * 256 + 256)
        grad_hidden = mm(gb_ref[...], w2_ref[cols, :], 1, 1) * sl_ref[:, cols]
        add_entry(56 + j, fold8(grad_hidden))
        grad_hidden_b = grad_hidden.astype(BF16)
        gh_ref[:, cols] = grad_hidden_b
        loc_ref[1, j * 256 : j * 256 + 256, :] = mm(nit_ref[...], grad_hidden_b, 1, 0)
        loc_ref[1, 1024 + j * 256 : 1024 + j * 256 + 256, :] = mm(gbt_ref[...], act_ref[:, cols], 1, 0).T

    hidden_back(0)
    second[0]((0,))
    hidden_back(1)
    second[0]((1,))
    first[1]()
    hidden_back(2)
    second[0]((2,))
    hidden_back(3)
    second[0]((3,))

    def backward(tx, c):
        rows = pl.ds(tx * 256, 256)
        grad_normed = mm(gh_ref[rows, :], w1_ref[...], 1, 1)
        normed = nc_ref[rows, :]
        add_entry(50, fold8(grad_normed * normed))
        add_entry(51, fold8(grad_normed))
        scaled = grad_normed * ng_ref[...]
        inv = inv_ref[rows, :]
        inv = jnp.concatenate([inv, inv], axis=1)
        grad_conv = inv * (scaled - row_mean(scaled) - normed * row_mean(scaled * normed))
        add_entry(49, fold8(grad_conv))
        for h in range(2):
            half = grad_conv[:, h * 128 : h * 128 + 128]
            co_ref[h, rows, :] = half
            for x in range(8):
                for q in range(4):
                    at = (x * 4 + q) * 8
                    pg_ref[h, pl.ds((tx * 8 + x + 3) * PITCH + LEFT + q, 8, stride=4), :] = half[at : at + 8, :]

        return c

    backward(0, 0)
    second[1]()
    for tx in range(1, 4):
        backward(tx, 0)

    pack(1, pg_ref)
    for copy in halo_copies(1):
        copy.start()

    def taps(a0, n, hooks):
        def half_step(h, c):
            def rows_step(i, sums):
                x = i * 2
                sums = list(sums)
                grads = [[co_ref[h, block8((x + d) * 4 + q), :] for q in range(4)] for d in range(2)]
                for r in range(n + 1):
                    rows = plane_rows(p_ref, h, x + a0 + r, 10)
                    for d in range(2):
                        a = r - d
                        if a < 0 or a >= n:
                            continue
                        for b in range(7):
                            g = grads[d]
                            sums[a * 7 + b] = sums[a * 7 + b] + (
                                (rows[b] * g[0] + rows[b + 1] * g[1]) + (rows[b + 2] * g[2] + rows[b + 3] * g[3])
                            )
                return tuple(sums)

            sums = lax.fori_loop(0, WX // 2, rows_step, tuple(jnp.zeros((8, 128), F32) for _ in range(7 * n)))
            for t in range(7 * n):
                kg_ref[h, pl.ds((a0 * 7 + t) * 8, 8), :] = sums[t]
            for when, hook in hooks:

                @pl.when(h == when)
                def _(hook=hook):
                    hook()

            return c

        lax.fori_loop(0, 2, half_step, 0)

    first[2]()
    taps(0, 4, ())
    taps(4, 3, ((0, second[2]),))

    for h in range(2):
        total = kg_ref[h, pl.ds(0, 64, stride=8), :]
        for s in range(1, 8):
            total = total + kg_ref[h, pl.ds(s, 64, stride=8), :]
        v_ref[h * 64 : h * 64 + 64, :] = total

    def small_rc(src, dst, k, dev):
        return pltpu.make_async_remote_copy(
            src_ref=src, dst_ref=dst, send_sem=vs_sem.at[k], recv_sem=vr_sem.at[k], device_id=dev,
            device_id_type=MESH,
        )

    def small_in(k):
        return small_rc(v_ref.at[block8(at_sx(k))], vr_ref.at[block8(sx)], k, {"sx": at_sx(k)})

    def small_z(k):
        return small_rc(vz_ref.at[sy], vz_ref.at[sy], 15 + k, {"sy": at_sy(k)})

    def small_out(k):
        return small_rc(vf_ref.at[block8(sx)], vf_ref.at[block8(sx)], 18 + k, {"sx": at_sx(k)})

    def each(make, act):
        def body(k, c):
            act(make(k))
            return c

        return body

    def small_step0():
        lax.fori_loop(1, N_SX, each(small_in, lambda copy: copy.start()), 0)
        vr_ref[block8(sx), :] = v_ref[block8(sx), :]

    def small_step1():
        lax.fori_loop(1, N_SX, each(small_in, lambda copy: copy.wait()), 0)
        vz_ref[sy] = jnp.sum(vr_ref[...].reshape(16, 8, 128), axis=0)
        for k in range(1, N_SY):
            small_z(k).start()

    def small_step2():
        for k in range(1, N_SY):
            small_z(k).wait()
        vf_ref[block8(sx), :] = (vz_ref[0] + vz_ref[1]) + (vz_ref[2] + vz_ref[3])
        lax.fori_loop(1, N_SX, each(small_out, lambda copy: copy.start()), 0)

    def small_step3():
        lax.fori_loop(1, N_SX, each(small_out, lambda copy: copy.wait()), 0)
        small_ref[...] = vf_ref[...]

    small_step0()

    for copy in halo_copies(1):
        copy.wait()
    unpack_sides(1, pg_ref)
    unpack_ends(1, pg_ref)

    def back_step(i, c):
        x = i * 2
        keep = mv_ref[x // 8]
        for h in range(2):
            sums = depthwise(pg_ref, h, x, True)
            for k in range(2):
                for q in range(4):
                    value = (sums[k][q] + gs_ref[h, block8((x + k) * 4 + q), :]) * keep
                    nat_ref[h, x + k, pl.ds(q, 8, stride=4), :] = value
        for k in range(2):
            gf_ref[x + k] = jnp.concatenate([nat_ref[0, x + k], nat_ref[1, x + k]], axis=1).astype(BF16)

        return c

    def back_part(g, c):
        lax.fori_loop(g * 4, g * 4 + 4, back_step, 0)
        for when, hook in ((0, first[3]), (2, second[3]),):

            @pl.when(g == when)
            def _(hook=hook):
                hook()

        return c

    lax.fori_loop(0, 4, back_part, 0)
    small_step1()
    first[4]()
    second[4]()
    small_step2()
    first[5]()
    pool = None
    for q in range(4):
        part = mm(two_terms(q), dw_ref[q * 256 : q * 256 + 256, :], 1, 0)
        part = part[:32] + part[32:]
        pool = part if pool is None else pool + part
    tissue = jnp.concatenate([mv_ref[...].reshape(32, 128)] * 4, axis=1)
    pooled_ref[...] = (pool * (1.0 / 16.0) + do_ref[...]) * tissue
    second[5]()
    small_step3()
    first[6]()
    second[6]()


def finish_kernel(
    pooled_in, gf_in, small_in, sums_in,
    pooled_out, gf_out, cw_out, expand_out, project_out, down_out, vec_out, eb_out, do_out,
    big_ref, pooled_ref, cw_ref, vec_ref, eb_ref, do_ref, sem,
):
    stores = []

    def store(src, dst):
        stores.append(pltpu.make_async_copy(src, dst, sem.at[len(stores)]))
        stores[-1].start()

    store(gf_in, gf_out)
    at = 0
    for dst, part, start, blocks in ((down_out, 0, 0, 2), (project_out, 1, 1024, 1), (expand_out, 1, 0, 4)):
        rows, lanes = dst.shape
        step = 131072 // lanes
        for i in range(0, rows, step):
            for q in range(blocks):
                first = start + q * rows + i
                big_ref[at : at + step, q * 256 : q * 256 + 256] = sums_in[part, first : first + step, :].astype(F32)
            store(big_ref.at[pl.ds(at, step), pl.ds(0, lanes)], dst.at[pl.ds(i, step)])
            at += step
    for tx in range(4):
        for ty in range(4):
            pooled_ref[tx, ty : ty + 1, :] = pooled_in[tx * 8 + ty * 2 : tx * 8 + ty * 2 + 1, :].astype(BF16)
    store(pooled_ref, pooled_out)
    for h in range(2):
        cols = slice(h * 128, h * 128 + 128)
        for a in range(7):
            cw_ref[a, :, cols] = small_in[h * 64 + a * 7 : h * 64 + a * 7 + 7, :]
        vec_ref[:, cols] = small_in[h * 64 + 49 : h * 64 + 56, :]
        for q in range(4):
            eb_ref[:, q * 256 + h * 128 : q * 256 + h * 128 + 128] = small_in[h * 64 + 56 + q : h * 64 + 57 + q, :]
        for q in range(2):
            do_ref[:, q * 256 + h * 128 : q * 256 + h * 128 + 128] = small_in[h * 64 + 60 + q : h * 64 + 61 + q, :]
    for src, dst in ((cw_ref, cw_out), (vec_ref, vec_out), (eb_ref, eb_out), (do_ref, do_out)):
        store(src, dst)
    for copy in stores:
        copy.wait()


def finish(pooled, grad_features, small, sums):
    hbm = pl.BlockSpec(memory_space=pl.ANY)
    out = pl.pallas_call(
        finish_kernel,
        out_shape=(
            jax.ShapeDtypeStruct((4, 4, 512), BF16),
            jax.ShapeDtypeStruct((WX, WY, 256), BF16),
            jax.ShapeDtypeStruct((7, 7, 256), F32),
            jax.ShapeDtypeStruct((256, 1024), F32),
            jax.ShapeDtypeStruct((1024, 256), F32),
            jax.ShapeDtypeStruct((1024, 512), F32),
            jax.ShapeDtypeStruct((7, 256), F32),
            jax.ShapeDtypeStruct((1, 1024), F32),
            jax.ShapeDtypeStruct((1, 512), F32),
        ),
        in_specs=[pl.BlockSpec(memory_space=pltpu.VMEM)] * 4,
        out_specs=(hbm,) * 9,
        scratch_shapes=[
            pltpu.VMEM((2304, 1024), F32),
            pltpu.VMEM((4, 4, 512), BF16), pltpu.VMEM((7, 7, 256), F32), pltpu.VMEM((7, 256), F32),
            pltpu.VMEM((1, 1024), F32), pltpu.VMEM((1, 512), F32),
            pltpu.SemaphoreType.DMA((14,)),
        ],
        compiler_params=pltpu.CompilerParams(vmem_limit_bytes=24 * 1024 * 1024),
        cost_estimate=pl.CostEstimate(flops=1_000_000, bytes_accessed=7_000_000, transcendentals=0),
    )(pooled, grad_features, small, sums)
    return out[:7] + (out[7].reshape(1024), out[8].reshape(512))


def on_device(
    features,
    return_slot,
    returned_grads,
    conv_weight,
    conv_bias,
    norm_gain,
    norm_bias,
    expand_weight,
    expand_bias,
    project_weight,
    project_bias,
    layer_scale,
    down_gain,
    down_bias,
    down_weight,
    down_offset,
):
    hbm = pl.BlockSpec(memory_space=pl.ANY)

    def row(v):
        return v.reshape(1, -1)

    def vm(*shape, dtype=F32):
        return pltpu.VMEM(shape, dtype)

    dma = pltpu.SemaphoreType.DMA
    parts = pl.pallas_call(
        kernel,
        out_shape=(
            pltpu.VMEM((32, 512), F32),
            pltpu.VMEM((WX, WY, 256), BF16),
            pltpu.VMEM((128, 128), F32),
            pltpu.VMEM((2, 2048, 256), BF16),
        ),
        in_specs=[pl.BlockSpec(memory_space=pltpu.HBM)] * 16,
        out_specs=(pl.BlockSpec(memory_space=pltpu.VMEM),) * 4,
        scratch_shapes=[
            pltpu.SMEM((4, 4), jnp.int32), vm(WX, WY, 256, dtype=BF16), vm(32, 512, dtype=BF16), vm(7, 7, 256),
            vm(1, 256), vm(1, 256), vm(1, 256), vm(256, 1024, dtype=BF16), vm(1, 1024), vm(1024, 256, dtype=BF16),
            vm(1, 256), vm(1, 256), vm(1, 256), vm(1, 256), vm(1024, 512, dtype=BF16), vm(1, 512),
            dma((16,)),
            vm(2, PLANE, 128), vm(2, PLANE, 128), vm(2, 2, 2, 3, 32, 128, dtype=BF16),
            vm(2, 2, 2, 3, 32, 128, dtype=BF16), vm(2, 2, 2, 3, 32, 128, dtype=BF16),
            vm(2, 2, 2, 3, 32, 128, dtype=BF16), vm(2, 4, 2, 3, 16, 128, dtype=BF16),
            vm(2, 49, 8, 128), vm(4, 32, 128), vm(4, 8, 128),
            vm(4, 32, 128), vm(128, 128), vm(128, 128), vm(4, 32, 128), vm(32, 512, dtype=BF16), vm(4, 8, 1024),
            vm(4, 32, 256),
            vm(2, 1024, 128), vm(1024, 256), vm(1024, 128), vm(256, 1024, dtype=BF16), vm(256, 1024, dtype=BF16),
            vm(1024, 1024, dtype=BF16), vm(1024, 1024, dtype=BF16),
            vm(1024, 1024), vm(2, 1024, 128), vm(1024, 256, dtype=BF16), vm(2, 32, 32, 128),
            vm(2, 512, 128), vm(128, 128), vm(128, 128), vm(4, 8, 128), vm(128, 128),
            vm(2, 2048, 256), vm(2, 1024, 256, dtype=BF16), vm(2, 1024, 256, dtype=BF16),
            vm(2, 1024, 256, dtype=BF16), vm(2, 2, 3, 128, 256, dtype=BF16),
            vm(2, 2, 128, 256, dtype=BF16), vm(2, 2, 7, 16, 256, dtype=BF16),
            dma((2, 8)), dma((2, 8)), dma((16,)), dma((16,)), dma((2, 52)), dma((2, 52)), dma((34,)), dma((34,)),
        ],
        compiler_params=pltpu.CompilerParams(
            collective_id=0, has_side_effects=True, vmem_limit_bytes=48 * 1024 * 1024
        ),
        cost_estimate=pl.CostEstimate(flops=4_000_000_000, bytes_accessed=8_000_000, transcendentals=1_000_000),
    )(
        *(pltpu.with_memory_space_constraint(v, pltpu.HBM) for v in (
        return_slot, features, returned_grads[0], conv_weight, row(conv_bias), row(norm_gain), row(norm_bias),
        expand_weight, row(expand_bias), project_weight, row(project_bias), row(layer_scale), row(down_gain),
        row(down_bias), down_weight, row(down_offset),
        ))
    )
    return finish(*parts)


def solution(mesh):
    placed = (
        P(("slide", "sx"), "sy", None),
        P(("slide", "sx"), "sy"),
        P("sy", ("slide", "sx"), None),
    ) + (P(),) * 13
    return jax.shard_map(
        on_device,
        mesh=mesh,
        in_specs=placed,
        out_specs=(
            P(("slide", "sx"), "sy", None),
            P(("slide", "sx"), "sy", None),
            P("slide", None, None),
            P("slide", None),
            P("slide", None),
            P("slide", None),
            P("slide", None),
            P("slide"),
            P("slide"),
        ),
        check_vma=False,
    )
```
